32 devices in a mesh: dist: 4 (over x, core), ctr: 8 (over z, y).
Axes of the slice: x: 2, y: 2, z: 4, core: 2. Of those that a mesh axis runs over, the one named last changes fastest.
Arguments:
- three_centre: bfloat16 [1024, 4, 4096], P(('dist', 'ctr')), may hold values from -0.359375 to 0.359375
- occupied_green: bfloat16 [128, 4096], P(('dist', 'ctr')), may hold values from -0.75 to 0.75
- virtual_green: bfloat16 [128, 4096], P(('dist', 'ctr')), may hold values from -0.75 to 0.75
- pair_index: int32 [16, 4], replicated, may hold values from 0 to 7, as said below
- source_slot: int32 [16, 4, 4], replicated, may hold values from -1 to 3, as said below
- occupied_index: int32 [16, 4, 4], replicated, may hold values from 0 to 127, as said below
- virtual_index: int32 [16, 4, 4], replicated, may hold values from 0 to 127, as said below
Outputs:
- density_response: float32 [1024, 256], P(('dist', 'ctr'))
The draws below stay inside these ranges and needn't reach their ends.
Inputs may be any that keep to these rules, and one draw needn't show every extreme that they name: `pair_index`: the 4 entries of a row are distinct. `source_slot`: for each slot the listed slots are distinct and come first, followed by -1 entries; all slots of one auxiliary atom list the same number of slots, at least 1; in every draw some auxiliary atom lists 4. `occupied_index`: for auxiliary atom p with g = p // 4, every entry lies in g * 32 to g * 32 + 2 * 32 - 1, taken modulo 128. `virtual_index`: for auxiliary atom p with g = p // 4, every entry lies in g * 32 to g * 32 + 2 * 32 - 1, taken modulo 128.
All inputs are finite; a program needn't handle non-finite values.
Results may differ from the reference program's by a relative error of at most 0.004.
Values may be sent and summed in bfloat16 or wider, within the bound.
A program may use at most 64 MiB of HBM per device.

```python
import jax
import jax.numpy as jnp
from jax import lax

BLK = 64
AUXB = 64
KP = 4
R = 4
PAIRW = 4096
NPR = 8
AUX = 1024
AUXA = 16
AUXR = 4
REGW = 256
NGB = 128
RGB = 32
N_DIST = 4


def draw_pair_index(key, part):
    keys = jax.random.split(jax.random.fold_in(key, 5), AUXA)
    rows = jax.vmap(lambda single: jax.random.permutation(single, NPR)[:KP])(keys)
    return rows.astype(jnp.int32)


def draw_source_slot(key, part):
    base = jax.random.fold_in(key, 11)
    first_key, count_key, full_key = jax.random.split(base, 3)
    keys = jax.random.split(first_key, AUXA * KP)
    picks = jax.vmap(lambda single: jax.random.permutation(single, KP)[:R])(keys).reshape(AUXA, KP, R)
    counts = jax.random.randint(count_key, (AUXA,), 1, R + 1)
    full_atom = jax.random.randint(full_key, (), 0, AUXA)
    counts = jnp.where(jnp.arange(AUXA) == full_atom, R, counts)
    live = jnp.arange(R)[None, None, :] < counts[:, None, None]
    return jnp.where(live, picks, -1).astype(jnp.int32)


def green_positions(key):
    region = jnp.arange(AUXA) // AUXR
    offset = jax.random.randint(key, (AUXA, KP, R), 0, 2 * RGB)
    return ((region[:, None, None] * RGB + offset) % NGB).astype(jnp.int32)


def draw_occupied_index(key, part):
    return green_positions(jax.random.fold_in(key, 21))


def draw_virtual_index(key, part):
    return green_positions(jax.random.fold_in(key, 22))


def block_levels(stream_key, extent, shards, least, high):
    gain = 1.0
    for axis_at, blocks in shards:
        steps = jax.random.uniform(jax.random.fold_in(jax.random.fold_in(stream_key, 6), axis_at), (blocks,), jnp.float32, least / len(shards), high / len(shards))
        gain = gain * jnp.repeat(jnp.exp(steps), extent[axis_at] // blocks).reshape((-1,) + (1,) * (len(extent) - 1 - axis_at))
    return gain


def noise(rng, extent, deviation, reach, cuts=(), held_as=jnp.bfloat16):
    entries = deviation * jax.random.normal(rng, extent, jnp.float32)
    if cuts:
        entries = entries * block_levels(rng, extent, cuts, -0.22, 0.18)
    return jnp.clip(entries, -reach, reach).astype(held_as)


def setup_inputs(seed: int = 0) -> dict:
    splits = jax.random.split(jax.random.key(seed), 8)
    three_centre = noise(splits[0], (AUX, KP, PAIRW), 0.06, 0.359375, ((0, 32),))
    occupied_green = noise(splits[1], (NGB, PAIRW), BLK ** -0.5, 0.75, ((0, 32),))
    virtual_green = noise(splits[2], (NGB, PAIRW), BLK ** -0.5, 0.75, ((0, 32),))
    pair_index = draw_pair_index(jax.random.fold_in(splits[7], 71), 0)
    source_slot = draw_source_slot(jax.random.fold_in(splits[7], 71), 0)
    occupied_index = draw_occupied_index(jax.random.fold_in(splits[7], 71), 0)
    virtual_index = draw_virtual_index(jax.random.fold_in(splits[7], 71), 0)
    return dict(three_centre=three_centre, occupied_green=occupied_green, virtual_green=virtual_green, pair_index=pair_index, source_slot=source_slot, occupied_index=occupied_index, virtual_index=virtual_index)


def green_apply(tensor_atom, source, occ_index, virt_index, occupied_green, virtual_green):
    accumulated = jnp.zeros(tensor_atom.shape, jnp.float32)
    occ_table = occupied_green.reshape(occupied_green.shape[0], BLK, BLK)
    virt_table = virtual_green.reshape(virtual_green.shape[0], BLK, BLK)
    for step in range(R):
        source_col = source[:, step]
        live_mask = (source_col >= 0).astype(jnp.float32)
        picked = jnp.take(tensor_atom, jnp.maximum(source_col, 0).astype(jnp.int32), axis=1)
        virt_blocks = jnp.take(virt_table, virt_index[:, step].astype(jnp.int32), axis=0)
        product = jnp.einsum('aslv,svz->aslz', picked.astype(jnp.float32), virt_blocks.astype(jnp.float32))
        product = (product * live_mask[None, :, None, None]).astype(jnp.bfloat16)
        product = lax.optimization_barrier(product)
        occ_blocks = jnp.take(occ_table, occ_index[:, step].astype(jnp.int32), axis=0)
        accumulated = accumulated + jnp.einsum('slm,aslz->asmz', occ_blocks.astype(jnp.float32), product.astype(jnp.float32))
    return accumulated.astype(jnp.bfloat16)


def region_response(inputs):
    upd_region, ten_region, pairs_region = inputs

    def row_atom(row_inputs):
        upd_atom, pairs_row = row_inputs

        def col_atom(col_inputs):
            ten_atom, pairs_col = col_inputs
            match = (pairs_row[:, None] == pairs_col[None, :]).astype(jnp.float32)
            matched = jnp.einsum('st,btc->sbc', match, ten_atom.astype(jnp.float32))
            return jnp.einsum('asc,sbc->ab', upd_atom.astype(jnp.float32), matched)

        blocks = lax.map(col_atom, (ten_region, pairs_region))
        return jnp.transpose(blocks, (1, 0, 2)).reshape(AUXB, REGW)

    row_blocks = lax.map(row_atom, (upd_region, pairs_region))
    return row_blocks.reshape(REGW, REGW)


def reference(three_centre, occupied_green, virtual_green, pair_index, source_slot, occupied_index, virtual_index):
    tensor_blocks = three_centre.reshape(AUXA, AUXB, KP, BLK, BLK)

    def one_atom(inputs):
        return green_apply(inputs[0], inputs[1], inputs[2], inputs[3], occupied_green, virtual_green)

    updated = lax.map(one_atom, (tensor_blocks, source_slot, occupied_index, virtual_index))
    updated = lax.optimization_barrier(updated)
    upd_regions = updated.reshape(N_DIST, AUXR, AUXB, KP, PAIRW)
    ten_regions = three_centre.reshape(N_DIST, AUXR, AUXB, KP, PAIRW)
    pair_regions = pair_index.reshape(N_DIST, AUXR, KP)
    result = lax.map(region_response, (upd_regions, ten_regions, pair_regions))
    return result.reshape(AUX, REGW)
```

```python
import functools

import jax
import jax.numpy as jnp
from jax import lax
from jax.experimental import pallas as pl
from jax.experimental.pallas import tpu as pltpu
from jax.sharding import PartitionSpec as P

BLK = 64
NPR = 8
LANES = 128
F32 = jnp.float32
BF16 = jnp.bfloat16


def kernel(n, groups, atoms, ids, t_ref, green_ref, out_ref, table, tf, tt, wcat, ocat, usend, urecv, trecv,
           uk, tk, part, psend, precv, g_send, g_recv, t_send, t_recv, u_send, u_recv, p_send, p_recv, own_sem):
    slots, rows, width = t_ref.shape
    chunks = width // LANES
    blocks = green_ref.shape[0] // 2
    cols = width // n
    per = cols // LANES
    dist = lax.axis_index("dist")
    me = lax.axis_index("ctr")
    before = lax.rem(dist + groups - 1, groups)
    after = lax.rem(dist + 1, groups)

    far_first = sorted(range(1, n), key=lambda k: -min(k, n - k))

    def ahead(k):
        return lax.rem(me + k, n)

    def signal(d, c):
        pl.semaphore_signal(barrier, inc=1, device_id=(d, c), device_id_type=pl.DeviceIdType.MESH)

    def remote(src, dst, send, recv, d, c):
        return pltpu.make_async_remote_copy(
            src_ref=src, dst_ref=dst, send_sem=send, recv_sem=recv, device_id=(d, c),
            device_id_type=pl.DeviceIdType.MESH,
        )

    barrier = pltpu.get_barrier_semaphore()
    for k in range(1, n):
        signal(dist, ahead(k))
    signal(before, me)
    signal(after, me)

    row = lax.broadcasted_iota(jnp.int32, (BLK, BLK), 0)
    col = lax.broadcasted_iota(jnp.int32, (BLK, BLK), 1)
    half = BLK // 2
    wanted = jnp.where(row < half, 2 * row, 2 * (row - half) + 1)
    perm = (wanted == col).astype(BF16)
    mine = me * blocks
    for b in range(blocks):
        occ = green_ref[blocks + b]
        turned = lax.dot_general(perm, occ, (((1,), (1,)), ((), ())), preferred_element_type=F32).astype(BF16)
        turned = lax.dot_general(turned, perm, (((1,), (1,)), ((), ())), preferred_element_type=F32).astype(BF16)
        table[mine + b] = jnp.concatenate([green_ref[b], turned], axis=1)

    pl.semaphore_wait(barrier, n + 1)

    lines = n // 2
    high, low = me // 2, lax.rem(me, 2)
    partner = high * 2 + 1 - low

    def line(k):
        return lax.rem(high + k, lines) * 2

    def at_home(c):
        return table.at[pl.ds(c * blocks, blocks)]

    def across(c):
        return table.at[pl.ds((n + c) * blocks, blocks)]

    first_hop = [
        remote(at_home(me), at_home(me), g_send.at[0, k], g_recv.at[0, k], dist, line(k) + low)
        for k in range(1, lines)
    ]
    for copy in first_hop:
        copy.start()

    def t_part(c):
        return t_ref.at[:, :, pl.ds(pl.multiple_of(c * cols, LANES), cols)]

    tensor = [
        remote(t_part(ahead(k)), trecv.at[me], t_send.at[k], t_recv.at[k], dist, ahead(k)) for k in far_first
    ]
    for copy in tensor:
        copy.start()
    own_t = pltpu.make_async_copy(t_part(me), trecv.at[me], own_sem.at[0])
    own_t.start()

    second_hop, third_hop = [], []
    for k in range(lines):
        if k:
            first_hop[k - 1].wait_recv()
        c = line(lines - k) + low
        second_hop.append(remote(at_home(c), at_home(c), g_send.at[1, k], g_recv.at[1, k], dist, partner))
        second_hop[-1].start()
        third_hop.append(remote(at_home(c), across(c), g_send.at[2, k], g_recv.at[2, k], before, me))
        third_hop[-1].start()

    def turn(s, carry):
        for j in range(chunks):
            tf[j * rows:(j + 1) * rows, :] = t_ref[s, :, j * LANES:(j + 1) * LANES].astype(F32)
        for i in range(rows):
            tt[s, i * chunks:(i + 1) * chunks, :] = tf[pl.ds(i, chunks, stride=rows), :].astype(BF16)
        return carry

    lax.fori_loop(0, slots, turn, 0)

    for k in range(lines):
        second_hop[k].wait_recv()
        c = line(lines - k) + 1 - low
        third_hop.append(remote(at_home(c), across(c), g_send.at[3, k], g_recv.at[3, k], before, me))
        third_hop[-1].start()
    for copy in third_hop:
        copy.wait()
    for copy in first_hop + second_hop:
        copy.wait_send()

    size = atoms * slots
    atom = (dist * n + me) * rows // BLK
    total = n * blocks * groups
    base = dist * n * blocks

    def position(value):
        shift = value - base
        return jnp.minimum(jnp.where(shift < 0, shift + total, shift), 2 * n * blocks - 1)

    step_rows = 8 * chunks
    lane = lax.broadcasted_iota(jnp.int32, (half, LANES), 1)

    def update(s, carry):
        at = (atom * slots + s) * slots
        for r in range(slots):
            src = ids[at + r]
            live = jnp.where(src >= 0, 1.0, 0.0).astype(F32)
            src = jnp.maximum(src, 0)
            virt = table[position(ids[2 * size * slots + at + r])].astype(F32)[:, :BLK] * live
            zero = jnp.zeros((BLK, LANES), F32)
            twice = jnp.concatenate([virt, virt], axis=1)
            weight = jnp.concatenate(
                [jnp.concatenate([twice, zero], axis=1), jnp.concatenate([zero, twice], axis=1)], axis=0
            ).astype(BF16)
            ocat[:, r * BLK:(r + 1) * BLK] = table[position(ids[size * slots + at + r])][:, BLK:]
            for h in range(rows // 8):
                got = jnp.dot(
                    tt[src, h * step_rows:(h + 1) * step_rows, :], weight, preferred_element_type=F32
                ).astype(BF16)
                for x in range(8):
                    i = h * 8 + x
                    for e in range(2):
                        wcat[r * BLK + e * half:r * BLK + (e + 1) * half, i * LANES:(i + 1) * LANES] = got[
                            x * chunks:(x + 1) * chunks, e * LANES:(e + 1) * LANES
                        ]
        occ = ocat[...]
        for h in range(rows // 4):
            both = jnp.dot(occ, wcat[:, h * 4 * LANES:(h + 1) * 4 * LANES], preferred_element_type=F32)
            for x in range(4):
                i = h * 4 + x
                piece = both[:, x * LANES:(x + 1) * LANES]
                tf[i * chunks:(i + 1) * chunks, :] = jnp.where(lane < BLK, piece[:half], piece[half:])
        for q in range(chunks):
            usend[s, q // per, :, (q % per) * LANES:(q % per + 1) * LANES] = tf[
                pl.ds(q, rows, stride=chunks), :
            ].astype(BF16)
        for k in far_first:
            sent(s, k).start()
        return carry

    def sent(s, k):
        return remote(
            usend.at[s, ahead(k)], urecv.at[me, s], u_send.at[s, k], u_recv.at[s, k], dist, ahead(k)
        )

    lax.fori_loop(0, slots, update, 0)
    own_u = pltpu.make_async_copy(usend.at[:, me], urecv.at[me], own_sem.at[1])
    own_u.start()
    own_t.wait()
    for copy in tensor:
        copy.wait()

    first = dist * (n * rows // BLK)
    pairs = 3 * size * slots

    def pick(src, pair, p):
        where = pairs + (first + p * rows // BLK) * slots
        slot = jnp.int32(0)
        live = jnp.int32(0)
        for s in range(slots):
            hit = ids[where + s] == pair
            slot = jnp.where(hit, s, slot)
            live = jnp.where(hit, 1, live)
        return (src[p, slot].astype(F32) * live.astype(F32)).astype(BF16)

    def at_rows(p):
        return pl.ds(pl.multiple_of(p * rows, rows), rows)

    def at_cols(pair):
        return pl.ds(pl.multiple_of(pair * cols, LANES), cols)

    def tensor_pair(pair, carry):
        def gather(p, inner):
            tk[at_rows(p), at_cols(pair)] = pick(trecv, pair, p)
            return inner

        return lax.fori_loop(0, n, gather, carry)

    lax.fori_loop(0, NPR, tensor_pair, 0)

    def updated_pairs(p):
        where = pairs + (first + p * rows // BLK) * slots

        def one_pair(pair, carry):
            chosen = jnp.zeros((rows, cols), F32)
            for s in range(slots):
                hit = jnp.where(ids[where + s] == pair, 1.0, 0.0).astype(F32)
                chosen = chosen + urecv[p, s].astype(F32) * hit
            uk[at_rows(p), at_cols(pair)] = chosen.astype(BF16)
            return carry

        lax.fori_loop(0, NPR, one_pair, 0)

    own_u.wait()
    updated_pairs(me)
    for k in far_first[::-1]:
        for s in range(slots):
            sent(s, k).wait()
        updated_pairs(lax.rem(me - k + n, n))

    def block(p, carry):
        at = pl.ds(pl.multiple_of(p * 256, 256), 256)
        total = lax.dot_general(uk[at, :], tk[...], (((1,), (1,)), ((), ())), preferred_element_type=F32)
        part[at, :] = total
        psend[at, :] = total.astype(BF16)
        return carry

    lax.fori_loop(0, n * rows // 256, block, 0)

    def p_part(c):
        return psend.at[pl.ds(pl.multiple_of(c * rows, rows), rows)]

    shares = [
        remote(p_part(ahead(k)), precv.at[k], p_send.at[k], p_recv.at[k], dist, ahead(k)) for k in far_first
    ]
    for copy in shares:
        copy.start()
    result = part[pl.ds(pl.multiple_of(me * rows, rows), rows), :]
    for k, copy in zip(far_first, shares):
        copy.wait()
        result = result + precv[k].astype(F32)
    out_ref[...] = result


def iota(shape, dim):
    return lax.broadcasted_iota(jnp.int32, shape, dim)


def nt(a, b):
    return lax.dot_general(a, b, (((1,), (1,)), ((), ())), preferred_element_type=F32)


def nn(a, b):
    return jnp.dot(a, b, preferred_element_type=F32)


def line_kernel(n, groups, atoms, ids, t_ref, green_ref, out_ref, table, halves, moved, stack, swapped, tf, xg, wg, uf,
                first_op, second_op, gather, select, place, lift, turn_v, blk, cross, partner_in, cross_in,
                g_send, g_recv, y_send, y_recv, m_send, m_recv, c_send, c_recv, p_send, p_recv):
    slots, rows, width = t_ref.shape
    blocks = green_ref.shape[0] // 2
    chunks = width // LANES
    half = BLK // 2
    part_rows = rows // 2
    deep = BLK * LANES
    dist = lax.axis_index("dist")
    me = lax.axis_index("ctr")
    before = lax.rem(dist + groups - 1, groups)
    after = lax.rem(dist + 1, groups)
    lines = n // 2
    high, low = me // 2, lax.rem(me, 2)
    partner = high * 2 + 1 - low
    mirrored = lax.rem(dist, 2)

    def flip(a):
        return jnp.where(mirrored == 1, lines - 1 - a, a)

    place_at = flip(high)

    def at_place(a, y):
        return flip(a) * 2 + y

    def signal(d, c):
        pl.semaphore_signal(barrier, inc=1, device_id=(d, c), device_id_type=pl.DeviceIdType.MESH)

    def remote(src, dst, send, recv, d, c):
        return pltpu.make_async_remote_copy(
            src_ref=src, dst_ref=dst, send_sem=send, recv_sem=recv, device_id=(d, c),
            device_id_type=pl.DeviceIdType.MESH,
        )

    barrier = pltpu.get_barrier_semaphore()
    for k in range(1, n):
        signal(dist, lax.rem(me + k, n))
    signal(before, me)
    signal(after, me)

    row, col = iota((BLK, BLK), 0), iota((BLK, BLK), 1)
    wanted = jnp.where(row < half, 2 * row, 2 * (row - half) + 1)
    perm = (wanted == col).astype(BF16)
    mine = me * blocks
    for b in range(blocks):
        turned = nn(perm, green_ref[blocks + b]).astype(BF16)
        turned = nt(turned, perm).astype(BF16)
        table[mine + b] = jnp.concatenate([green_ref[b], turned], axis=1)

    wide = slots * LANES
    r_, c_ = iota((wide, wide), 0), iota((wide, wide), 1)
    select[...] = (
        r_ == ((c_ // half) % slots) * LANES + ((c_ // LANES) % 2) * BLK + (c_ // (2 * LANES)) * half + c_ % half
    ).astype(BF16)
    r_, c_ = iota((wide, slots * BLK), 0), iota((wide, slots * BLK), 1)
    place[...] = ((r_ % LANES >= BLK) & (c_ == (r_ // LANES) * BLK + r_ % LANES - BLK)).astype(BF16)
    r_, c_ = iota((2 * LANES, LANES), 0), iota((2 * LANES, LANES), 1)
    for t in range(slots):
        lift[t] = ((c_ < BLK) & (r_ == (c_ // half) * LANES + t * half + c_ % half)).astype(BF16)
    r_, c_ = iota((LANES, wide), 0), iota((LANES, wide), 1)
    turn_v[...] = ((r_ // half == c_ // LANES) & (c_ % LANES == low * half + r_ % half)).astype(BF16)

    own_rows = pl.ds(pl.multiple_of(low * rows, rows), rows)
    per = 8
    for q in range(0, chunks, per):
        x = jnp.concatenate(
            [
                jnp.concatenate([t_ref[j, :, (q + p) * LANES:(q + p + 1) * LANES] for j in range(slots)], axis=1)
                for p in range(per)
            ],
            axis=0,
        )
        got = nn(x, select[...]).astype(BF16)
        for p in range(per):
            for h in range(2):
                for e in range(2):
                    at = (e * half + q + p) * LANES
                    halves[h, own_rows, at:at + LANES] = got[
                        p * rows:(p + 1) * rows, (h * 2 + e) * LANES:(h * 2 + e + 1) * LANES
                    ]

    pl.semaphore_wait(barrier, n + 1)

    def line(k):
        return lax.rem(high + k, lines) * 2

    def at_home(c):
        return table.at[pl.ds(c * blocks, blocks)]

    def across(c):
        return table.at[pl.ds((n + c) * blocks, blocks)]

    first_hop = [
        remote(at_home(me), at_home(me), g_send.at[0, k], g_recv.at[0, k], dist, line(k) + low)
        for k in range(1, lines)
    ]
    for copy in first_hop:
        copy.start()

    def rows_of(k):
        y = low if k < 2 else 1 - low
        return pl.ds(pl.multiple_of(y * rows + (k % 2) * part_rows, part_rows), part_rows)

    def over_y(phase, k):
        h = 1 - low if phase == 0 else low
        at = halves.at[h, rows_of(k)]
        return remote(at, at, y_send.at[phase, k], y_recv.at[phase, k], dist, partner)

    def from_y(phase, k):
        at = halves.at[low if phase == 0 else 1 - low, rows_of(2 + k)]
        return remote(at, at, y_send.at[phase, k], y_recv.at[phase, k], dist, partner)

    pieces = 2
    piece = deep // pieces

    def over_z(slot, k, x, own, to):
        at, lanes = rows_of(k), pl.ds(x * piece, piece)
        src = halves.at[low, at, lanes] if own else moved.at[slot, at, lanes]
        sem = k * pieces + x
        return remote(
            src, moved.at[slot, at, lanes], m_send.at[slot, sem], m_recv.at[slot, sem], dist, at_place(to, low)
        )

    starts = {0: (0, 1), 1: (1, 2), 3: (2, 2)}

    def send_own(k):
        for a, (slot, to) in starts.items():
            @pl.when(place_at == a)
            def _():
                for x in range(pieces):
                    over_z(slot, k, x, True, to).start()

    over_y(0, 0).start()
    for k in range(2):
        send_own(k)
    second_hop, third_hop = [], []
    for k in range(lines):
        if k:
            first_hop[k - 1].wait_recv()
        c = line(lines - k) + low
        second_hop.append(remote(at_home(c), at_home(c), g_send.at[1, k], g_recv.at[1, k], dist, partner))
        second_hop[-1].start()
        third_hop.append(remote(at_home(c), across(c), g_send.at[2, k], g_recv.at[2, k], before, me))
        third_hop[-1].start()
    over_y(0, 1).start()

    def relay(slot, k):
        for a in {0: (1, 2), 1: (2,), 2: ()}[slot]:
            @pl.when(place_at == a)
            def _():
                for x in range(pieces):
                    over_z(slot, k, x, False, a).wait_recv()
                    over_z(slot, k, x, False, a + 1).start()

    relay(1, 0)
    relay(0, 0)
    from_y(0, 0).wait_recv()
    send_own(2)
    relay(1, 1)
    relay(0, 1)

    for k in range(lines):
        second_hop[k].wait_recv()
        c = line(lines - k) + 1 - low
        third_hop.append(remote(at_home(c), across(c), g_send.at[3, k], g_recv.at[3, k], before, me))
        third_hop[-1].start()

    from_y(0, 1).wait_recv()
    send_own(3)
    for k in range(2):
        over_y(0, k).wait_send()
        over_y(1, k).start()
    for copy in third_hop:
        copy.wait()
    for copy in first_hop + second_hop:
        copy.wait_send()
    relay(1, 2)
    relay(0, 2)

    size = atoms * slots
    occ_at, virt_at, pair_at = size * slots, 2 * size * slots, 3 * size * slots
    total = n * blocks * groups
    base = dist * n * blocks
    atom = dist * lines + high

    def position(value):
        shift = value - base
        return jnp.minimum(jnp.where(shift < 0, shift + total, shift), 2 * n * blocks - 1)

    def atom_at(a):
        return dist * lines + flip(a)

    def feeding(a, s, j):
        r, live = jnp.int32(0), jnp.int32(0)
        for x in range(slots):
            hit = ids[(a * slots + s) * slots + x] == j
            r, live = jnp.where(hit, x, r), jnp.where(hit, 1, live)
        return r, live

    def green(a, s, r, live):
        at = (a * slots + s) * slots + r
        return position(ids[occ_at + at]), position(ids[virt_at + at]), live.astype(F32)

    for t in range(slots):
        virt = []
        for o in range(slots):
            r, live = feeding(atom, o, t)
            occ_pos, virt_pos, live = green(atom, o, r, live)
            virt.append((table[virt_pos].astype(F32) * live).astype(BF16))
            gather[t * BLK:(t + 1) * BLK, o * LANES:(o + 1) * LANES] = table[occ_pos]
        b = nt(turn_v[...], jnp.concatenate(virt, axis=1)).astype(BF16)
        second_op[0, :, t * LANES:(t + 1) * LANES] = nt(lift[t][:, :BLK], b).astype(BF16)
    size_op = slots * BLK
    unit = (iota((size_op, size_op), 0) == iota((size_op, size_op), 1)).astype(BF16)
    first_op[0] = nt(unit, nn(gather[...], place[...]).astype(BF16)).astype(BF16)

    def operators(slot, a):
        other = atom_at(a)
        for t in range(slots):
            pair = ids[pair_at + atom * slots + t]
            s, met = jnp.int32(0), jnp.int32(0)
            for x in range(slots):
                hit = ids[pair_at + other * slots + x] == pair
                s, met = jnp.where(hit, x, s), jnp.where(hit, 1, met)
            virt = []
            for o in range(slots):
                r, live = feeding(other, s, o)
                occ_pos, virt_pos, live = green(other, s, r, live * met)
                virt.append(
                    (table[virt_pos, pl.ds(pl.multiple_of(low * half, half), half), :].astype(F32) * live).astype(BF16)
                )
                gather[o * BLK:(o + 1) * BLK, t * LANES:(t + 1) * LANES] = table[occ_pos]
            second_op[1 + slot, :, t * LANES:(t + 1) * LANES] = nt(lift[t], jnp.concatenate(virt, axis=0)).astype(BF16)
        first_op[1 + slot] = nn(gather[...], place[...]).astype(BF16)

    used = {0: (0, (1, 2, 3)), 1: (1, (2, 3)), 2: (3, (2,))}

    def wanted_here(slot):
        hit = place_at == used[slot][1][0]
        for a in used[slot][1][1:]:
            hit = hit | (place_at == a)
        return hit

    for slot in used:
        @pl.when(wanted_here(slot))
        def _():
            operators(slot, used[slot][0])

    lanes2 = (iota((BLK, 2 * LANES), 1) // half) % slots

    def one_stack(k, at_rows):
        got = nn(xg[...], second_op[k]).astype(BF16)
        for i in range(part_rows):
            for t in range(slots):
                wg[i, t * BLK:(t + 1) * BLK, :] = got[i * BLK:(i + 1) * BLK, t * LANES:(t + 1) * LANES]
        for p in range(part_rows // 2):
            both = nn(first_op[k], jnp.concatenate([wg[2 * p], wg[2 * p + 1]], axis=1))
            res = both[:BLK]
            for o in range(1, slots):
                res = jnp.where(lanes2 == o, both[o * BLK:(o + 1) * BLK], res)
            for x in range(2):
                uf[(2 * p + x) * BLK:(2 * p + x + 1) * BLK, :] = res[:, x * LANES:(x + 1) * LANES]
        for m in range(BLK):
            stack[k, at_rows, m * LANES:(m + 1) * LANES] = uf[pl.ds(m, part_rows, stride=BLK), :].astype(BF16)

    def transform(g):
        at_rows = rows_of(g)
        for h in range(2):
            for m in range(BLK):
                tf[h, m * part_rows:(m + 1) * part_rows, :] = halves[h, at_rows, m * LANES:(m + 1) * LANES].astype(F32)
            for i in range(part_rows):
                xg[i * BLK:(i + 1) * BLK, h * LANES:(h + 1) * LANES] = tf[
                    h, pl.ds(i, BLK, stride=part_rows), :
                ].astype(BF16)

        def each(k, carry):
            hit = (k == 0) | ((k == 1) & wanted_here(0)) | ((k == 2) & wanted_here(1)) | ((k == 3) & wanted_here(2))

            @pl.when(hit)
            def _():
                one_stack(k, at_rows)
            return carry

        lax.fori_loop(0, 1 + len(used), each, 0)

    for g in range(4):
        if g >= 2:
            from_y(1, g - 2).wait_recv()
        transform(g)
        if g == 0:
            relay(1, 3)
            relay(0, 3)

    for c in range(lines):
        blk[c] = jnp.zeros((BLK, LANES), F32)

    def lay(x):
        return jnp.concatenate([x, jnp.zeros((BLK, LANES - BLK), F32)], axis=1)

    blk[high] = lay(nt(stack[0], halves[low]))

    def returned(slot, y):
        a = used[slot][0]
        return remote(
            cross.at[slot, pl.ds(y * rows, rows)], cross_in.at[place_at, low], c_send.at[slot, y],
            c_recv.at[place_at, low], dist, at_place(a, y),
        )

    def product(slot):
        a = used[slot][0]
        for k in range(4):
            if slot == 2:
                for x in range(pieces):
                    over_z(slot, k, x, False, a).wait_recv()
            else:
                @pl.when(place_at == 3)
                def _():
                    for x in range(pieces):
                        over_z(slot, k, x, False, a).wait_recv()
        cross[slot] = lay(nt(moved[slot], stack[1 + slot]))
        for y in range(2):
            returned(slot, y).start()
        other = atom_at(a)
        r_, c_ = iota((LANES, LANES), 0), iota((LANES, LANES), 1)
        match = jnp.zeros((LANES, LANES), F32)
        for s in range(slots):
            for t in range(slots):
                hit = jnp.where(ids[pair_at + atom * slots + s] == ids[pair_at + other * slots + t], 1.0, 0.0)
                match = jnp.where((r_ // half == s) & (c_ // half == t), hit.astype(F32), match)
        match = jnp.where(r_ % half == c_ % half, match, 0.0).astype(BF16)
        for m in range(0, BLK, 8):
            x = jnp.concatenate([stack[0, :, (m + p) * LANES:(m + p + 1) * LANES] for p in range(8)], axis=0)
            got = nn(x, match).astype(BF16)
            for p in range(8):
                swapped[:, (m + p) * LANES:(m + p + 1) * LANES] = got[p * BLK:(p + 1) * BLK]
        blk[flip(a)] = lay(nt(swapped[...], moved[slot]))

    for slot in (1, 0, 2):
        @pl.when(wanted_here(slot))
        def _():
            product(slot)

    other_rows = pl.ds(pl.multiple_of((1 - low) * rows, rows), rows)
    to_partner = remote(blk.at[:, other_rows], partner_in, p_send.at[0], p_recv.at[0], dist, partner)
    to_partner.start()

    came = {1: (0,), 2: (0, 1, 3), 3: (0, 1)}
    for src, takers in came.items():
        for a in takers:
            @pl.when(place_at == a)
            def _():
                for y in range(2):
                    remote(
                        cross.at[0, pl.ds(0, rows)], cross_in.at[src, y], c_send.at[0, 0], c_recv.at[src, y], dist, me
                    ).wait_recv()
                blk[flip(src), own_rows] = cross_in[src, 0] + cross_in[src, 1]
    to_partner.wait()
    tiles = [(blk[c, own_rows] + partner_in[c])[:, :BLK] for c in range(lines)]
    out_ref[...] = jnp.concatenate(tiles, axis=1)

    for k in range(2):
        over_y(1, k).wait_send()
    for slot, senders in {0: (0, 1, 2), 1: (1, 2), 2: (3,)}.items():
        for a in senders:
            @pl.when(place_at == a)
            def _():
                for k in range(4):
                    for x in range(pieces):
                        over_z(slot, k, x, False, 0).wait_send()

        @pl.when(wanted_here(slot))
        def _():
            for y in range(2):
                returned(slot, y).wait_send()


def on_line(n, groups, atoms, ids, tensor, green):
    slots, rows, width = tensor.shape
    blocks = green.shape[0] // 2
    lines = n // 2
    deep = BLK * LANES
    part_rows = rows // 2
    vmem = pl.BlockSpec(memory_space=pltpu.VMEM)
    dma = pltpu.SemaphoreType.DMA
    return pl.pallas_call(
        functools.partial(line_kernel, n, groups, atoms),
        out_shape=jax.ShapeDtypeStruct((rows, lines * BLK), F32),
        in_specs=[pl.BlockSpec(memory_space=pltpu.SMEM), vmem, vmem],
        out_specs=vmem,
        scratch_shapes=[
            pltpu.VMEM((2 * n * blocks, BLK, LANES), BF16),
            pltpu.VMEM((2, BLK, deep), BF16),
            pltpu.VMEM((3, BLK, deep), BF16),
            pltpu.VMEM((4, BLK, deep), BF16),
            pltpu.VMEM((BLK, deep), BF16),
            pltpu.VMEM((2, part_rows * BLK, LANES), F32),
            pltpu.VMEM((part_rows * BLK, 2 * LANES), BF16),
            pltpu.VMEM((part_rows, slots * BLK, LANES), BF16),
            pltpu.VMEM((part_rows * BLK, LANES), F32),
            pltpu.VMEM((4, slots * BLK, slots * BLK), BF16),
            pltpu.VMEM((4, 2 * LANES, slots * LANES), BF16),
            pltpu.VMEM((slots * BLK, slots * LANES), BF16),
            pltpu.VMEM((slots * LANES, slots * LANES), BF16),
            pltpu.VMEM((slots * LANES, slots * BLK), BF16),
            pltpu.VMEM((slots, 2 * LANES, LANES), BF16),
            pltpu.VMEM((LANES, slots * LANES), BF16),
            pltpu.VMEM((lines, BLK, LANES), F32),
            pltpu.VMEM((3, BLK, LANES), F32),
            pltpu.VMEM((lines, rows, LANES), F32),
            pltpu.VMEM((lines, 2, rows, LANES), F32),
            dma((4, lines)),
            dma((4, lines)),
            dma((2, 2)),
            dma((2, 2)),
            dma((3, 8)),
            dma((3, 8)),
            dma((3, 2)),
            dma((lines, 2)),
            dma((1,)),
            dma((1,)),
        ],
        compiler_params=pltpu.CompilerParams(
            collective_id=1, has_side_effects=True, vmem_limit_bytes=48 * 2**20
        ),
    )(ids, tensor, green)


def solution(mesh):
    n = mesh.shape["ctr"]
    groups = mesh.shape["dist"]

    def shards(three_centre, occupied_green, virtual_green, pair_index, source_slot, occupied_index, virtual_index):
        rows, slots, width = three_centre.shape
        blocks = occupied_green.shape[0]
        atoms = pair_index.shape[0]
        chunks = width // LANES
        cols = width // n
        tensor = jnp.transpose(three_centre, (1, 0, 2))
        green = jnp.concatenate([virtual_green, occupied_green], axis=0).reshape(2 * blocks, BLK, BLK)
        ids = jnp.concatenate(
            [x.reshape(-1) for x in (source_slot, occupied_index, virtual_index, pair_index)]
        )
        vmem = pl.BlockSpec(memory_space=pltpu.VMEM)
        dma = pltpu.SemaphoreType.DMA
        if n == 8 and groups % 2 == 0 and rows * 2 == BLK:
            return on_line(n, groups, atoms, ids, tensor, green)
        return pl.pallas_call(
            functools.partial(kernel, n, groups, atoms),
            out_shape=jax.ShapeDtypeStruct((rows, n * rows), F32),
            in_specs=[pl.BlockSpec(memory_space=pltpu.SMEM), vmem, vmem],
            out_specs=vmem,
            scratch_shapes=[
                pltpu.VMEM((2 * n * blocks, BLK, LANES), BF16),
                pltpu.VMEM((rows * chunks, LANES), F32),
                pltpu.VMEM((slots, rows * chunks, LANES), BF16),
                pltpu.VMEM((slots * BLK, rows * LANES), BF16),
                pltpu.VMEM((BLK, slots * BLK), BF16),
                pltpu.VMEM((slots, n, rows, cols), BF16),
                pltpu.VMEM((n, slots, rows, cols), BF16),
                pltpu.VMEM((n, slots, rows, cols), BF16),
                pltpu.VMEM((n * rows, NPR * cols), BF16),
                pltpu.VMEM((n * rows, NPR * cols), BF16),
                pltpu.VMEM((n * rows, n * rows), F32),
                pltpu.VMEM((n * rows, n * rows), BF16),
                pltpu.VMEM((n, rows, n * rows), BF16),
                dma((4, n // 2)),
                dma((4, n // 2)),
                dma((n,)),
                dma((n,)),
                dma((slots, n)),
                dma((slots, n)),
                dma((n,)),
                dma((n,)),
                dma((2,)),
            ],
            compiler_params=pltpu.CompilerParams(
                collective_id=0, has_side_effects=True, vmem_limit_bytes=48 * 2**20
            ),
        )(ids, tensor, green)

    return jax.shard_map(
        shards,
        mesh=mesh,
        in_specs=(
            P(("dist", "ctr"), None, None),
            P(("dist", "ctr"), None),
            P(("dist", "ctr"), None),
            P(),
            P(),
            P(),
            P(),
        ),
        out_specs=P(("dist", "ctr"), None),
        check_vma=False,
    )
```

```python
import functools

import jax
import jax.numpy as jnp
from jax import lax
from jax.experimental import pallas as pl
from jax.experimental.pallas import tpu as pltpu
from jax.sharding import PartitionSpec as P

BLK = 64
NPR = 8
LANES = 128
F32 = jnp.float32
BF16 = jnp.bfloat16


def kernel(n, groups, atoms, ids, t_ref, green_ref, out_ref, table, tf, tt, wcat, ocat, usend, urecv, trecv,
           uk, tk, part, psend, precv, g_send, g_recv, t_send, t_recv, u_send, u_recv, p_send, p_recv, own_sem):
    slots, rows, width = t_ref.shape
    chunks = width // LANES
    blocks = green_ref.shape[0] // 2
    cols = width // n
    per = cols // LANES
    dist = lax.axis_index("dist")
    me = lax.axis_index("ctr")
    before = lax.rem(dist + groups - 1, groups)
    after = lax.rem(dist + 1, groups)

    far_first = sorted(range(1, n), key=lambda k: -min(k, n - k))

    def ahead(k):
        return lax.rem(me + k, n)

    def signal(d, c):
        pl.semaphore_signal(barrier, inc=1, device_id=(d, c), device_id_type=pl.DeviceIdType.MESH)

    def remote(src, dst, send, recv, d, c):
        return pltpu.make_async_remote_copy(
            src_ref=src, dst_ref=dst, send_sem=send, recv_sem=recv, device_id=(d, c),
            device_id_type=pl.DeviceIdType.MESH,
        )

    barrier = pltpu.get_barrier_semaphore()
    for k in range(1, n):
        signal(dist, ahead(k))
    signal(before, me)
    signal(after, me)

    row = lax.broadcasted_iota(jnp.int32, (BLK, BLK), 0)
    col = lax.broadcasted_iota(jnp.int32, (BLK, BLK), 1)
    half = BLK // 2
    wanted = jnp.where(row < half, 2 * row, 2 * (row - half) + 1)
    perm = (wanted == col).astype(BF16)
    mine = me * blocks
    for b in range(blocks):
        occ = green_ref[blocks + b]
        turned = lax.dot_general(perm, occ, (((1,), (1,)), ((), ())), preferred_element_type=F32).astype(BF16)
        turned = lax.dot_general(turned, perm, (((1,), (1,)), ((), ())), preferred_element_type=F32).astype(BF16)
        table[mine + b] = jnp.concatenate([green_ref[b], turned], axis=1)

    pl.semaphore_wait(barrier, n + 1)

    lines = n // 2
    high, low = me // 2, lax.rem(me, 2)
    partner = high * 2 + 1 - low

    def line(k):
        return lax.rem(high + k, lines) * 2

    def at_home(c):
        return table.at[pl.ds(c * blocks, blocks)]

    def across(c):
        return table.at[pl.ds((n + c) * blocks, blocks)]

    first_hop = [
        remote(at_home(me), at_home(me), g_send.at[0, k], g_recv.at[0, k], dist, line(k) + low)
        for k in range(1, lines)
    ]
    for copy in first_hop:
        copy.start()

    def t_part(c):
        return t_ref.at[:, :, pl.ds(pl.multiple_of(c * cols, LANES), cols)]

    tensor = [
        remote(t_part(ahead(k)), trecv.at[me], t_send.at[k], t_recv.at[k], dist, ahead(k)) for k in far_first
    ]
    for copy in tensor:
        copy.start()
    own_t = pltpu.make_async_copy(t_part(me), trecv.at[me], own_sem.at[0])
    own_t.start()

    second_hop, third_hop = [], []
    for k in range(lines):
        if k:
            first_hop[k - 1].wait_recv()
        c = line(lines - k) + low
        second_hop.append(remote(at_home(c), at_home(c), g_send.at[1, k], g_recv.at[1, k], dist, partner))
        second_hop[-1].start()
        third_hop.append(remote(at_home(c), across(c), g_send.at[2, k], g_recv.at[2, k], before, me))
        third_hop[-1].start()

    def turn(s, carry):
        for j in range(chunks):
            tf[j * rows:(j + 1) * rows, :] = t_ref[s, :, j * LANES:(j + 1) * LANES].astype(F32)
        for i in range(rows):
            tt[s, i * chunks:(i + 1) * chunks, :] = tf[pl.ds(i, chunks, stride=rows), :].astype(BF16)
        return carry

    lax.fori_loop(0, slots, turn, 0)

    for k in range(lines):
        second_hop[k].wait_recv()
        c = line(lines - k) + 1 - low
        third_hop.append(remote(at_home(c), across(c), g_send.at[3, k], g_recv.at[3, k], before, me))
        third_hop[-1].start()
    for copy in third_hop:
        copy.wait()
    for copy in first_hop + second_hop:
        copy.wait_send()

    size = atoms * slots
    atom = (dist * n + me) * rows // BLK
    total = n * blocks * groups
    base = dist * n * blocks

    def position(value):
        shift = value - base
        return jnp.minimum(jnp.where(shift < 0, shift + total, shift), 2 * n * blocks - 1)

    step_rows = 8 * chunks
    lane = lax.broadcasted_iota(jnp.int32, (half, LANES), 1)

    def update(s, carry):
        at = (atom * slots + s) * slots
        for r in range(slots):
            src = ids[at + r]
            live = jnp.where(src >= 0, 1.0, 0.0).astype(F32)
            src = jnp.maximum(src, 0)
            virt = table[position(ids[2 * size * slots + at + r])].astype(F32)[:, :BLK] * live
            zero = jnp.zeros((BLK, LANES), F32)
            twice = jnp.concatenate([virt, virt], axis=1)
            weight = jnp.concatenate(
                [jnp.concatenate([twice, zero], axis=1), jnp.concatenate([zero, twice], axis=1)], axis=0
            ).astype(BF16)
            ocat[:, r * BLK:(r + 1) * BLK] = table[position(ids[size * slots + at + r])][:, BLK:]
            for h in range(rows // 8):
                got = jnp.dot(
                    tt[src, h * step_rows:(h + 1) * step_rows, :], weight, preferred_element_type=F32
                ).astype(BF16)
                for x in range(8):
                    i = h * 8 + x
                    for e in range(2):
                        wcat[r * BLK + e * half:r * BLK + (e + 1) * half, i * LANES:(i + 1) * LANES] = got[
                            x * chunks:(x + 1) * chunks, e * LANES:(e + 1) * LANES
                        ]
        occ = ocat[...]
        for h in range(rows // 4):
            both = jnp.dot(occ, wcat[:, h * 4 * LANES:(h + 1) * 4 * LANES], preferred_element_type=F32)
            for x in range(4):
                i = h * 4 + x
                piece = both[:, x * LANES:(x + 1) * LANES]
                tf[i * chunks:(i + 1) * chunks, :] = jnp.where(lane < BLK, piece[:half], piece[half:])
        for q in range(chunks):
            usend[s, q // per, :, (q % per) * LANES:(q % per + 1) * LANES] = tf[
                pl.ds(q, rows, stride=chunks), :
            ].astype(BF16)
        for k in far_first:
            sent(s, k).start()
        return carry

    def sent(s, k):
        return remote(
            usend.at[s, ahead(k)], urecv.at[me, s], u_send.at[s, k], u_recv.at[s, k], dist, ahead(k)
        )

    lax.fori_loop(0, slots, update, 0)
    own_u = pltpu.make_async_copy(usend.at[:, me], urecv.at[me], own_sem.at[1])
    own_u.start()
    own_t.wait()
    for copy in tensor:
        copy.wait()

    first = dist * (n * rows // BLK)
    pairs = 3 * size * slots

    def pick(src, pair, p):
        where = pairs + (first + p * rows // BLK) * slots
        slot = jnp.int32(0)
        live = jnp.int32(0)
        for s in range(slots):
            hit = ids[where + s] == pair
            slot = jnp.where(hit, s, slot)
            live = jnp.where(hit, 1, live)
        return (src[p, slot].astype(F32) * live.astype(F32)).astype(BF16)

    def at_rows(p):
        return pl.ds(pl.multiple_of(p * rows, rows), rows)

    def at_cols(pair):
        return pl.ds(pl.multiple_of(pair * cols, LANES), cols)

    def tensor_pair(pair, carry):
        def gather(p, inner):
            tk[at_rows(p), at_cols(pair)] = pick(trecv, pair, p)
            return inner

        return lax.fori_loop(0, n, gather, carry)

    lax.fori_loop(0, NPR, tensor_pair, 0)

    def updated_pairs(p):
        where = pairs + (first + p * rows // BLK) * slots

        def one_pair(pair, carry):
            chosen = jnp.zeros((rows, cols), F32)
            for s in range(slots):
                hit = jnp.where(ids[where + s] == pair, 1.0, 0.0).astype(F32)
                chosen = chosen + urecv[p, s].astype(F32) * hit
            uk[at_rows(p), at_cols(pair)] = chosen.astype(BF16)
            return carry

        lax.fori_loop(0, NPR, one_pair, 0)

    own_u.wait()
    updated_pairs(me)
    for k in far_first[::-1]:
        for s in range(slots):
            sent(s, k).wait()
        updated_pairs(lax.rem(me - k + n, n))

    def block(p, carry):
        at = pl.ds(pl.multiple_of(p * 256, 256), 256)
        total = lax.dot_general(uk[at, :], tk[...], (((1,), (1,)), ((), ())), preferred_element_type=F32)
        part[at, :] = total
        psend[at, :] = total.astype(BF16)
        return carry

    lax.fori_loop(0, n * rows // 256, block, 0)

    def p_part(c):
        return psend.at[pl.ds(pl.multiple_of(c * rows, rows), rows)]

    shares = [
        remote(p_part(ahead(k)), precv.at[k], p_send.at[k], p_recv.at[k], dist, ahead(k)) for k in far_first
    ]
    for copy in shares:
        copy.start()
    result = part[pl.ds(pl.multiple_of(me * rows, rows), rows), :]
    for k, copy in zip(far_first, shares):
        copy.wait()
        result = result + precv[k].astype(F32)
    out_ref[...] = result


def iota(shape, dim):
    return lax.broadcasted_iota(jnp.int32, shape, dim)


def nt(a, b):
    return lax.dot_general(a, b, (((1,), (1,)), ((), ())), preferred_element_type=F32)


def nn(a, b):
    return jnp.dot(a, b, preferred_element_type=F32)


def line_kernel(n, groups, atoms, ids, t_ref, green_ref, out_ref, table, halves, moved, stack, match_op, tf, xg, wg, uf,
                first_op, second_op, gather, select, place, lift, turn_v, blk, cross, partner_in, cross_in,
                g_send, g_recv, y_send, y_recv, m_send, m_recv, c_send, c_recv, p_send, p_recv):
    slots, rows, width = t_ref.shape
    blocks = green_ref.shape[0] // 2
    chunks = width // LANES
    half = BLK // 2
    part_rows = rows // 2
    deep = BLK * LANES
    dist = lax.axis_index("dist")
    me = lax.axis_index("ctr")
    before = lax.rem(dist + groups - 1, groups)
    after = lax.rem(dist + 1, groups)
    lines = n // 2
    high, low = me // 2, lax.rem(me, 2)
    partner = high * 2 + 1 - low
    mirrored = lax.rem(dist, 2)

    def flip(a):
        return jnp.where(mirrored == 1, lines - 1 - a, a)

    place_at = flip(high)

    def at_place(a, y):
        return flip(a) * 2 + y

    def signal(d, c):
        pl.semaphore_signal(barrier, inc=1, device_id=(d, c), device_id_type=pl.DeviceIdType.MESH)

    def remote(src, dst, send, recv, d, c):
        return pltpu.make_async_remote_copy(
            src_ref=src, dst_ref=dst, send_sem=send, recv_sem=recv, device_id=(d, c),
            device_id_type=pl.DeviceIdType.MESH,
        )

    barrier = pltpu.get_barrier_semaphore()
    for k in range(1, n):
        signal(dist, lax.rem(me + k, n))
    signal(before, me)
    signal(after, me)

    row, col = iota((BLK, BLK), 0), iota((BLK, BLK), 1)
    wanted = jnp.where(row < half, 2 * row, 2 * (row - half) + 1)
    perm = (wanted == col).astype(BF16)
    mine = me * blocks
    for b in range(blocks):
        turned = nn(perm, green_ref[blocks + b]).astype(BF16)
        turned = nt(turned, perm).astype(BF16)
        table[mine + b] = jnp.concatenate([green_ref[b], turned], axis=1)

    wide = slots * LANES
    r_, c_ = iota((wide, wide), 0), iota((wide, wide), 1)
    select[...] = (
        r_ == ((c_ // half) % slots) * LANES + ((c_ // LANES) % 2) * BLK + (c_ // (2 * LANES)) * half + c_ % half
    ).astype(BF16)
    r_, c_ = iota((wide, slots * BLK), 0), iota((wide, slots * BLK), 1)
    place[...] = ((r_ % LANES >= BLK) & (c_ == (r_ // LANES) * BLK + r_ % LANES - BLK)).astype(BF16)
    r_, c_ = iota((2 * LANES, LANES), 0), iota((2 * LANES, LANES), 1)
    for t in range(slots):
        lift[t] = ((c_ < BLK) & (r_ == (c_ // half) * LANES + t * half + c_ % half)).astype(BF16)
    r_, c_ = iota((LANES, wide), 0), iota((LANES, wide), 1)
    turn_v[...] = ((r_ // half == c_ // LANES) & (c_ % LANES == low * half + r_ % half)).astype(BF16)

    own_rows = pl.ds(pl.multiple_of(low * rows, rows), rows)
    per = 8
    for q in range(0, chunks, per):
        x = jnp.concatenate(
            [
                jnp.concatenate([t_ref[j, :, (q + p) * LANES:(q + p + 1) * LANES] for j in range(slots)], axis=1)
                for p in range(per)
            ],
            axis=0,
        )
        got = nn(x, select[...]).astype(BF16)
        for p in range(per):
            for h in range(2):
                for e in range(2):
                    at = (e * half + q + p) * LANES
                    halves[h, own_rows, at:at + LANES] = got[
                        p * rows:(p + 1) * rows, (h * 2 + e) * LANES:(h * 2 + e + 1) * LANES
                    ]

    pl.semaphore_wait(barrier, n + 1)

    def line(k):
        return lax.rem(high + k, lines) * 2

    def at_home(c):
        return table.at[pl.ds(c * blocks, blocks)]

    def across(c):
        return table.at[pl.ds((n + c) * blocks, blocks)]

    first_hop = [
        remote(at_home(me), at_home(me), g_send.at[0, k], g_recv.at[0, k], dist, line(k) + low)
        for k in range(1, lines)
    ]
    for copy in first_hop:
        copy.start()

    def rows_of(k):
        y = low if k < 2 else 1 - low
        return pl.ds(pl.multiple_of(y * rows + (k % 2) * part_rows, part_rows), part_rows)

    def over_y(phase, k):
        h = 1 - low if phase == 0 else low
        at = halves.at[h, rows_of(k)]
        return remote(at, at, y_send.at[phase, k], y_recv.at[phase, k], dist, partner)

    def from_y(phase, k):
        at = halves.at[low if phase == 0 else 1 - low, rows_of(2 + k)]
        return remote(at, at, y_send.at[phase, k], y_recv.at[phase, k], dist, partner)

    pieces = 2
    piece = deep // pieces

    def over_z(slot, k, x, own, to):
        at, lanes = rows_of(k), pl.ds(x * piece, piece)
        src = halves.at[low, at, lanes] if own else moved.at[slot, at, lanes]
        sem = k * pieces + x
        return remote(
            src, moved.at[slot, at, lanes], m_send.at[slot, sem], m_recv.at[slot, sem], dist, at_place(to, low)
        )

    starts = {0: (0, 1), 1: (1, 2), 3: (2, 2)}

    def send_own(k):
        for a, (slot, to) in starts.items():
            @pl.when(place_at == a)
            def _():
                for x in range(pieces):
                    over_z(slot, k, x, True, to).start()

    over_y(0, 0).start()
    for k in range(2):
        send_own(k)
    second_hop, third_hop = [], []
    for k in range(lines):
        if k:
            first_hop[k - 1].wait_recv()
        c = line(lines - k) + low
        second_hop.append(remote(at_home(c), at_home(c), g_send.at[1, k], g_recv.at[1, k], dist, partner))
        second_hop[-1].start()
        third_hop.append(remote(at_home(c), across(c), g_send.at[2, k], g_recv.at[2, k], before, me))
        third_hop[-1].start()
    over_y(0, 1).start()
    for k in range(2):
        over_y(1, k).start()

    def relay(a, slot, k):
        @pl.when(place_at == a)
        def _():
            for x in range(pieces):
                over_z(slot, k, x, False, a).wait_recv()
                over_z(slot, k, x, False, a + 1).start()

    from_y(0, 0).wait_recv()
    send_own(2)
    relay(2, 1, 0)
    relay(1, 0, 0)
    relay(2, 1, 1)

    for k in range(lines):
        second_hop[k].wait_recv()
        c = line(lines - k) + 1 - low
        third_hop.append(remote(at_home(c), across(c), g_send.at[3, k], g_recv.at[3, k], before, me))
        third_hop[-1].start()

    relay(2, 1, 2)
    relay(2, 0, 0)
    relay(1, 0, 1)
    for copy in third_hop:
        copy.wait_recv()

    size = atoms * slots
    occ_at, virt_at, pair_at = size * slots, 2 * size * slots, 3 * size * slots
    total = n * blocks * groups
    base = dist * n * blocks
    atom = dist * lines + high

    def position(value):
        shift = value - base
        return jnp.minimum(jnp.where(shift < 0, shift + total, shift), 2 * n * blocks - 1)

    def atom_at(a):
        return dist * lines + flip(a)

    def feeding(a, s, j):
        r, live = jnp.int32(0), jnp.int32(0)
        for x in range(slots):
            hit = ids[(a * slots + s) * slots + x] == j
            r, live = jnp.where(hit, x, r), jnp.where(hit, 1, live)
        return r, live

    def green(a, s, r, live):
        at = (a * slots + s) * slots + r
        return position(ids[occ_at + at]), position(ids[virt_at + at]), live.astype(F32)

    for t in range(slots):
        virt = []
        for o in range(slots):
            r, live = feeding(atom, o, t)
            occ_pos, virt_pos, live = green(atom, o, r, live)
            virt.append((table[virt_pos].astype(F32) * live).astype(BF16))
            gather[t * BLK:(t + 1) * BLK, o * LANES:(o + 1) * LANES] = table[occ_pos]
        b = nt(turn_v[...], jnp.concatenate(virt, axis=1)).astype(BF16)
        second_op[0, :, t * LANES:(t + 1) * LANES] = nt(lift[t][:, :BLK], b).astype(BF16)
    size_op = slots * BLK
    unit = (iota((size_op, size_op), 0) == iota((size_op, size_op), 1)).astype(BF16)
    first_op[0] = nt(unit, nn(gather[...], place[...]).astype(BF16)).astype(BF16)

    from_y(0, 1).wait_recv()
    send_own(3)
    relay(2, 0, 1)

    def operators(slot, a):
        other = atom_at(a)
        for t in range(slots):
            pair = ids[pair_at + atom * slots + t]
            s, met = jnp.int32(0), jnp.int32(0)
            for x in range(slots):
                hit = ids[pair_at + other * slots + x] == pair
                s, met = jnp.where(hit, x, s), jnp.where(hit, 1, met)
            virt = []
            for o in range(slots):
                r, live = feeding(other, s, o)
                occ_pos, virt_pos, live = green(other, s, r, live * met)
                virt.append(
                    (table[virt_pos, pl.ds(pl.multiple_of(low * half, half), half), :].astype(F32) * live).astype(BF16)
                )
                gather[o * BLK:(o + 1) * BLK, t * LANES:(t + 1) * LANES] = table[occ_pos]
            second_op[1 + slot, :, t * LANES:(t + 1) * LANES] = nt(lift[t], jnp.concatenate(virt, axis=0)).astype(BF16)
        first_op[1 + slot] = nn(gather[...], place[...]).astype(BF16)

    used = {0: (0, (1, 2, 3)), 1: (1, (2, 3)), 2: (3, (2,))}

    def wanted_here(slot):
        hit = place_at == used[slot][1][0]
        for a in used[slot][1][1:]:
            hit = hit | (place_at == a)
        return hit

    for slot in used:
        @pl.when(wanted_here(slot))
        def _():
            operators(slot, used[slot][0])

    r_, c_ = iota((LANES, LANES), 0), iota((LANES, LANES), 1)
    for slot in used:
        other = atom_at(used[slot][0])
        match = jnp.zeros((LANES, LANES), F32)
        for s in range(slots):
            for t in range(slots):
                hit = jnp.where(ids[pair_at + atom * slots + s] == ids[pair_at + other * slots + t], 1.0, 0.0)
                match = jnp.where((r_ // half == s) & (c_ // half == t), hit.astype(F32), match)
        match_op[:, slot * LANES:(slot + 1) * LANES] = jnp.where(r_ % half == c_ % half, match, 0.0).astype(BF16)

    lanes2 = (iota((BLK, 2 * LANES), 1) // half) % slots

    def one_stack(k, at_rows):
        got = nn(xg[...], second_op[k]).astype(BF16)
        for i in range(part_rows):
            for t in range(slots):
                wg[i, t * BLK:(t + 1) * BLK, :] = got[i * BLK:(i + 1) * BLK, t * LANES:(t + 1) * LANES]
        for p in range(part_rows // 2):
            both = nn(first_op[k], jnp.concatenate([wg[2 * p], wg[2 * p + 1]], axis=1))
            res = both[:BLK]
            for o in range(1, slots):
                res = jnp.where(lanes2 == o, both[o * BLK:(o + 1) * BLK], res)
            for x in range(2):
                uf[(2 * p + x) * BLK:(2 * p + x + 1) * BLK, :] = res[:, x * LANES:(x + 1) * LANES]
        for m in range(BLK):
            stack[k, at_rows, m * LANES:(m + 1) * LANES] = uf[pl.ds(m, part_rows, stride=BLK), :].astype(BF16)

    def reorder(at_rows):
        x = jnp.concatenate([stack[0, at_rows, m * LANES:(m + 1) * LANES] for m in range(BLK)], axis=0)
        got = nn(x, match_op[...]).astype(BF16)
        below = pl.ds(at_rows.start + BLK, part_rows)
        for m in range(BLK):
            for slot in used:
                stack[1 + slot, below, m * LANES:(m + 1) * LANES] = got[
                    m * part_rows:(m + 1) * part_rows, slot * LANES:(slot + 1) * LANES
                ]

    def transform(g):
        at_rows = rows_of(g)
        for h in range(2):
            for m in range(BLK):
                tf[h, m * part_rows:(m + 1) * part_rows, :] = halves[h, at_rows, m * LANES:(m + 1) * LANES].astype(F32)
            for i in range(part_rows):
                xg[i * BLK:(i + 1) * BLK, h * LANES:(h + 1) * LANES] = tf[
                    h, pl.ds(i, BLK, stride=part_rows), :
                ].astype(BF16)

        def each(k, carry):
            hit = (k == 0) | ((k == 1) & wanted_here(0)) | ((k == 2) & wanted_here(1)) | ((k == 3) & wanted_here(2))

            @pl.when(hit)
            def _():
                one_stack(k, at_rows)
            return carry

        lax.fori_loop(0, 1 + len(used), each, 0)

        @pl.when(place_at > 0)
        def _():
            reorder(at_rows)

    relay(1, 0, 2)
    relay(2, 1, 3)
    transform(0)
    relay(2, 0, 2)
    relay(1, 0, 3)
    transform(1)
    from_y(1, 0).wait_recv()
    transform(2)
    relay(2, 0, 3)
    from_y(1, 1).wait_recv()
    transform(3)

    for c in range(lines):
        blk[c] = jnp.zeros((BLK, LANES), F32)

    def lay(x):
        return jnp.concatenate([x, jnp.zeros((BLK, LANES - BLK), F32)], axis=1)

    blk[high] = lay(nt(stack[0, :BLK], halves[low]))

    def returned(slot, y):
        a = used[slot][0]
        return remote(
            cross.at[slot, pl.ds(y * rows, rows)], cross_in.at[place_at, low], c_send.at[slot, y],
            c_recv.at[place_at, low], dist, at_place(a, y),
        )

    def product(slot):
        a = used[slot][0]
        for k in range(4):
            if slot == 2:
                for x in range(pieces):
                    over_z(slot, k, x, False, a).wait_recv()
            else:
                @pl.when(place_at == 3)
                def _():
                    for x in range(pieces):
                        over_z(slot, k, x, False, a).wait_recv()
        both = nt(moved[slot], stack[1 + slot])
        cross[slot] = both
        for y in range(2):
            returned(slot, y).start()
        blk[flip(a)] = lay(both.T[BLK:])

    for slot in (2, 1, 0):
        @pl.when(wanted_here(slot))
        def _():
            product(slot)

    other_rows = pl.ds(pl.multiple_of((1 - low) * rows, rows), rows)
    to_partner = remote(blk.at[:, other_rows], partner_in, p_send.at[0], p_recv.at[0], dist, partner)
    to_partner.start()

    came = {1: (0,), 2: (0, 1, 3), 3: (0, 1)}
    for src, takers in came.items():
        for a in takers:
            @pl.when(place_at == a)
            def _():
                for y in range(2):
                    remote(
                        cross.at[0, pl.ds(0, rows)], cross_in.at[src, y], c_send.at[0, 0], c_recv.at[src, y], dist, me
                    ).wait_recv()
                blk[flip(src), own_rows] = cross_in[src, 0] + cross_in[src, 1]
    to_partner.wait()
    tiles = [(blk[c, own_rows] + partner_in[c])[:, :BLK] for c in range(lines)]
    out_ref[...] = jnp.concatenate(tiles, axis=1)

    for copy in first_hop + second_hop + third_hop:
        copy.wait_send()
    for k in range(2):
        over_y(0, k).wait_send()
        over_y(1, k).wait_send()
    for slot, senders in {0: (0, 1, 2), 1: (1, 2), 2: (3,)}.items():
        for a in senders:
            @pl.when(place_at == a)
            def _():
                for k in range(4):
                    for x in range(pieces):
                        over_z(slot, k, x, False, 0).wait_send()

        @pl.when(wanted_here(slot))
        def _():
            for y in range(2):
                returned(slot, y).wait_send()


def on_line(n, groups, atoms, ids, tensor, green):
    slots, rows, width = tensor.shape
    blocks = green.shape[0] // 2
    lines = n // 2
    deep = BLK * LANES
    part_rows = rows // 2
    vmem = pl.BlockSpec(memory_space=pltpu.VMEM)
    dma = pltpu.SemaphoreType.DMA
    return pl.pallas_call(
        functools.partial(line_kernel, n, groups, atoms),
        out_shape=jax.ShapeDtypeStruct((rows, lines * BLK), F32),
        in_specs=[pl.BlockSpec(memory_space=pltpu.SMEM), vmem, vmem],
        out_specs=vmem,
        scratch_shapes=[
            pltpu.VMEM((2 * n * blocks, BLK, LANES), BF16),
            pltpu.VMEM((2, BLK, deep), BF16),
            pltpu.VMEM((3, BLK, deep), BF16),
            pltpu.VMEM((4, 2 * BLK, deep), BF16),
            pltpu.VMEM((LANES, 3 * LANES), BF16),
            pltpu.VMEM((2, part_rows * BLK, LANES), F32),
            pltpu.VMEM((part_rows * BLK, 2 * LANES), BF16),
            pltpu.VMEM((part_rows, slots * BLK, LANES), BF16),
            pltpu.VMEM((part_rows * BLK, LANES), F32),
            pltpu.VMEM((4, slots * BLK, slots * BLK), BF16),
            pltpu.VMEM((4, 2 * LANES, slots * LANES), BF16),
            pltpu.VMEM((slots * BLK, slots * LANES), BF16),
            pltpu.VMEM((slots * LANES, slots * LANES), BF16),
            pltpu.VMEM((slots * LANES, slots * BLK), BF16),
            pltpu.VMEM((slots, 2 * LANES, LANES), BF16),
            pltpu.VMEM((LANES, slots * LANES), BF16),
            pltpu.VMEM((lines, BLK, LANES), F32),
            pltpu.VMEM((3, BLK, LANES), F32),
            pltpu.VMEM((lines, rows, LANES), F32),
            pltpu.VMEM((lines, 2, rows, LANES), F32),
            dma((4, lines)),
            dma((4, lines)),
            dma((2, 2)),
            dma((2, 2)),
            dma((3, 8)),
            dma((3, 8)),
            dma((3, 2)),
            dma((lines, 2)),
            dma((1,)),
            dma((1,)),
        ],
        compiler_params=pltpu.CompilerParams(
            collective_id=1, has_side_effects=True, vmem_limit_bytes=48 * 2**20
        ),
    )(ids, tensor, green)


def solution(mesh):
    n = mesh.shape["ctr"]
    groups = mesh.shape["dist"]

    def shards(three_centre, occupied_green, virtual_green, pair_index, source_slot, occupied_index, virtual_index):
        rows, slots, width = three_centre.shape
        blocks = occupied_green.shape[0]
        atoms = pair_index.shape[0]
        chunks = width // LANES
        cols = width // n
        tensor = jnp.transpose(three_centre, (1, 0, 2))
        green = jnp.concatenate([virtual_green, occupied_green], axis=0).reshape(2 * blocks, BLK, BLK)
        ids = jnp.concatenate(
            [x.reshape(-1) for x in (source_slot, occupied_index, virtual_index, pair_index)]
        )
        vmem = pl.BlockSpec(memory_space=pltpu.VMEM)
        dma = pltpu.SemaphoreType.DMA
        if n == 8 and groups % 2 == 0 and rows * 2 == BLK:
            return on_line(n, groups, atoms, ids, tensor, green)
        return pl.pallas_call(
            functools.partial(kernel, n, groups, atoms),
            out_shape=jax.ShapeDtypeStruct((rows, n * rows), F32),
            in_specs=[pl.BlockSpec(memory_space=pltpu.SMEM), vmem, vmem],
            out_specs=vmem,
            scratch_shapes=[
                pltpu.VMEM((2 * n * blocks, BLK, LANES), BF16),
                pltpu.VMEM((rows * chunks, LANES), F32),
                pltpu.VMEM((slots, rows * chunks, LANES), BF16),
                pltpu.VMEM((slots * BLK, rows * LANES), BF16),
                pltpu.VMEM((BLK, slots * BLK), BF16),
                pltpu.VMEM((slots, n, rows, cols), BF16),
                pltpu.VMEM((n, slots, rows, cols), BF16),
                pltpu.VMEM((n, slots, rows, cols), BF16),
                pltpu.VMEM((n * rows, NPR * cols), BF16),
                pltpu.VMEM((n * rows, NPR * cols), BF16),
                pltpu.VMEM((n * rows, n * rows), F32),
                pltpu.VMEM((n * rows, n * rows), BF16),
                pltpu.VMEM((n, rows, n * rows), BF16),
                dma((4, n // 2)),
                dma((4, n // 2)),
                dma((n,)),
                dma((n,)),
                dma((slots, n)),
                dma((slots, n)),
                dma((n,)),
                dma((n,)),
                dma((2,)),
            ],
            compiler_params=pltpu.CompilerParams(
                collective_id=0, has_side_effects=True, vmem_limit_bytes=48 * 2**20
            ),
        )(ids, tensor, green)

    return jax.shard_map(
        shards,
        mesh=mesh,
        in_specs=(
            P(("dist", "ctr"), None, None),
            P(("dist", "ctr"), None),
            P(("dist", "ctr"), None),
            P(),
            P(),
            P(),
            P(),
        ),
        out_specs=P(("dist", "ctr"), None),
        check_vma=False,
    )
```

```python
import functools

import jax
import jax.numpy as jnp
from jax import lax
from jax.experimental import pallas as pl
from jax.experimental.pallas import tpu as pltpu
from jax.sharding import PartitionSpec as P

BLK = 64
NPR = 8
LANES = 128
F32 = jnp.float32
BF16 = jnp.bfloat16


def kernel(n, groups, atoms, ids, t_ref, green_ref, out_ref, table, tf, tt, wcat, ocat, usend, urecv, trecv,
           uk, tk, part, psend, precv, g_send, g_recv, t_send, t_recv, u_send, u_recv, p_send, p_recv, own_sem):
    slots, rows, width = t_ref.shape
    chunks = width // LANES
    blocks = green_ref.shape[0] // 2
    cols = width // n
    per = cols // LANES
    dist = lax.axis_index("dist")
    me = lax.axis_index("ctr")
    before = lax.rem(dist + groups - 1, groups)
    after = lax.rem(dist + 1, groups)

    far_first = sorted(range(1, n), key=lambda k: -min(k, n - k))

    def ahead(k):
        return lax.rem(me + k, n)

    def signal(d, c):
        pl.semaphore_signal(barrier, inc=1, device_id=(d, c), device_id_type=pl.DeviceIdType.MESH)

    def remote(src, dst, send, recv, d, c):
        return pltpu.make_async_remote_copy(
            src_ref=src, dst_ref=dst, send_sem=send, recv_sem=recv, device_id=(d, c),
            device_id_type=pl.DeviceIdType.MESH,
        )

    barrier = pltpu.get_barrier_semaphore()
    for k in range(1, n):
        signal(dist, ahead(k))
    signal(before, me)
    signal(after, me)

    row = lax.broadcasted_iota(jnp.int32, (BLK, BLK), 0)
    col = lax.broadcasted_iota(jnp.int32, (BLK, BLK), 1)
    half = BLK // 2
    wanted = jnp.where(row < half, 2 * row, 2 * (row - half) + 1)
    perm = (wanted == col).astype(BF16)
    mine = me * blocks
    for b in range(blocks):
        occ = green_ref[blocks + b]
        turned = lax.dot_general(perm, occ, (((1,), (1,)), ((), ())), preferred_element_type=F32).astype(BF16)
        turned = lax.dot_general(turned, perm, (((1,), (1,)), ((), ())), preferred_element_type=F32).astype(BF16)
        table[mine + b] = jnp.concatenate([green_ref[b], turned], axis=1)

    pl.semaphore_wait(barrier, n + 1)

    lines = n // 2
    high, low = me // 2, lax.rem(me, 2)
    partner = high * 2 + 1 - low

    def line(k):
        return lax.rem(high + k, lines) * 2

    def at_home(c):
        return table.at[pl.ds(c * blocks, blocks)]

    def across(c):
        return table.at[pl.ds((n + c) * blocks, blocks)]

    first_hop = [
        remote(at_home(me), at_home(me), g_send.at[0, k], g_recv.at[0, k], dist, line(k) + low)
        for k in range(1, lines)
    ]
    for copy in first_hop:
        copy.start()

    def t_part(c):
        return t_ref.at[:, :, pl.ds(pl.multiple_of(c * cols, LANES), cols)]

    tensor = [
        remote(t_part(ahead(k)), trecv.at[me], t_send.at[k], t_recv.at[k], dist, ahead(k)) for k in far_first
    ]
    for copy in tensor:
        copy.start()
    own_t = pltpu.make_async_copy(t_part(me), trecv.at[me], own_sem.at[0])
    own_t.start()

    second_hop, third_hop = [], []
    for k in range(lines):
        if k:
            first_hop[k - 1].wait_recv()
        c = line(lines - k) + low
        second_hop.append(remote(at_home(c), at_home(c), g_send.at[1, k], g_recv.at[1, k], dist, partner))
        second_hop[-1].start()
        third_hop.append(remote(at_home(c), across(c), g_send.at[2, k], g_recv.at[2, k], before, me))
        third_hop[-1].start()

    def turn(s, carry):
        for j in range(chunks):
            tf[j * rows:(j + 1) * rows, :] = t_ref[s, :, j * LANES:(j + 1) * LANES].astype(F32)
        for i in range(rows):
            tt[s, i * chunks:(i + 1) * chunks, :] = tf[pl.ds(i, chunks, stride=rows), :].astype(BF16)
        return carry

    lax.fori_loop(0, slots, turn, 0)

    for k in range(lines):
        second_hop[k].wait_recv()
        c = line(lines - k) + 1 - low
        third_hop.append(remote(at_home(c), across(c), g_send.at[3, k], g_recv.at[3, k], before, me))
        third_hop[-1].start()
    for copy in third_hop:
        copy.wait()
    for copy in first_hop + second_hop:
        copy.wait_send()

    size = atoms * slots
    atom = (dist * n + me) * rows // BLK
    total = n * blocks * groups
    base = dist * n * blocks

    def position(value):
        shift = value - base
        return jnp.minimum(jnp.where(shift < 0, shift + total, shift), 2 * n * blocks - 1)

    step_rows = 8 * chunks
    lane = lax.broadcasted_iota(jnp.int32, (half, LANES), 1)

    def update(s, carry):
        at = (atom * slots + s) * slots
        for r in range(slots):
            src = ids[at + r]
            live = jnp.where(src >= 0, 1.0, 0.0).astype(F32)
            src = jnp.maximum(src, 0)
            virt = table[position(ids[2 * size * slots + at + r])].astype(F32)[:, :BLK] * live
            zero = jnp.zeros((BLK, LANES), F32)
            twice = jnp.concatenate([virt, virt], axis=1)
            weight = jnp.concatenate(
                [jnp.concatenate([twice, zero], axis=1), jnp.concatenate([zero, twice], axis=1)], axis=0
            ).astype(BF16)
            ocat[:, r * BLK:(r + 1) * BLK] = table[position(ids[size * slots + at + r])][:, BLK:]
            for h in range(rows // 8):
                got = jnp.dot(
                    tt[src, h * step_rows:(h + 1) * step_rows, :], weight, preferred_element_type=F32
                ).astype(BF16)
                for x in range(8):
                    i = h * 8 + x
                    for e in range(2):
                        wcat[r * BLK + e * half:r * BLK + (e + 1) * half, i * LANES:(i + 1) * LANES] = got[
                            x * chunks:(x + 1) * chunks, e * LANES:(e + 1) * LANES
                        ]
        occ = ocat[...]
        for h in range(rows // 4):
            both = jnp.dot(occ, wcat[:, h * 4 * LANES:(h + 1) * 4 * LANES], preferred_element_type=F32)
            for x in range(4):
                i = h * 4 + x
                piece = both[:, x * LANES:(x + 1) * LANES]
                tf[i * chunks:(i + 1) * chunks, :] = jnp.where(lane < BLK, piece[:half], piece[half:])
        for q in range(chunks):
            usend[s, q // per, :, (q % per) * LANES:(q % per + 1) * LANES] = tf[
                pl.ds(q, rows, stride=chunks), :
            ].astype(BF16)
        for k in far_first:
            sent(s, k).start()
        return carry

    def sent(s, k):
        return remote(
            usend.at[s, ahead(k)], urecv.at[me, s], u_send.at[s, k], u_recv.at[s, k], dist, ahead(k)
        )

    lax.fori_loop(0, slots, update, 0)
    own_u = pltpu.make_async_copy(usend.at[:, me], urecv.at[me], own_sem.at[1])
    own_u.start()
    own_t.wait()
    for copy in tensor:
        copy.wait()

    first = dist * (n * rows // BLK)
    pairs = 3 * size * slots

    def pick(src, pair, p):
        where = pairs + (first + p * rows // BLK) * slots
        slot = jnp.int32(0)
        live = jnp.int32(0)
        for s in range(slots):
            hit = ids[where + s] == pair
            slot = jnp.where(hit, s, slot)
            live = jnp.where(hit, 1, live)
        return (src[p, slot].astype(F32) * live.astype(F32)).astype(BF16)

    def at_rows(p):
        return pl.ds(pl.multiple_of(p * rows, rows), rows)

    def at_cols(pair):
        return pl.ds(pl.multiple_of(pair * cols, LANES), cols)

    def tensor_pair(pair, carry):
        def gather(p, inner):
            tk[at_rows(p), at_cols(pair)] = pick(trecv, pair, p)
            return inner

        return lax.fori_loop(0, n, gather, carry)

    lax.fori_loop(0, NPR, tensor_pair, 0)

    def updated_pairs(p):
        where = pairs + (first + p * rows // BLK) * slots

        def one_pair(pair, carry):
            chosen = jnp.zeros((rows, cols), F32)
            for s in range(slots):
                hit = jnp.where(ids[where + s] == pair, 1.0, 0.0).astype(F32)
                chosen = chosen + urecv[p, s].astype(F32) * hit
            uk[at_rows(p), at_cols(pair)] = chosen.astype(BF16)
            return carry

        lax.fori_loop(0, NPR, one_pair, 0)

    own_u.wait()
    updated_pairs(me)
    for k in far_first[::-1]:
        for s in range(slots):
            sent(s, k).wait()
        updated_pairs(lax.rem(me - k + n, n))

    def block(p, carry):
        at = pl.ds(pl.multiple_of(p * 256, 256), 256)
        total = lax.dot_general(uk[at, :], tk[...], (((1,), (1,)), ((), ())), preferred_element_type=F32)
        part[at, :] = total
        psend[at, :] = total.astype(BF16)
        return carry

    lax.fori_loop(0, n * rows // 256, block, 0)

    def p_part(c):
        return psend.at[pl.ds(pl.multiple_of(c * rows, rows), rows)]

    shares = [
        remote(p_part(ahead(k)), precv.at[k], p_send.at[k], p_recv.at[k], dist, ahead(k)) for k in far_first
    ]
    for copy in shares:
        copy.start()
    result = part[pl.ds(pl.multiple_of(me * rows, rows), rows), :]
    for k, copy in zip(far_first, shares):
        copy.wait()
        result = result + precv[k].astype(F32)
    out_ref[...] = result


def iota(shape, dim):
    return lax.broadcasted_iota(jnp.int32, shape, dim)


def nt(a, b):
    return lax.dot_general(a, b, (((1,), (1,)), ((), ())), preferred_element_type=F32)


def nn(a, b):
    return jnp.dot(a, b, preferred_element_type=F32)


def line_kernel(n, groups, atoms, ids, t_ref, green_ref, out_ref, table, halves, moved, stack, match_op, tf, xg, wg, uf,
                first_op, second_op, gather, select, place, lift, turn_v, blk, cross, partner_in, cross_in,
                g_send, g_recv, y_send, y_recv, m_send, m_recv, c_send, c_recv, p_send, p_recv):
    slots, rows, width = t_ref.shape
    blocks = green_ref.shape[0] // 2
    chunks = width // LANES
    half = BLK // 2
    part_rows = rows // 2
    deep = BLK * LANES
    dist = lax.axis_index("dist")
    me = lax.axis_index("ctr")
    before = lax.rem(dist + groups - 1, groups)
    after = lax.rem(dist + 1, groups)
    lines = n // 2
    high, low = me // 2, lax.rem(me, 2)
    partner = high * 2 + 1 - low
    mirrored = lax.rem(dist, 2)

    def flip(a):
        return jnp.where(mirrored == 1, lines - 1 - a, a)

    place_at = flip(high)

    def at_place(a, y):
        return flip(a) * 2 + y

    def signal(d, c):
        pl.semaphore_signal(barrier, inc=1, device_id=(d, c), device_id_type=pl.DeviceIdType.MESH)

    def remote(src, dst, send, recv, d, c):
        return pltpu.make_async_remote_copy(
            src_ref=src, dst_ref=dst, send_sem=send, recv_sem=recv, device_id=(d, c),
            device_id_type=pl.DeviceIdType.MESH,
        )

    barrier = pltpu.get_barrier_semaphore()
    for k in range(1, n):
        signal(dist, lax.rem(me + k, n))
    signal(before, me)
    signal(after, me)

    row, col = iota((BLK, BLK), 0), iota((BLK, BLK), 1)
    wanted = jnp.where(row < half, 2 * row, 2 * (row - half) + 1)
    perm = (wanted == col).astype(BF16)
    mine = me * blocks
    for b in range(blocks):
        turned = nn(perm, green_ref[blocks + b]).astype(BF16)
        turned = nt(turned, perm).astype(BF16)
        table[mine + b] = jnp.concatenate([green_ref[b], turned], axis=1)

    wide = slots * LANES
    r_, c_ = iota((wide, wide), 0), iota((wide, wide), 1)
    select[...] = (
        r_ == ((c_ // half) % slots) * LANES + ((c_ // LANES) % 2) * BLK + (c_ // (2 * LANES)) * half + c_ % half
    ).astype(BF16)
    r_, c_ = iota((wide, slots * BLK), 0), iota((wide, slots * BLK), 1)
    place[...] = ((r_ % LANES >= BLK) & (c_ == (r_ // LANES) * BLK + r_ % LANES - BLK)).astype(BF16)
    r_, c_ = iota((2 * LANES, LANES), 0), iota((2 * LANES, LANES), 1)
    for t in range(slots):
        lift[t] = ((c_ < BLK) & (r_ == (c_ // half) * LANES + t * half + c_ % half)).astype(BF16)
    r_, c_ = iota((LANES, wide), 0), iota((LANES, wide), 1)
    turn_v[...] = ((r_ // half == c_ // LANES) & (c_ % LANES == low * half + r_ % half)).astype(BF16)

    own_rows = pl.ds(pl.multiple_of(low * rows, rows), rows)
    per = 8
    for q in range(0, chunks, per):
        x = jnp.concatenate(
            [
                jnp.concatenate([t_ref[j, :, (q + p) * LANES:(q + p + 1) * LANES] for j in range(slots)], axis=1)
                for p in range(per)
            ],
            axis=0,
        )
        got = nn(x, select[...]).astype(BF16)
        for p in range(per):
            for h in range(2):
                for e in range(2):
                    at = (e * half + q + p) * LANES
                    halves[h, own_rows, at:at + LANES] = got[
                        p * rows:(p + 1) * rows, (h * 2 + e) * LANES:(h * 2 + e + 1) * LANES
                    ]

    pl.semaphore_wait(barrier, n + 1)

    def line(k):
        return lax.rem(high + k, lines) * 2

    def at_home(c):
        return table.at[pl.ds(c * blocks, blocks)]

    def across(c):
        return table.at[pl.ds((n + c) * blocks, blocks)]

    first_hop = [
        remote(at_home(me), at_home(me), g_send.at[0, k], g_recv.at[0, k], dist, line(k) + low)
        for k in range(1, lines)
    ]
    for copy in first_hop:
        copy.start()

    def rows_of(k):
        y = low if k < 2 else 1 - low
        return pl.ds(pl.multiple_of(y * rows + (k % 2) * part_rows, part_rows), part_rows)

    def over_y(phase, k):
        h = 1 - low if phase == 0 else low
        at = halves.at[h, rows_of(k)]
        return remote(at, at, y_send.at[phase, k], y_recv.at[phase, k], dist, partner)

    def from_y(phase, k):
        at = halves.at[low if phase == 0 else 1 - low, rows_of(2 + k)]
        return remote(at, at, y_send.at[phase, k], y_recv.at[phase, k], dist, partner)

    pieces = 2
    piece = deep // pieces

    def over_z(slot, k, x, own, to):
        at, lanes = rows_of(k), pl.ds(x * piece, piece)
        src = halves.at[low, at, lanes] if own else moved.at[slot, at, lanes]
        sem = k * pieces + x
        return remote(
            src, moved.at[slot, at, lanes], m_send.at[slot, sem], m_recv.at[slot, sem], dist, at_place(to, low)
        )

    starts = {0: (0, 1), 1: (1, 2), 3: (2, 2)}

    def send_own(k):
        for a, (slot, to) in starts.items():
            @pl.when(place_at == a)
            def _():
                for x in range(pieces):
                    over_z(slot, k, x, True, to).start()

    over_y(0, 0).start()
    for k in range(2):
        send_own(k)
    second_hop, third_hop = [], []
    for k in range(lines):
        if k:
            first_hop[k - 1].wait_recv()
        c = line(lines - k) + low
        second_hop.append(remote(at_home(c), at_home(c), g_send.at[1, k], g_recv.at[1, k], dist, partner))
        second_hop[-1].start()
        third_hop.append(remote(at_home(c), across(c), g_send.at[2, k], g_recv.at[2, k], before, me))
        third_hop[-1].start()
    over_y(0, 1).start()
    for k in range(2):
        over_y(1, k).start()

    def relay(a, slot, k):
        @pl.when(place_at == a)
        def _():
            for x in range(pieces):
                over_z(slot, k, x, False, a).wait_recv()
                over_z(slot, k, x, False, a + 1).start()

    from_y(0, 0).wait_recv()
    send_own(2)
    relay(2, 1, 0)
    relay(1, 0, 0)
    relay(2, 1, 1)

    for k in range(lines):
        second_hop[k].wait_recv()
        c = line(lines - k) + 1 - low
        third_hop.append(remote(at_home(c), across(c), g_send.at[3, k], g_recv.at[3, k], before, me))
        third_hop[-1].start()

    relay(2, 1, 2)
    relay(2, 0, 0)
    relay(1, 0, 1)
    for copy in third_hop:
        copy.wait_recv()

    size = atoms * slots
    occ_at, virt_at, pair_at = size * slots, 2 * size * slots, 3 * size * slots
    total = n * blocks * groups
    base = dist * n * blocks
    atom = dist * lines + high

    def position(value):
        shift = value - base
        return jnp.minimum(jnp.where(shift < 0, shift + total, shift), 2 * n * blocks - 1)

    def atom_at(a):
        return dist * lines + flip(a)

    def feeding(a, s, j):
        r, live = jnp.int32(0), jnp.int32(0)
        for x in range(slots):
            hit = ids[(a * slots + s) * slots + x] == j
            r, live = jnp.where(hit, x, r), jnp.where(hit, 1, live)
        return r, live

    def green(a, s, r, live):
        at = (a * slots + s) * slots + r
        return position(ids[occ_at + at]), position(ids[virt_at + at]), live.astype(F32)

    for t in range(slots):
        virt = []
        for o in range(slots):
            r, live = feeding(atom, o, t)
            occ_pos, virt_pos, live = green(atom, o, r, live)
            virt.append((table[virt_pos].astype(F32) * live).astype(BF16))
            gather[t * BLK:(t + 1) * BLK, o * LANES:(o + 1) * LANES] = table[occ_pos]
        b = nt(turn_v[...], jnp.concatenate(virt, axis=1)).astype(BF16)
        second_op[0, :, t * LANES:(t + 1) * LANES] = nt(lift[t][:, :BLK], b).astype(BF16)
    size_op = slots * BLK
    unit = (iota((size_op, size_op), 0) == iota((size_op, size_op), 1)).astype(BF16)
    first_op[0] = nt(unit, nn(gather[...], place[...]).astype(BF16)).astype(BF16)

    from_y(0, 1).wait_recv()
    send_own(3)

    def operators(slot, a):
        other = atom_at(a)
        for t in range(slots):
            pair = ids[pair_at + atom * slots + t]
            s, met = jnp.int32(0), jnp.int32(0)
            for x in range(slots):
                hit = ids[pair_at + other * slots + x] == pair
                s, met = jnp.where(hit, x, s), jnp.where(hit, 1, met)
            virt = []
            for o in range(slots):
                r, live = feeding(other, s, o)
                occ_pos, virt_pos, live = green(other, s, r, live * met)
                virt.append(
                    (table[virt_pos, pl.ds(pl.multiple_of(low * half, half), half), :].astype(F32) * live).astype(BF16)
                )
                gather[o * BLK:(o + 1) * BLK, t * LANES:(t + 1) * LANES] = table[occ_pos]
            second_op[1 + slot, :, t * LANES:(t + 1) * LANES] = nt(lift[t], jnp.concatenate(virt, axis=0)).astype(BF16)
        first_op[1 + slot] = nn(gather[...], place[...]).astype(BF16)

    used = {0: (0, (1, 2, 3)), 1: (1, (2, 3)), 2: (3, (2,))}

    def wanted_here(slot):
        hit = place_at == used[slot][1][0]
        for a in used[slot][1][1:]:
            hit = hit | (place_at == a)
        return hit

    for slot in used:
        @pl.when(wanted_here(slot))
        def _():
            operators(slot, used[slot][0])

    r_, c_ = iota((LANES, LANES), 0), iota((LANES, LANES), 1)
    for slot in used:
        other = atom_at(used[slot][0])
        match = jnp.zeros((LANES, LANES), F32)
        for s in range(slots):
            for t in range(slots):
                hit = jnp.where(ids[pair_at + atom * slots + s] == ids[pair_at + other * slots + t], 1.0, 0.0)
                match = jnp.where((r_ // half == s) & (c_ // half == t), hit.astype(F32), match)
        match_op[:, slot * LANES:(slot + 1) * LANES] = jnp.where(r_ % half == c_ % half, match, 0.0).astype(BF16)

    lanes2 = (iota((BLK, 2 * LANES), 1) // half) % slots

    def first(k, u):
        got = nn(xg[...], second_op[k]).astype(BF16)
        for i in range(part_rows):
            for t in range(slots):
                wg[u, i, t * BLK:(t + 1) * BLK, :] = got[i * BLK:(i + 1) * BLK, t * LANES:(t + 1) * LANES]

    def second(k, u):
        for p in range(part_rows // 2):
            both = nn(first_op[k], jnp.concatenate([wg[u, 2 * p], wg[u, 2 * p + 1]], axis=1))
            res = both[:BLK]
            for o in range(1, slots):
                res = jnp.where(lanes2 == o, both[o * BLK:(o + 1) * BLK], res)
            for x in range(2):
                uf[u, (2 * p + x) * BLK:(2 * p + x + 1) * BLK, :] = res[:, x * LANES:(x + 1) * LANES]

    def keep(k, u, at_rows):
        for m in range(BLK):
            stack[k, at_rows, m * LANES:(m + 1) * LANES] = uf[u, pl.ds(m, part_rows, stride=BLK), :].astype(BF16)

    def two_stacks(k, at_rows):
        for u in range(2):
            first(k + u, u)
        for u in range(2):
            second(k + u, u)
        for u in range(2):
            keep(k + u, u, at_rows)

    def reorder(at_rows):
        x = jnp.concatenate([stack[0, at_rows, m * LANES:(m + 1) * LANES] for m in range(BLK)], axis=0)
        got = nn(x, match_op[...]).astype(BF16)
        below = pl.ds(at_rows.start + BLK, part_rows)
        for m in range(BLK):
            for slot in used:
                stack[1 + slot, below, m * LANES:(m + 1) * LANES] = got[
                    m * part_rows:(m + 1) * part_rows, slot * LANES:(slot + 1) * LANES
                ]

    def spread(at_rows):
        for h in range(2):
            for m in range(BLK):
                tf[h, m * part_rows:(m + 1) * part_rows, :] = halves[h, at_rows, m * LANES:(m + 1) * LANES].astype(F32)
            for i in range(part_rows):
                xg[i * BLK:(i + 1) * BLK, h * LANES:(h + 1) * LANES] = tf[
                    h, pl.ds(i, BLK, stride=part_rows), :
                ].astype(BF16)

    due = ((0, 2, 0, 1), (1, 2, 1, 3), (1, 1, 0, 2), (2, 2, 0, 2), (4, 1, 0, 3), (5, 2, 0, 3))

    def step(g, carry):
        y = jnp.where(g < 2, low, 1 - low)
        at_rows = pl.ds(pl.multiple_of(y * rows + lax.rem(g, 2) * part_rows, part_rows), part_rows)
        for x in range(2):
            @pl.when(g == 2 + x)
            def _():
                from_y(1, x).wait_recv()

        def relays(side):
            for at, a, slot, group in due:
                if at % 2 == side:
                    @pl.when(g == at // 2)
                    def _():
                        relay(a, slot, group)

        spread(at_rows)
        two_stacks(0, at_rows)
        reorder(at_rows)
        relays(0)

        @pl.when(place_at >= 2)
        def _():
            two_stacks(2, at_rows)
        relays(1)
        return carry

    lax.fori_loop(0, 4, step, 0)

    for c in range(lines):
        blk[c] = jnp.zeros((BLK, LANES), F32)

    def lay(x):
        return jnp.concatenate([x, jnp.zeros((BLK, LANES - BLK), F32)], axis=1)

    blk[high] = lay(nt(stack[0, :BLK], halves[low]))

    def returned(slot, y):
        a = used[slot][0]
        return remote(
            cross.at[slot, pl.ds(y * rows, rows)], cross_in.at[place_at, low], c_send.at[slot, y],
            c_recv.at[place_at, low], dist, at_place(a, y),
        )

    def product(slot):
        a = used[slot][0]
        for k in range(4):
            if slot == 2:
                for x in range(pieces):
                    over_z(slot, k, x, False, a).wait_recv()
            else:
                @pl.when(place_at == 3)
                def _():
                    for x in range(pieces):
                        over_z(slot, k, x, False, a).wait_recv()
        both = nt(moved[slot], stack[1 + slot])
        cross[slot] = both
        for y in range(2):
            returned(slot, y).start()
        blk[flip(a)] = lay(both.T[BLK:])

    for slot in (2, 1, 0):
        @pl.when(wanted_here(slot))
        def _():
            product(slot)

    other_rows = pl.ds(pl.multiple_of((1 - low) * rows, rows), rows)
    to_partner = remote(blk.at[:, other_rows], partner_in, p_send.at[0], p_recv.at[0], dist, partner)
    to_partner.start()

    came = {1: (0,), 2: (0, 1, 3), 3: (0, 1)}
    for src, takers in came.items():
        for a in takers:
            @pl.when(place_at == a)
            def _():
                for y in range(2):
                    remote(
                        cross.at[0, pl.ds(0, rows)], cross_in.at[src, y], c_send.at[0, 0], c_recv.at[src, y], dist, me
                    ).wait_recv()
                blk[flip(src), own_rows] = cross_in[src, 0] + cross_in[src, 1]
    to_partner.wait()
    tiles = [(blk[c, own_rows] + partner_in[c])[:, :BLK] for c in range(lines)]
    out_ref[...] = jnp.concatenate(tiles, axis=1)

    for copy in first_hop + second_hop + third_hop:
        copy.wait_send()
    for k in range(2):
        over_y(0, k).wait_send()
        over_y(1, k).wait_send()
    for slot, senders in {0: (0, 1, 2), 1: (1, 2), 2: (3,)}.items():
        for a in senders:
            @pl.when(place_at == a)
            def _():
                for k in range(4):
                    for x in range(pieces):
                        over_z(slot, k, x, False, 0).wait_send()

        @pl.when(wanted_here(slot))
        def _():
            for y in range(2):
                returned(slot, y).wait_send()


def on_line(n, groups, atoms, ids, tensor, green):
    slots, rows, width = tensor.shape
    blocks = green.shape[0] // 2
    lines = n // 2
    deep = BLK * LANES
    part_rows = rows // 2
    vmem = pl.BlockSpec(memory_space=pltpu.VMEM)
    dma = pltpu.SemaphoreType.DMA
    return pl.pallas_call(
        functools.partial(line_kernel, n, groups, atoms),
        out_shape=jax.ShapeDtypeStruct((rows, lines * BLK), F32),
        in_specs=[pl.BlockSpec(memory_space=pltpu.SMEM), vmem, vmem],
        out_specs=vmem,
        scratch_shapes=[
            pltpu.VMEM((2 * n * blocks, BLK, LANES), BF16),
            pltpu.VMEM((2, BLK, deep), BF16),
            pltpu.VMEM((3, BLK, deep), BF16),
            pltpu.VMEM((4, 2 * BLK, deep), BF16),
            pltpu.VMEM((LANES, 3 * LANES), BF16),
            pltpu.VMEM((2, part_rows * BLK, LANES), F32),
            pltpu.VMEM((part_rows * BLK, 2 * LANES), BF16),
            pltpu.VMEM((2, part_rows, slots * BLK, LANES), BF16),
            pltpu.VMEM((2, part_rows * BLK, LANES), F32),
            pltpu.VMEM((4, slots * BLK, slots * BLK), BF16),
            pltpu.VMEM((4, 2 * LANES, slots * LANES), BF16),
            pltpu.VMEM((slots * BLK, slots * LANES), BF16),
            pltpu.VMEM((slots * LANES, slots * LANES), BF16),
            pltpu.VMEM((slots * LANES, slots * BLK), BF16),
            pltpu.VMEM((slots, 2 * LANES, LANES), BF16),
            pltpu.VMEM((LANES, slots * LANES), BF16),
            pltpu.VMEM((lines, BLK, LANES), F32),
            pltpu.VMEM((3, BLK, LANES), F32),
            pltpu.VMEM((lines, rows, LANES), F32),
            pltpu.VMEM((lines, 2, rows, LANES), F32),
            dma((4, lines)),
            dma((4, lines)),
            dma((2, 2)),
            dma((2, 2)),
            dma((3, 8)),
            dma((3, 8)),
            dma((3, 2)),
            dma((lines, 2)),
            dma((1,)),
            dma((1,)),
        ],
        compiler_params=pltpu.CompilerParams(
            collective_id=1, has_side_effects=True, vmem_limit_bytes=48 * 2**20
        ),
    )(ids, tensor, green)


def solution(mesh):
    n = mesh.shape["ctr"]
    groups = mesh.shape["dist"]

    def shards(three_centre, occupied_green, virtual_green, pair_index, source_slot, occupied_index, virtual_index):
        rows, slots, width = three_centre.shape
        blocks = occupied_green.shape[0]
        atoms = pair_index.shape[0]
        chunks = width // LANES
        cols = width // n
        tensor = jnp.transpose(three_centre, (1, 0, 2))
        green = jnp.concatenate([virtual_green, occupied_green], axis=0).reshape(2 * blocks, BLK, BLK)
        ids = jnp.concatenate(
            [x.reshape(-1) for x in (source_slot, occupied_index, virtual_index, pair_index)]
        )
        vmem = pl.BlockSpec(memory_space=pltpu.VMEM)
        dma = pltpu.SemaphoreType.DMA
        if n == 8 and groups % 2 == 0 and rows * 2 == BLK:
            return on_line(n, groups, atoms, ids, tensor, green)
        return pl.pallas_call(
            functools.partial(kernel, n, groups, atoms),
            out_shape=jax.ShapeDtypeStruct((rows, n * rows), F32),
            in_specs=[pl.BlockSpec(memory_space=pltpu.SMEM), vmem, vmem],
            out_specs=vmem,
            scratch_shapes=[
                pltpu.VMEM((2 * n * blocks, BLK, LANES), BF16),
                pltpu.VMEM((rows * chunks, LANES), F32),
                pltpu.VMEM((slots, rows * chunks, LANES), BF16),
                pltpu.VMEM((slots * BLK, rows * LANES), BF16),
                pltpu.VMEM((BLK, slots * BLK), BF16),
                pltpu.VMEM((slots, n, rows, cols), BF16),
                pltpu.VMEM((n, slots, rows, cols), BF16),
                pltpu.VMEM((n, slots, rows, cols), BF16),
                pltpu.VMEM((n * rows, NPR * cols), BF16),
                pltpu.VMEM((n * rows, NPR * cols), BF16),
                pltpu.VMEM((n * rows, n * rows), F32),
                pltpu.VMEM((n * rows, n * rows), BF16),
                pltpu.VMEM((n, rows, n * rows), BF16),
                dma((4, n // 2)),
                dma((4, n // 2)),
                dma((n,)),
                dma((n,)),
                dma((slots, n)),
                dma((slots, n)),
                dma((n,)),
                dma((n,)),
                dma((2,)),
            ],
            compiler_params=pltpu.CompilerParams(
                collective_id=0, has_side_effects=True, vmem_limit_bytes=48 * 2**20
            ),
        )(ids, tensor, green)

    return jax.shard_map(
        shards,
        mesh=mesh,
        in_specs=(
            P(("dist", "ctr"), None, None),
            P(("dist", "ctr"), None),
            P(("dist", "ctr"), None),
            P(),
            P(),
            P(),
            P(),
        ),
        out_specs=P(("dist", "ctr"), None),
        check_vma=False,
    )
```

```python
import functools

import jax
import jax.numpy as jnp
from jax import lax
from jax.experimental import pallas as pl
from jax.experimental.pallas import tpu as pltpu
from jax.sharding import PartitionSpec as P

BLK = 64
NPR = 8
LANES = 128
F32 = jnp.float32
BF16 = jnp.bfloat16


def kernel(n, groups, atoms, ids, t_ref, green_ref, out_ref, table, tf, tt, wcat, ocat, usend, urecv, trecv,
           uk, tk, part, psend, precv, g_send, g_recv, t_send, t_recv, u_send, u_recv, p_send, p_recv, own_sem):
    slots, rows, width = t_ref.shape
    chunks = width // LANES
    blocks = green_ref.shape[0] // 2
    cols = width // n
    per = cols // LANES
    dist = lax.axis_index("dist")
    me = lax.axis_index("ctr")
    before = lax.rem(dist + groups - 1, groups)
    after = lax.rem(dist + 1, groups)

    far_first = sorted(range(1, n), key=lambda k: -min(k, n - k))

    def ahead(k):
        return lax.rem(me + k, n)

    def signal(d, c):
        pl.semaphore_signal(barrier, inc=1, device_id=(d, c), device_id_type=pl.DeviceIdType.MESH)

    def remote(src, dst, send, recv, d, c):
        return pltpu.make_async_remote_copy(
            src_ref=src, dst_ref=dst, send_sem=send, recv_sem=recv, device_id=(d, c),
            device_id_type=pl.DeviceIdType.MESH,
        )

    barrier = pltpu.get_barrier_semaphore()
    for k in range(1, n):
        signal(dist, ahead(k))
    signal(before, me)
    signal(after, me)

    row = lax.broadcasted_iota(jnp.int32, (BLK, BLK), 0)
    col = lax.broadcasted_iota(jnp.int32, (BLK, BLK), 1)
    half = BLK // 2
    wanted = jnp.where(row < half, 2 * row, 2 * (row - half) + 1)
    perm = (wanted == col).astype(BF16)
    mine = me * blocks
    for b in range(blocks):
        occ = green_ref[blocks + b]
        turned = lax.dot_general(perm, occ, (((1,), (1,)), ((), ())), preferred_element_type=F32).astype(BF16)
        turned = lax.dot_general(turned, perm, (((1,), (1,)), ((), ())), preferred_element_type=F32).astype(BF16)
        table[mine + b] = jnp.concatenate([green_ref[b], turned], axis=1)

    pl.semaphore_wait(barrier, n + 1)

    lines = n // 2
    high, low = me // 2, lax.rem(me, 2)
    partner = high * 2 + 1 - low

    def line(k):
        return lax.rem(high + k, lines) * 2

    def at_home(c):
        return table.at[pl.ds(c * blocks, blocks)]

    def across(c):
        return table.at[pl.ds((n + c) * blocks, blocks)]

    first_hop = [
        remote(at_home(me), at_home(me), g_send.at[0, k], g_recv.at[0, k], dist, line(k) + low)
        for k in range(1, lines)
    ]
    for copy in first_hop:
        copy.start()

    def t_part(c):
        return t_ref.at[:, :, pl.ds(pl.multiple_of(c * cols, LANES), cols)]

    tensor = [
        remote(t_part(ahead(k)), trecv.at[me], t_send.at[k], t_recv.at[k], dist, ahead(k)) for k in far_first
    ]
    for copy in tensor:
        copy.start()
    own_t = pltpu.make_async_copy(t_part(me), trecv.at[me], own_sem.at[0])
    own_t.start()

    second_hop, third_hop = [], []
    for k in range(lines):
        if k:
            first_hop[k - 1].wait_recv()
        c = line(lines - k) + low
        second_hop.append(remote(at_home(c), at_home(c), g_send.at[1, k], g_recv.at[1, k], dist, partner))
        second_hop[-1].start()
        third_hop.append(remote(at_home(c), across(c), g_send.at[2, k], g_recv.at[2, k], before, me))
        third_hop[-1].start()

    def turn(s, carry):
        for j in range(chunks):
            tf[j * rows:(j + 1) * rows, :] = t_ref[s, :, j * LANES:(j + 1) * LANES].astype(F32)
        for i in range(rows):
            tt[s, i * chunks:(i + 1) * chunks, :] = tf[pl.ds(i, chunks, stride=rows), :].astype(BF16)
        return carry

    lax.fori_loop(0, slots, turn, 0)

    for k in range(lines):
        second_hop[k].wait_recv()
        c = line(lines - k) + 1 - low
        third_hop.append(remote(at_home(c), across(c), g_send.at[3, k], g_recv.at[3, k], before, me))
        third_hop[-1].start()
    for copy in third_hop:
        copy.wait()
    for copy in first_hop + second_hop:
        copy.wait_send()

    size = atoms * slots
    atom = (dist * n + me) * rows // BLK
    total = n * blocks * groups
    base = dist * n * blocks

    def position(value):
        shift = value - base
        return jnp.minimum(jnp.where(shift < 0, shift + total, shift), 2 * n * blocks - 1)

    step_rows = 8 * chunks
    lane = lax.broadcasted_iota(jnp.int32, (half, LANES), 1)

    def update(s, carry):
        at = (atom * slots + s) * slots
        for r in range(slots):
            src = ids[at + r]
            live = jnp.where(src >= 0, 1.0, 0.0).astype(F32)
            src = jnp.maximum(src, 0)
            virt = table[position(ids[2 * size * slots + at + r])].astype(F32)[:, :BLK] * live
            zero = jnp.zeros((BLK, LANES), F32)
            twice = jnp.concatenate([virt, virt], axis=1)
            weight = jnp.concatenate(
                [jnp.concatenate([twice, zero], axis=1), jnp.concatenate([zero, twice], axis=1)], axis=0
            ).astype(BF16)
            ocat[:, r * BLK:(r + 1) * BLK] = table[position(ids[size * slots + at + r])][:, BLK:]
            for h in range(rows // 8):
                got = jnp.dot(
                    tt[src, h * step_rows:(h + 1) * step_rows, :], weight, preferred_element_type=F32
                ).astype(BF16)
                for x in range(8):
                    i = h * 8 + x
                    for e in range(2):
                        wcat[r * BLK + e * half:r * BLK + (e + 1) * half, i * LANES:(i + 1) * LANES] = got[
                            x * chunks:(x + 1) * chunks, e * LANES:(e + 1) * LANES
                        ]
        occ = ocat[...]
        for h in range(rows // 4):
            both = jnp.dot(occ, wcat[:, h * 4 * LANES:(h + 1) * 4 * LANES], preferred_element_type=F32)
            for x in range(4):
                i = h * 4 + x
                piece = both[:, x * LANES:(x + 1) * LANES]
                tf[i * chunks:(i + 1) * chunks, :] = jnp.where(lane < BLK, piece[:half], piece[half:])
        for q in range(chunks):
            usend[s, q // per, :, (q % per) * LANES:(q % per + 1) * LANES] = tf[
                pl.ds(q, rows, stride=chunks), :
            ].astype(BF16)
        for k in far_first:
            sent(s, k).start()
        return carry

    def sent(s, k):
        return remote(
            usend.at[s, ahead(k)], urecv.at[me, s], u_send.at[s, k], u_recv.at[s, k], dist, ahead(k)
        )

    lax.fori_loop(0, slots, update, 0)
    own_u = pltpu.make_async_copy(usend.at[:, me], urecv.at[me], own_sem.at[1])
    own_u.start()
    own_t.wait()
    for copy in tensor:
        copy.wait()

    first = dist * (n * rows // BLK)
    pairs = 3 * size * slots

    def pick(src, pair, p):
        where = pairs + (first + p * rows // BLK) * slots
        slot = jnp.int32(0)
        live = jnp.int32(0)
        for s in range(slots):
            hit = ids[where + s] == pair
            slot = jnp.where(hit, s, slot)
            live = jnp.where(hit, 1, live)
        return (src[p, slot].astype(F32) * live.astype(F32)).astype(BF16)

    def at_rows(p):
        return pl.ds(pl.multiple_of(p * rows, rows), rows)

    def at_cols(pair):
        return pl.ds(pl.multiple_of(pair * cols, LANES), cols)

    def tensor_pair(pair, carry):
        def gather(p, inner):
            tk[at_rows(p), at_cols(pair)] = pick(trecv, pair, p)
            return inner

        return lax.fori_loop(0, n, gather, carry)

    lax.fori_loop(0, NPR, tensor_pair, 0)

    def updated_pairs(p):
        where = pairs + (first + p * rows // BLK) * slots

        def one_pair(pair, carry):
            chosen = jnp.zeros((rows, cols), F32)
            for s in range(slots):
                hit = jnp.where(ids[where + s] == pair, 1.0, 0.0).astype(F32)
                chosen = chosen + urecv[p, s].astype(F32) * hit
            uk[at_rows(p), at_cols(pair)] = chosen.astype(BF16)
            return carry

        lax.fori_loop(0, NPR, one_pair, 0)

    own_u.wait()
    updated_pairs(me)
    for k in far_first[::-1]:
        for s in range(slots):
            sent(s, k).wait()
        updated_pairs(lax.rem(me - k + n, n))

    def block(p, carry):
        at = pl.ds(pl.multiple_of(p * 256, 256), 256)
        total = lax.dot_general(uk[at, :], tk[...], (((1,), (1,)), ((), ())), preferred_element_type=F32)
        part[at, :] = total
        psend[at, :] = total.astype(BF16)
        return carry

    lax.fori_loop(0, n * rows // 256, block, 0)

    def p_part(c):
        return psend.at[pl.ds(pl.multiple_of(c * rows, rows), rows)]

    shares = [
        remote(p_part(ahead(k)), precv.at[k], p_send.at[k], p_recv.at[k], dist, ahead(k)) for k in far_first
    ]
    for copy in shares:
        copy.start()
    result = part[pl.ds(pl.multiple_of(me * rows, rows), rows), :]
    for k, copy in zip(far_first, shares):
        copy.wait()
        result = result + precv[k].astype(F32)
    out_ref[...] = result


def iota(shape, dim):
    return lax.broadcasted_iota(jnp.int32, shape, dim)


def nt(a, b):
    return lax.dot_general(a, b, (((1,), (1,)), ((), ())), preferred_element_type=F32)


def nn(a, b):
    return jnp.dot(a, b, preferred_element_type=F32)


def line_kernel(n, groups, atoms, source_ids, occ_ids, virt_ids, pair_ids, t_ref, green_ref, out_ref, table, halves, moved, stack, match_op, tf, xg, wg, uf,
                first_op, second_op, gather, select, place, lift, turn_v, blk, cross, partner_in, cross_in,
                g_send, g_recv, y_send, y_recv, m_send, m_recv, c_send, c_recv, p_send, p_recv):
    slots, rows, width = t_ref.shape
    blocks = green_ref.shape[0] // 2
    chunks = width // LANES
    half = BLK // 2
    part_rows = rows // 2
    deep = BLK * LANES
    dist = lax.axis_index("dist")
    me = lax.axis_index("ctr")
    before = lax.rem(dist + groups - 1, groups)
    after = lax.rem(dist + 1, groups)
    lines = n // 2
    high, low = me // 2, lax.rem(me, 2)
    partner = high * 2 + 1 - low
    mirrored = lax.rem(dist, 2)

    def flip(a):
        return jnp.where(mirrored == 1, lines - 1 - a, a)

    place_at = flip(high)

    def at_place(a, y):
        return flip(a) * 2 + y

    def signal(d, c):
        pl.semaphore_signal(barrier, inc=1, device_id=(d, c), device_id_type=pl.DeviceIdType.MESH)

    def remote(src, dst, send, recv, d, c):
        return pltpu.make_async_remote_copy(
            src_ref=src, dst_ref=dst, send_sem=send, recv_sem=recv, device_id=(d, c),
            device_id_type=pl.DeviceIdType.MESH,
        )

    barrier = pltpu.get_barrier_semaphore()
    for k in range(1, n):
        signal(dist, lax.rem(me + k, n))
    signal(before, me)
    signal(after, me)

    row, col = iota((BLK, BLK), 0), iota((BLK, BLK), 1)
    wanted = jnp.where(row < half, 2 * row, 2 * (row - half) + 1)
    perm = (wanted == col).astype(BF16)
    mine = me * blocks
    for b in range(blocks):
        turned = nn(perm, green_ref[blocks + b]).astype(BF16)
        turned = nt(turned, perm).astype(BF16)
        table[mine + b] = jnp.concatenate([green_ref[b], turned], axis=1)

    wide = slots * LANES
    r_, c_ = iota((wide, wide), 0), iota((wide, wide), 1)
    select[...] = (
        r_ == ((c_ // half) % slots) * LANES + ((c_ // LANES) % 2) * BLK + (c_ // (2 * LANES)) * half + c_ % half
    ).astype(BF16)
    r_, c_ = iota((wide, slots * BLK), 0), iota((wide, slots * BLK), 1)
    place[...] = ((r_ % LANES >= BLK) & (c_ == (r_ // LANES) * BLK + r_ % LANES - BLK)).astype(BF16)
    r_, c_ = iota((2 * LANES, LANES), 0), iota((2 * LANES, LANES), 1)
    for t in range(slots):
        lift[t] = ((c_ < BLK) & (r_ == (c_ // half) * LANES + t * half + c_ % half)).astype(BF16)
    r_, c_ = iota((LANES, wide), 0), iota((LANES, wide), 1)
    turn_v[...] = ((r_ // half == c_ // LANES) & (c_ % LANES == low * half + r_ % half)).astype(BF16)

    own_rows = pl.ds(pl.multiple_of(low * rows, rows), rows)
    per = 8
    for q in range(0, chunks, per):
        x = jnp.concatenate(
            [
                jnp.concatenate([t_ref[j, :, (q + p) * LANES:(q + p + 1) * LANES] for j in range(slots)], axis=1)
                for p in range(per)
            ],
            axis=0,
        )
        got = nn(x, select[...]).astype(BF16)
        for p in range(per):
            for h in range(2):
                for e in range(2):
                    at = (e * half + q + p) * LANES
                    halves[h, own_rows, at:at + LANES] = got[
                        p * rows:(p + 1) * rows, (h * 2 + e) * LANES:(h * 2 + e + 1) * LANES
                    ]

    pl.semaphore_wait(barrier, n + 1)

    def line(k):
        return lax.rem(high + k, lines) * 2

    def at_home(c):
        return table.at[pl.ds(c * blocks, blocks)]

    def across(c):
        return table.at[pl.ds((n + c) * blocks, blocks)]

    first_hop = [
        remote(at_home(me), at_home(me), g_send.at[0, k], g_recv.at[0, k], dist, line(k) + low)
        for k in range(1, lines)
    ]
    for copy in first_hop:
        copy.start()
    second_hop, third_hop = [], []

    def onward(k):
        c = line(lines - k) + low
        second_hop.append(remote(at_home(c), at_home(c), g_send.at[1, k], g_recv.at[1, k], dist, partner))
        second_hop[-1].start()
        third_hop.append(remote(at_home(c), across(c), g_send.at[2, k], g_recv.at[2, k], before, me))
        third_hop[-1].start()

    onward(0)

    def rows_of(k):
        y = low if k < 2 else 1 - low
        return pl.ds(pl.multiple_of(y * rows + (k % 2) * part_rows, part_rows), part_rows)

    pieces = 2
    piece = deep // pieces

    def over_y(phase, k, x):
        h = 1 - low if phase == 0 else low
        at = halves.at[h, rows_of(k), pl.ds(x * piece, piece)]
        sem = k * pieces + x
        return remote(at, at, y_send.at[phase, sem], y_recv.at[phase, sem], dist, partner)

    def from_y(phase, k, x):
        at = halves.at[low if phase == 0 else 1 - low, rows_of(2 + k), pl.ds(x * piece, piece)]
        sem = k * pieces + x
        return remote(at, at, y_send.at[phase, sem], y_recv.at[phase, sem], dist, partner)

    def over_z(slot, k, x, own, to):
        at, lanes = rows_of(k), pl.ds(x * piece, piece)
        src = halves.at[low, at, lanes] if own else moved.at[slot, at, lanes]
        sem = k * pieces + x
        return remote(
            src, moved.at[slot, at, lanes], m_send.at[slot, sem], m_recv.at[slot, sem], dist, at_place(to, low)
        )

    def spread(g):
        at_rows = rows_of(g)
        for h in range(2):
            for m in range(BLK):
                tf[h, m * part_rows:(m + 1) * part_rows, :] = halves[h, at_rows, m * LANES:(m + 1) * LANES].astype(F32)
            for i in range(part_rows):
                xg[g % 2, i * BLK:(i + 1) * BLK, h * LANES:(h + 1) * LANES] = tf[
                    h, pl.ds(i, BLK, stride=part_rows), :
                ].astype(BF16)

    starts = {0: (0, 1), 1: (1, 2), 3: (2, 2)}

    def send_own(k, places):
        for a in places:
            slot, to = starts[a]

            @pl.when(place_at == a)
            def _():
                for x in range(pieces):
                    over_z(slot, k, x, True, to).start()

    over_y(0, 0, 0).start()
    over_y(0, 0, 1).start()
    for k in range(2):
        send_own(k, (0, 1))
    for k in range(1, lines):
        first_hop[k - 1].wait_recv()
        onward(k)
    for phase, k in ((0, 1), (1, 0), (1, 1)):
        for x in range(pieces):
            over_y(phase, k, x).start()

    def relay(a, slot, k):
        @pl.when(place_at == a)
        def _():
            for x in range(pieces):
                over_z(slot, k, x, False, a).wait_recv()
                over_z(slot, k, x, False, a + 1).start()

    def third(k):
        second_hop[k].wait_recv()
        c = line(lines - k) + 1 - low
        third_hop.append(remote(at_home(c), across(c), g_send.at[3, k], g_recv.at[3, k], before, me))
        third_hop[-1].start()

    third(0)
    for x in range(pieces):
        from_y(0, 0, x).wait_recv()
    send_own(2, (0, 1))
    for k in range(1, lines):
        third(k)
    relay(1, 0, 0)
    relay(2, 1, 0)
    relay(2, 1, 1)
    relay(1, 0, 1)
    spread(0)
    spread(1)
    relay(2, 1, 2)
    relay(2, 0, 0)
    for copy in third_hop:
        copy.wait_recv()
    for k in range(3):
        send_own(k, (3,))

    total = n * blocks * groups
    base = dist * n * blocks
    atom = dist * lines + high

    def position(value):
        shift = value - base
        return jnp.minimum(jnp.where(shift < 0, shift + total, shift), 2 * n * blocks - 1)

    def atom_at(a):
        return dist * lines + flip(a)

    def feeding(a, s, j):
        r, live = jnp.int32(0), jnp.int32(0)
        for x in range(slots):
            hit = source_ids[s, x, a] == j
            r, live = jnp.where(hit, x, r), jnp.where(hit, 1, live)
        return r, live

    def green(a, s, r, live):
        return position(occ_ids[s, r, a]), position(virt_ids[s, r, a]), live.astype(F32)

    for t in range(slots):
        virt = []
        for o in range(slots):
            r, live = feeding(atom, o, t)
            occ_pos, virt_pos, live = green(atom, o, r, live)
            virt.append((table[virt_pos].astype(F32) * live).astype(BF16))
            gather[3, t * BLK:(t + 1) * BLK, o * LANES:(o + 1) * LANES] = table[occ_pos]
        b = nt(turn_v[...], jnp.concatenate(virt, axis=1)).astype(BF16)
        second_op[0, :, t * LANES:(t + 1) * LANES] = nt(lift[t][:, :BLK], b).astype(BF16)
    size_op = slots * BLK
    unit = (iota((size_op, size_op), 0) == iota((size_op, size_op), 1)).astype(BF16)
    first_op[0] = nt(unit, nn(gather[3], place[...]).astype(BF16)).astype(BF16)

    for x in range(pieces):
        from_y(0, 1, x).wait_recv()
    send_own(3, (0, 1, 3))

    def operators(slot, a):
        other = atom_at(a)
        for t in range(slots):
            pair = pair_ids[t, atom]
            s, met = jnp.int32(0), jnp.int32(0)
            for x in range(slots):
                hit = pair_ids[x, other] == pair
                s, met = jnp.where(hit, x, s), jnp.where(hit, 1, met)
            virt = []
            for o in range(slots):
                r, live = feeding(other, s, o)
                occ_pos, virt_pos, live = green(other, s, r, live * met)
                virt.append(
                    (table[virt_pos, pl.ds(pl.multiple_of(low * half, half), half), :].astype(F32) * live).astype(BF16)
                )
                gather[slot, o * BLK:(o + 1) * BLK, t * LANES:(t + 1) * LANES] = table[occ_pos]
            second_op[1 + slot, :, t * LANES:(t + 1) * LANES] = nt(lift[t], jnp.concatenate(virt, axis=0)).astype(BF16)
        first_op[1 + slot] = nn(gather[slot], place[...]).astype(BF16)

    used = {0: (0, (1, 2, 3)), 1: (1, (2, 3)), 2: (3, (2,))}

    def wanted_here(slot):
        hit = place_at == used[slot][1][0]
        for a in used[slot][1][1:]:
            hit = hit | (place_at == a)
        return hit

    for slot in used:
        operators(slot, used[slot][0])

    r_, c_ = iota((LANES, LANES), 0), iota((LANES, LANES), 1)
    for slot in used:
        other = atom_at(used[slot][0])
        match = jnp.zeros((LANES, LANES), F32)
        for s in range(slots):
            for t in range(slots):
                hit = jnp.where(pair_ids[s, atom] == pair_ids[t, other], 1.0, 0.0)
                match = jnp.where((r_ // half == s) & (c_ // half == t), hit.astype(F32), match)
        match_op[:, slot * LANES:(slot + 1) * LANES] = jnp.where(r_ % half == c_ % half, match, 0.0).astype(BF16)

    lanes2 = (iota((BLK, 2 * LANES), 1) // half) % slots

    def first(k, u, g):
        got = nn(xg[lax.rem(g, 2)], second_op[k]).astype(BF16)
        for i in range(part_rows):
            for t in range(slots):
                wg[u, i, t * BLK:(t + 1) * BLK, :] = got[i * BLK:(i + 1) * BLK, t * LANES:(t + 1) * LANES]

    def second(k, u):
        for p in range(part_rows // 2):
            both = nn(first_op[k], jnp.concatenate([wg[u, 2 * p], wg[u, 2 * p + 1]], axis=1))
            res = both[:BLK]
            for o in range(1, slots):
                res = jnp.where(lanes2 == o, both[o * BLK:(o + 1) * BLK], res)
            for x in range(2):
                uf[u, (2 * p + x) * BLK:(2 * p + x + 1) * BLK, :] = res[:, x * LANES:(x + 1) * LANES]

    def keep(k, u, at_rows):
        for m in range(BLK):
            stack[k, at_rows, m * LANES:(m + 1) * LANES] = uf[u, pl.ds(m, part_rows, stride=BLK), :].astype(BF16)

    def two_stacks(k, at_rows, g):
        for u in range(2):
            first(k + u, u, g)
        for u in range(2):
            second(k + u, u)
        for u in range(2):
            keep(k + u, u, at_rows)

    def reorder(at_rows):
        x = jnp.concatenate([stack[0, at_rows, m * LANES:(m + 1) * LANES] for m in range(BLK)], axis=0)
        got = nn(x, match_op[...]).astype(BF16)
        below = pl.ds(at_rows.start + BLK, part_rows)
        for m in range(BLK):
            for slot in used:
                stack[1 + slot, below, m * LANES:(m + 1) * LANES] = got[
                    m * part_rows:(m + 1) * part_rows, slot * LANES:(slot + 1) * LANES
                ]

    due = ((0, 2, 0, 1), (1, 2, 1, 3), (0, 1, 0, 2), (2, 2, 0, 2), (2, 1, 0, 3), (4, 2, 0, 3))

    def step(g, carry):
        y = jnp.where(g < 2, low, 1 - low)
        at_rows = pl.ds(pl.multiple_of(y * rows + lax.rem(g, 2) * part_rows, part_rows), part_rows)
        for x in range(2):
            @pl.when(g == 2 + x)
            def _():
                for p in range(pieces):
                    from_y(1, x, p).wait_recv()
                spread(2 + x)

        def relays(side):
            for at, a, slot, group in due:
                if at % 2 == side:
                    @pl.when(g == at // 2)
                    def _():
                        relay(a, slot, group)

        two_stacks(0, at_rows, g)
        reorder(at_rows)
        relays(0)

        @pl.when(place_at >= 2)
        def _():
            two_stacks(2, at_rows, g)
        relays(1)
        return carry

    lax.fori_loop(0, 4, step, 0)

    for c in range(lines):
        blk[c] = jnp.zeros((BLK, LANES), F32)

    def lay(x):
        return jnp.concatenate([x, jnp.zeros((BLK, LANES - BLK), F32)], axis=1)


    def returned(slot, y):
        a = used[slot][0]
        return remote(
            cross.at[slot, pl.ds(y * rows, rows)], cross_in.at[place_at, low], c_send.at[slot, y],
            c_recv.at[place_at, low], dist, at_place(a, y),
        )

    def product(slot):
        a = used[slot][0]
        for k in range(4):
            if slot == 2:
                for x in range(pieces):
                    over_z(slot, k, x, False, a).wait_recv()
            else:
                @pl.when(place_at == 3)
                def _():
                    for x in range(pieces):
                        over_z(slot, k, x, False, a).wait_recv()
        both = nt(stack[1 + slot], moved[slot])
        both = jnp.concatenate([both, jnp.zeros((2 * BLK, LANES - BLK), F32)], axis=1)
        cross[slot] = both.T[:BLK]
        for y in range(2):
            returned(slot, y).start()
        blk[flip(a)] = both[BLK:]

    for slot in (2, 1, 0):
        @pl.when(wanted_here(slot))
        def _():
            product(slot)

    blk[high] = lay(nt(stack[0, :BLK], halves[low]))
    other_rows = pl.ds(pl.multiple_of((1 - low) * rows, rows), rows)
    to_partner = remote(blk.at[:, other_rows], partner_in, p_send.at[0], p_recv.at[0], dist, partner)
    to_partner.start()

    came = {1: (0,), 2: (0, 1, 3), 3: (0, 1)}
    for src, takers in came.items():
        for a in takers:
            @pl.when(place_at == a)
            def _():
                for y in range(2):
                    remote(
                        cross.at[0, pl.ds(0, rows)], cross_in.at[src, y], c_send.at[0, 0], c_recv.at[src, y], dist, me
                    ).wait_recv()
                blk[flip(src), own_rows] = cross_in[src, 0] + cross_in[src, 1]
    to_partner.wait()
    tiles = [(blk[c, own_rows] + partner_in[c])[:, :BLK] for c in range(lines)]
    out_ref[...] = jnp.concatenate(tiles, axis=1)

    for copy in first_hop + second_hop + third_hop:
        copy.wait_send()
    for k in range(2):
        for x in range(pieces):
            over_y(0, k, x).wait_send()
            over_y(1, k, x).wait_send()
    for slot, senders in {0: (0, 1, 2), 1: (1, 2), 2: (3,)}.items():
        for a in senders:
            @pl.when(place_at == a)
            def _():
                for k in range(4):
                    for x in range(pieces):
                        over_z(slot, k, x, False, 0).wait_send()

        @pl.when(wanted_here(slot))
        def _():
            for y in range(2):
                returned(slot, y).wait_send()


def on_line(n, groups, atoms, source, occ, virt, pairs, tensor, green):
    slots, rows, width = tensor.shape
    blocks = green.shape[0] // 2
    lines = n // 2
    deep = BLK * LANES
    part_rows = rows // 2
    vmem = pl.BlockSpec(memory_space=pltpu.VMEM)
    dma = pltpu.SemaphoreType.DMA
    return pl.pallas_call(
        functools.partial(line_kernel, n, groups, atoms),
        out_shape=jax.ShapeDtypeStruct((rows, lines * BLK), F32),
        in_specs=[pl.BlockSpec(memory_space=pltpu.SMEM)] * 4 + [vmem, vmem],
        out_specs=vmem,
        scratch_shapes=[
            pltpu.VMEM((2 * n * blocks, BLK, LANES), BF16),
            pltpu.VMEM((2, BLK, deep), BF16),
            pltpu.VMEM((3, BLK, deep), BF16),
            pltpu.VMEM((4, 2 * BLK, deep), BF16),
            pltpu.VMEM((LANES, 3 * LANES), BF16),
            pltpu.VMEM((2, part_rows * BLK, LANES), F32),
            pltpu.VMEM((2, part_rows * BLK, 2 * LANES), BF16),
            pltpu.VMEM((2, part_rows, slots * BLK, LANES), BF16),
            pltpu.VMEM((2, part_rows * BLK, LANES), F32),
            pltpu.VMEM((4, slots * BLK, slots * BLK), BF16),
            pltpu.VMEM((4, 2 * LANES, slots * LANES), BF16),
            pltpu.VMEM((4, slots * BLK, slots * LANES), BF16),
            pltpu.VMEM((slots * LANES, slots * LANES), BF16),
            pltpu.VMEM((slots * LANES, slots * BLK), BF16),
            pltpu.VMEM((slots, 2 * LANES, LANES), BF16),
            pltpu.VMEM((LANES, slots * LANES), BF16),
            pltpu.VMEM((lines, BLK, LANES), F32),
            pltpu.VMEM((3, BLK, LANES), F32),
            pltpu.VMEM((lines, rows, LANES), F32),
            pltpu.VMEM((lines, 2, rows, LANES), F32),
            dma((4, lines)),
            dma((4, lines)),
            dma((2, 4)),
            dma((2, 4)),
            dma((3, 8)),
            dma((3, 8)),
            dma((3, 2)),
            dma((lines, 2)),
            dma((1,)),
            dma((1,)),
        ],
        compiler_params=pltpu.CompilerParams(
            collective_id=1, has_side_effects=True, vmem_limit_bytes=48 * 2**20
        ),
    )(*[jnp.transpose(x, (1, 2, 0)) for x in (source, occ, virt)], pairs.T, tensor, green)


def solution(mesh):
    n = mesh.shape["ctr"]
    groups = mesh.shape["dist"]

    def shards(three_centre, occupied_green, virtual_green, pair_index, source_slot, occupied_index, virtual_index):
        rows, slots, width = three_centre.shape
        blocks = occupied_green.shape[0]
        atoms = pair_index.shape[0]
        chunks = width // LANES
        cols = width // n
        tensor = jnp.transpose(three_centre, (1, 0, 2))
        green = jnp.concatenate([virtual_green, occupied_green], axis=0).reshape(2 * blocks, BLK, BLK)
        ids = jnp.concatenate(
            [x.reshape(-1) for x in (source_slot, occupied_index, virtual_index, pair_index)]
        )
        vmem = pl.BlockSpec(memory_space=pltpu.VMEM)
        dma = pltpu.SemaphoreType.DMA
        if n == 8 and groups % 2 == 0 and rows * 2 == BLK:
            return on_line(
                n, groups, atoms, source_slot, occupied_index, virtual_index, pair_index, tensor, green
            )
        return pl.pallas_call(
            functools.partial(kernel, n, groups, atoms),
            out_shape=jax.ShapeDtypeStruct((rows, n * rows), F32),
            in_specs=[pl.BlockSpec(memory_space=pltpu.SMEM), vmem, vmem],
            out_specs=vmem,
            scratch_shapes=[
                pltpu.VMEM((2 * n * blocks, BLK, LANES), BF16),
                pltpu.VMEM((rows * chunks, LANES), F32),
                pltpu.VMEM((slots, rows * chunks, LANES), BF16),
                pltpu.VMEM((slots * BLK, rows * LANES), BF16),
                pltpu.VMEM((BLK, slots * BLK), BF16),
                pltpu.VMEM((slots, n, rows, cols), BF16),
                pltpu.VMEM((n, slots, rows, cols), BF16),
                pltpu.VMEM((n, slots, rows, cols), BF16),
                pltpu.VMEM((n * rows, NPR * cols), BF16),
                pltpu.VMEM((n * rows, NPR * cols), BF16),
                pltpu.VMEM((n * rows, n * rows), F32),
                pltpu.VMEM((n * rows, n * rows), BF16),
                pltpu.VMEM((n, rows, n * rows), BF16),
                dma((4, n // 2)),
                dma((4, n // 2)),
                dma((n,)),
                dma((n,)),
                dma((slots, n)),
                dma((slots, n)),
                dma((n,)),
                dma((n,)),
                dma((2,)),
            ],
            compiler_params=pltpu.CompilerParams(
                collective_id=0, has_side_effects=True, vmem_limit_bytes=48 * 2**20
            ),
        )(ids, tensor, green)

    return jax.shard_map(
        shards,
        mesh=mesh,
        in_specs=(
            P(("dist", "ctr"), None, None),
            P(("dist", "ctr"), None),
            P(("dist", "ctr"), None),
            P(),
            P(),
            P(),
            P(),
        ),
        out_specs=P(("dist", "ctr"), None),
        check_vma=False,
    )
```

```python
import functools

import jax
import jax.numpy as jnp
from jax import lax
from jax.experimental import pallas as pl
from jax.experimental.pallas import tpu as pltpu
from jax.sharding import PartitionSpec as P

BLK = 64
NPR = 8
LANES = 128
F32 = jnp.float32
BF16 = jnp.bfloat16


def kernel(n, groups, atoms, ids, t_ref, green_ref, out_ref, table, tf, tt, wcat, ocat, usend, urecv, trecv,
           uk, tk, part, psend, precv, g_send, g_recv, t_send, t_recv, u_send, u_recv, p_send, p_recv, own_sem):
    slots, rows, width = t_ref.shape
    chunks = width // LANES
    blocks = green_ref.shape[0] // 2
    cols = width // n
    per = cols // LANES
    dist = lax.axis_index("dist")
    me = lax.axis_index("ctr")
    before = lax.rem(dist + groups - 1, groups)
    after = lax.rem(dist + 1, groups)

    far_first = sorted(range(1, n), key=lambda k: -min(k, n - k))

    def ahead(k):
        return lax.rem(me + k, n)

    def signal(d, c):
        pl.semaphore_signal(barrier, inc=1, device_id=(d, c), device_id_type=pl.DeviceIdType.MESH)

    def remote(src, dst, send, recv, d, c):
        return pltpu.make_async_remote_copy(
            src_ref=src, dst_ref=dst, send_sem=send, recv_sem=recv, device_id=(d, c),
            device_id_type=pl.DeviceIdType.MESH,
        )

    barrier = pltpu.get_barrier_semaphore()
    for k in range(1, n):
        signal(dist, ahead(k))
    signal(before, me)
    signal(after, me)

    row = lax.broadcasted_iota(jnp.int32, (BLK, BLK), 0)
    col = lax.broadcasted_iota(jnp.int32, (BLK, BLK), 1)
    half = BLK // 2
    wanted = jnp.where(row < half, 2 * row, 2 * (row - half) + 1)
    perm = (wanted == col).astype(BF16)
    mine = me * blocks
    for b in range(blocks):
        occ = green_ref[blocks + b]
        turned = lax.dot_general(perm, occ, (((1,), (1,)), ((), ())), preferred_element_type=F32).astype(BF16)
        turned = lax.dot_general(turned, perm, (((1,), (1,)), ((), ())), preferred_element_type=F32).astype(BF16)
        table[mine + b] = jnp.concatenate([green_ref[b], turned], axis=1)

    pl.semaphore_wait(barrier, n + 1)

    lines = n // 2
    high, low = me // 2, lax.rem(me, 2)
    partner = high * 2 + 1 - low

    def line(k):
        return lax.rem(high + k, lines) * 2

    def at_home(c):
        return table.at[pl.ds(c * blocks, blocks)]

    def across(c):
        return table.at[pl.ds((n + c) * blocks, blocks)]

    first_hop = [
        remote(at_home(me), at_home(me), g_send.at[0, k], g_recv.at[0, k], dist, line(k) + low)
        for k in range(1, lines)
    ]
    for copy in first_hop:
        copy.start()

    def t_part(c):
        return t_ref.at[:, :, pl.ds(pl.multiple_of(c * cols, LANES), cols)]

    tensor = [
        remote(t_part(ahead(k)), trecv.at[me], t_send.at[k], t_recv.at[k], dist, ahead(k)) for k in far_first
    ]
    for copy in tensor:
        copy.start()
    own_t = pltpu.make_async_copy(t_part(me), trecv.at[me], own_sem.at[0])
    own_t.start()

    second_hop, third_hop = [], []
    for k in range(lines):
        if k:
            first_hop[k - 1].wait_recv()
        c = line(lines - k) + low
        second_hop.append(remote(at_home(c), at_home(c), g_send.at[1, k], g_recv.at[1, k], dist, partner))
        second_hop[-1].start()
        third_hop.append(remote(at_home(c), across(c), g_send.at[2, k], g_recv.at[2, k], before, me))
        third_hop[-1].start()

    def turn(s, carry):
        for j in range(chunks):
            tf[j * rows:(j + 1) * rows, :] = t_ref[s, :, j * LANES:(j + 1) * LANES].astype(F32)
        for i in range(rows):
            tt[s, i * chunks:(i + 1) * chunks, :] = tf[pl.ds(i, chunks, stride=rows), :].astype(BF16)
        return carry

    lax.fori_loop(0, slots, turn, 0)

    for k in range(lines):
        second_hop[k].wait_recv()
        c = line(lines - k) + 1 - low
        third_hop.append(remote(at_home(c), across(c), g_send.at[3, k], g_recv.at[3, k], before, me))
        third_hop[-1].start()
    for copy in third_hop:
        copy.wait()
    for copy in first_hop + second_hop:
        copy.wait_send()

    size = atoms * slots
    atom = (dist * n + me) * rows // BLK
    total = n * blocks * groups
    base = dist * n * blocks

    def position(value):
        shift = value - base
        return jnp.minimum(jnp.where(shift < 0, shift + total, shift), 2 * n * blocks - 1)

    step_rows = 8 * chunks
    lane = lax.broadcasted_iota(jnp.int32, (half, LANES), 1)

    def update(s, carry):
        at = (atom * slots + s) * slots
        for r in range(slots):
            src = ids[at + r]
            live = jnp.where(src >= 0, 1.0, 0.0).astype(F32)
            src = jnp.maximum(src, 0)
            virt = table[position(ids[2 * size * slots + at + r])].astype(F32)[:, :BLK] * live
            zero = jnp.zeros((BLK, LANES), F32)
            twice = jnp.concatenate([virt, virt], axis=1)
            weight = jnp.concatenate(
                [jnp.concatenate([twice, zero], axis=1), jnp.concatenate([zero, twice], axis=1)], axis=0
            ).astype(BF16)
            ocat[:, r * BLK:(r + 1) * BLK] = table[position(ids[size * slots + at + r])][:, BLK:]
            for h in range(rows // 8):
                got = jnp.dot(
                    tt[src, h * step_rows:(h + 1) * step_rows, :], weight, preferred_element_type=F32
                ).astype(BF16)
                for x in range(8):
                    i = h * 8 + x
                    for e in range(2):
                        wcat[r * BLK + e * half:r * BLK + (e + 1) * half, i * LANES:(i + 1) * LANES] = got[
                            x * chunks:(x + 1) * chunks, e * LANES:(e + 1) * LANES
                        ]
        occ = ocat[...]
        for h in range(rows // 4):
            both = jnp.dot(occ, wcat[:, h * 4 * LANES:(h + 1) * 4 * LANES], preferred_element_type=F32)
            for x in range(4):
                i = h * 4 + x
                piece = both[:, x * LANES:(x + 1) * LANES]
                tf[i * chunks:(i + 1) * chunks, :] = jnp.where(lane < BLK, piece[:half], piece[half:])
        for q in range(chunks):
            usend[s, q // per, :, (q % per) * LANES:(q % per + 1) * LANES] = tf[
                pl.ds(q, rows, stride=chunks), :
            ].astype(BF16)
        for k in far_first:
            sent(s, k).start()
        return carry

    def sent(s, k):
        return remote(
            usend.at[s, ahead(k)], urecv.at[me, s], u_send.at[s, k], u_recv.at[s, k], dist, ahead(k)
        )

    lax.fori_loop(0, slots, update, 0)
    own_u = pltpu.make_async_copy(usend.at[:, me], urecv.at[me], own_sem.at[1])
    own_u.start()
    own_t.wait()
    for copy in tensor:
        copy.wait()

    first = dist * (n * rows // BLK)
    pairs = 3 * size * slots

    def pick(src, pair, p):
        where = pairs + (first + p * rows // BLK) * slots
        slot = jnp.int32(0)
        live = jnp.int32(0)
        for s in range(slots):
            hit = ids[where + s] == pair
            slot = jnp.where(hit, s, slot)
            live = jnp.where(hit, 1, live)
        return (src[p, slot].astype(F32) * live.astype(F32)).astype(BF16)

    def at_rows(p):
        return pl.ds(pl.multiple_of(p * rows, rows), rows)

    def at_cols(pair):
        return pl.ds(pl.multiple_of(pair * cols, LANES), cols)

    def tensor_pair(pair, carry):
        def gather(p, inner):
            tk[at_rows(p), at_cols(pair)] = pick(trecv, pair, p)
            return inner

        return lax.fori_loop(0, n, gather, carry)

    lax.fori_loop(0, NPR, tensor_pair, 0)

    def updated_pairs(p):
        where = pairs + (first + p * rows // BLK) * slots

        def one_pair(pair, carry):
            chosen = jnp.zeros((rows, cols), F32)
            for s in range(slots):
                hit = jnp.where(ids[where + s] == pair, 1.0, 0.0).astype(F32)
                chosen = chosen + urecv[p, s].astype(F32) * hit
            uk[at_rows(p), at_cols(pair)] = chosen.astype(BF16)
            return carry

        lax.fori_loop(0, NPR, one_pair, 0)

    own_u.wait()
    updated_pairs(me)
    for k in far_first[::-1]:
        for s in range(slots):
            sent(s, k).wait()
        updated_pairs(lax.rem(me - k + n, n))

    def block(p, carry):
        at = pl.ds(pl.multiple_of(p * 256, 256), 256)
        total = lax.dot_general(uk[at, :], tk[...], (((1,), (1,)), ((), ())), preferred_element_type=F32)
        part[at, :] = total
        psend[at, :] = total.astype(BF16)
        return carry

    lax.fori_loop(0, n * rows // 256, block, 0)

    def p_part(c):
        return psend.at[pl.ds(pl.multiple_of(c * rows, rows), rows)]

    shares = [
        remote(p_part(ahead(k)), precv.at[k], p_send.at[k], p_recv.at[k], dist, ahead(k)) for k in far_first
    ]
    for copy in shares:
        copy.start()
    result = part[pl.ds(pl.multiple_of(me * rows, rows), rows), :]
    for k, copy in zip(far_first, shares):
        copy.wait()
        result = result + precv[k].astype(F32)
    out_ref[...] = result


def iota(shape, dim):
    return lax.broadcasted_iota(jnp.int32, shape, dim)


def nt(a, b):
    return lax.dot_general(a, b, (((1,), (1,)), ((), ())), preferred_element_type=F32)


def nn(a, b):
    return jnp.dot(a, b, preferred_element_type=F32)


def line_kernel(n, groups, atoms, source_ids, occ_ids, virt_ids, pair_ids, t_ref, green_ref, out_ref, table, halves, moved, stack, match_op, tf, xg, wg, uf,
                first_op, second_op, gather, select, place, lift, turn_v, blk, cross, partner_in, cross_in,
                g_send, g_recv, y_send, y_recv, m_send, m_recv, c_send, c_recv, p_send, p_recv):
    slots, rows, width = t_ref.shape
    blocks = green_ref.shape[0] // 2
    chunks = width // LANES
    half = BLK // 2
    part_rows = rows // 2
    deep = BLK * LANES
    dist = lax.axis_index("dist")
    me = lax.axis_index("ctr")
    before = lax.rem(dist + groups - 1, groups)
    after = lax.rem(dist + 1, groups)
    lines = n // 2
    high, low = me // 2, lax.rem(me, 2)
    partner = high * 2 + 1 - low
    mirrored = lax.rem(dist, 2)

    def flip(a):
        return jnp.where(mirrored == 1, lines - 1 - a, a)

    place_at = flip(high)

    def at_place(a, y):
        return flip(a) * 2 + y

    def signal(d, c):
        pl.semaphore_signal(barrier, inc=1, device_id=(d, c), device_id_type=pl.DeviceIdType.MESH)

    def remote(src, dst, send, recv, d, c):
        return pltpu.make_async_remote_copy(
            src_ref=src, dst_ref=dst, send_sem=send, recv_sem=recv, device_id=(d, c),
            device_id_type=pl.DeviceIdType.MESH,
        )

    barrier = pltpu.get_barrier_semaphore()
    for k in range(1, n):
        signal(dist, lax.rem(me + k, n))
    signal(before, me)
    signal(after, me)

    row, col = iota((BLK, BLK), 0), iota((BLK, BLK), 1)
    wanted = jnp.where(row < half, 2 * row, 2 * (row - half) + 1)
    perm = (wanted == col).astype(BF16)
    mine = me * blocks
    for b in range(blocks):
        turned = nn(perm, green_ref[blocks + b]).astype(BF16)
        turned = nt(turned, perm).astype(BF16)
        table[mine + b] = jnp.concatenate([green_ref[b], turned], axis=1)

    pl.semaphore_wait(barrier, n + 1)

    def line(k):
        return lax.rem(high + k, lines) * 2

    def at_home(c):
        return table.at[pl.ds(c * blocks, blocks)]

    def across(c):
        return table.at[pl.ds((n + c) * blocks, blocks)]

    first_hop = [
        remote(at_home(me), at_home(me), g_send.at[0, k], g_recv.at[0, k], dist, line(k) + low)
        for k in range(1, lines)
    ]
    for copy in first_hop:
        copy.start()
    second_hop, third_hop = [], []

    def onward(k):
        c = line(lines - k) + low
        second_hop.append(remote(at_home(c), at_home(c), g_send.at[1, k], g_recv.at[1, k], dist, partner))
        second_hop[-1].start()
        third_hop.append(remote(at_home(c), across(c), g_send.at[2, k], g_recv.at[2, k], before, me))
        third_hop[-1].start()

    onward(0)

    wide = slots * LANES
    r_, c_ = iota((wide, wide), 0), iota((wide, wide), 1)
    select[...] = (
        r_ == ((c_ // half) % slots) * LANES + ((c_ // LANES) % 2) * BLK + (c_ // (2 * LANES)) * half + c_ % half
    ).astype(BF16)
    own_rows = pl.ds(pl.multiple_of(low * rows, rows), rows)
    per = 8
    for q in range(0, chunks, per):
        x = jnp.concatenate(
            [
                jnp.concatenate([t_ref[j, :, (q + p) * LANES:(q + p + 1) * LANES] for j in range(slots)], axis=1)
                for p in range(per)
            ],
            axis=0,
        )
        got = nn(x, select[...]).astype(BF16)
        for p in range(per):
            for h in range(2):
                for e in range(2):
                    at = (e * half + q + p) * LANES
                    halves[h, own_rows, at:at + LANES] = got[
                        p * rows:(p + 1) * rows, (h * 2 + e) * LANES:(h * 2 + e + 1) * LANES
                    ]

    def rows_of(k):
        y = low if k < 2 else 1 - low
        return pl.ds(pl.multiple_of(y * rows + (k % 2) * part_rows, part_rows), part_rows)

    pieces = 2
    piece = deep // pieces

    def over_y(phase, k, x):
        h = 1 - low if phase == 0 else low
        at = halves.at[h, rows_of(k), pl.ds(x * piece, piece)]
        sem = k * pieces + x
        return remote(at, at, y_send.at[phase, sem], y_recv.at[phase, sem], dist, partner)

    def from_y(phase, k, x):
        at = halves.at[low if phase == 0 else 1 - low, rows_of(2 + k), pl.ds(x * piece, piece)]
        sem = k * pieces + x
        return remote(at, at, y_send.at[phase, sem], y_recv.at[phase, sem], dist, partner)

    def over_z(slot, k, x, own, to):
        at, lanes = rows_of(k), pl.ds(x * piece, piece)
        src = halves.at[low, at, lanes] if own else moved.at[slot, at, lanes]
        sem = k * pieces + x
        return remote(
            src, moved.at[slot, at, lanes], m_send.at[slot, sem], m_recv.at[slot, sem], dist, at_place(to, low)
        )

    def spread(g):
        at_rows = rows_of(g)
        for h in range(2):
            for m in range(BLK):
                tf[h, m * part_rows:(m + 1) * part_rows, :] = halves[h, at_rows, m * LANES:(m + 1) * LANES].astype(F32)
            for i in range(part_rows):
                xg[g % 2, i * BLK:(i + 1) * BLK, h * LANES:(h + 1) * LANES] = tf[
                    h, pl.ds(i, BLK, stride=part_rows), :
                ].astype(BF16)

    starts = {0: (0, 1), 1: (1, 2), 3: (2, 2)}

    def send_own(k, places):
        for a in places:
            slot, to = starts[a]

            @pl.when(place_at == a)
            def _():
                for x in range(pieces):
                    over_z(slot, k, x, True, to).start()

    over_y(0, 0, 0).start()
    over_y(0, 0, 1).start()
    for k in range(2):
        send_own(k, (0, 1))
    for k in range(1, lines):
        first_hop[k - 1].wait_recv()
        onward(k)
    for phase, k in ((0, 1), (1, 0), (1, 1)):
        for x in range(pieces):
            over_y(phase, k, x).start()

    def relay(a, slot, k):
        @pl.when(place_at == a)
        def _():
            for x in range(pieces):
                over_z(slot, k, x, False, a).wait_recv()
                over_z(slot, k, x, False, a + 1).start()

    r_, c_ = iota((wide, slots * BLK), 0), iota((wide, slots * BLK), 1)
    place[...] = ((r_ % LANES >= BLK) & (c_ == (r_ // LANES) * BLK + r_ % LANES - BLK)).astype(BF16)
    r_, c_ = iota((2 * LANES, LANES), 0), iota((2 * LANES, LANES), 1)
    for t in range(slots):
        lift[t] = ((c_ < BLK) & (r_ == (c_ // half) * LANES + t * half + c_ % half)).astype(BF16)
    r_, c_ = iota((LANES, wide), 0), iota((LANES, wide), 1)
    turn_v[...] = ((r_ // half == c_ // LANES) & (c_ % LANES == low * half + r_ % half)).astype(BF16)

    def third(k):
        second_hop[k].wait_recv()
        c = line(lines - k) + 1 - low
        third_hop.append(remote(at_home(c), across(c), g_send.at[3, k], g_recv.at[3, k], before, me))
        third_hop[-1].start()

    third(0)
    for x in range(pieces):
        from_y(0, 0, x).wait_recv()
    send_own(2, (0, 1))
    for k in range(1, lines):
        third(k)
    relay(1, 0, 0)
    relay(2, 1, 0)
    relay(2, 1, 1)
    relay(1, 0, 1)
    total = n * blocks * groups
    base = dist * n * blocks
    atom = dist * lines + high

    def position(value):
        shift = value - base
        return jnp.minimum(jnp.where(shift < 0, shift + total, shift), 2 * n * blocks - 1)

    def atom_at(a):
        return dist * lines + flip(a)

    def feeding(a, s, j):
        r, live = jnp.int32(0), jnp.int32(0)
        for x in range(slots):
            hit = source_ids[s, x, a] == j
            r, live = jnp.where(hit, x, r), jnp.where(hit, 1, live)
        return r, live

    def green(a, s, r, live):
        return position(occ_ids[s, r, a]), position(virt_ids[s, r, a]), live.astype(F32)

    used = {0: (0, (1, 2, 3)), 1: (1, (2, 3)), 2: (3, (2,))}

    def wanted_here(slot):
        hit = place_at == used[slot][1][0]
        for a in used[slot][1][1:]:
            hit = hit | (place_at == a)
        return hit

    def adjoint_entries(a):
        other = atom_at(a)
        entries = []
        for t in range(slots):
            pair = pair_ids[t, atom]
            s, met = jnp.int32(0), jnp.int32(0)
            for x in range(slots):
                hit = pair_ids[x, other] == pair
                s, met = jnp.where(hit, x, s), jnp.where(hit, 1, met)
            row = []
            for o in range(slots):
                r, live = feeding(other, s, o)
                row.append(green(other, s, r, live * met))
            entries.append(row)
        return entries

    own_entries = [[green(atom, o, *feeding(atom, o, t)) for o in range(slots)] for t in range(slots)]
    entries = {slot: adjoint_entries(used[slot][0]) for slot in used}

    r_, c_ = iota((LANES, LANES), 0), iota((LANES, LANES), 1)
    for slot in used:
        other = atom_at(used[slot][0])
        match = jnp.zeros((LANES, LANES), F32)
        for s in range(slots):
            for t in range(slots):
                hit = jnp.where(pair_ids[s, atom] == pair_ids[t, other], 1.0, 0.0)
                match = jnp.where((r_ // half == s) & (c_ // half == t), hit.astype(F32), match)
        match_op[:, slot * LANES:(slot + 1) * LANES] = jnp.where(r_ % half == c_ % half, match, 0.0).astype(BF16)

    spread(0)
    spread(1)
    relay(2, 1, 2)
    relay(2, 0, 0)
    for copy in third_hop:
        copy.wait_recv()
    for k in range(3):
        send_own(k, (3,))

    for t in range(slots):
        virt = []
        for o in range(slots):
            occ_pos, virt_pos, live = own_entries[t][o]
            virt.append((table[virt_pos].astype(F32) * live).astype(BF16))
            gather[3, t * BLK:(t + 1) * BLK, o * LANES:(o + 1) * LANES] = table[occ_pos]
        b = nt(turn_v[...], jnp.concatenate(virt, axis=1)).astype(BF16)
        second_op[0, :, t * LANES:(t + 1) * LANES] = nt(lift[t][:, :BLK], b).astype(BF16)
    size_op = slots * BLK
    unit = (iota((size_op, size_op), 0) == iota((size_op, size_op), 1)).astype(BF16)
    first_op[0] = nt(unit, nn(gather[3], place[...]).astype(BF16)).astype(BF16)

    for x in range(pieces):
        from_y(0, 1, x).wait_recv()
    send_own(3, (0, 1, 3))

    def operators(slot):
        for t in range(slots):
            virt = []
            for o in range(slots):
                occ_pos, virt_pos, live = entries[slot][t][o]
                virt.append(
                    (table[virt_pos, pl.ds(pl.multiple_of(low * half, half), half), :].astype(F32) * live).astype(BF16)
                )
                gather[slot, o * BLK:(o + 1) * BLK, t * LANES:(t + 1) * LANES] = table[occ_pos]
            second_op[1 + slot, :, t * LANES:(t + 1) * LANES] = nt(lift[t], jnp.concatenate(virt, axis=0)).astype(BF16)
        first_op[1 + slot] = nn(gather[slot], place[...]).astype(BF16)

    for slot in used:
        operators(slot)

    lanes2 = (iota((BLK, 2 * LANES), 1) // half) % slots

    def first(k, u, g):
        got = nn(xg[lax.rem(g, 2)], second_op[k]).astype(BF16)
        for i in range(part_rows):
            for t in range(slots):
                wg[u, i, t * BLK:(t + 1) * BLK, :] = got[i * BLK:(i + 1) * BLK, t * LANES:(t + 1) * LANES]

    def second(k, u):
        for p in range(part_rows // 2):
            both = nn(first_op[k], jnp.concatenate([wg[u, 2 * p], wg[u, 2 * p + 1]], axis=1))
            res = both[:BLK]
            for o in range(1, slots):
                res = jnp.where(lanes2 == o, both[o * BLK:(o + 1) * BLK], res)
            for x in range(2):
                uf[u, (2 * p + x) * BLK:(2 * p + x + 1) * BLK, :] = res[:, x * LANES:(x + 1) * LANES]

    def keep(k, u, at_rows):
        for m in range(BLK):
            stack[k, at_rows, m * LANES:(m + 1) * LANES] = uf[u, pl.ds(m, part_rows, stride=BLK), :].astype(BF16)

    def two_stacks(k, at_rows, g):
        for u in range(2):
            first(k + u, u, g)
        for u in range(2):
            second(k + u, u)
        for u in range(2):
            keep(k + u, u, at_rows)

    def reorder(at_rows):
        x = jnp.concatenate([stack[0, at_rows, m * LANES:(m + 1) * LANES] for m in range(BLK)], axis=0)
        got = nn(x, match_op[...]).astype(BF16)
        below = pl.ds(at_rows.start + BLK, part_rows)
        for m in range(BLK):
            for slot in used:
                stack[1 + slot, below, m * LANES:(m + 1) * LANES] = got[
                    m * part_rows:(m + 1) * part_rows, slot * LANES:(slot + 1) * LANES
                ]

    due = ((0, 2, 0, 1), (1, 2, 1, 3), (0, 1, 0, 2), (2, 2, 0, 2), (2, 1, 0, 3), (4, 2, 0, 3))

    def step(g, carry):
        y = jnp.where(g < 2, low, 1 - low)
        at_rows = pl.ds(pl.multiple_of(y * rows + lax.rem(g, 2) * part_rows, part_rows), part_rows)
        for x in range(2):
            @pl.when(g == 2 + x)
            def _():
                for p in range(pieces):
                    from_y(1, x, p).wait_recv()
                spread(2 + x)

        def relays(side):
            for at, a, slot, group in due:
                if at % 2 == side:
                    @pl.when(g == at // 2)
                    def _():
                        relay(a, slot, group)

        two_stacks(0, at_rows, g)
        relays(0)

        @pl.when(place_at >= 2)
        def _():
            reorder(at_rows)
            two_stacks(2, at_rows, g)

        @pl.when(place_at == 1)
        def _():
            reorder(at_rows)
        relays(1)
        return carry

    lax.fori_loop(0, 4, step, 0)

    for c in range(lines):
        blk[c] = jnp.zeros((BLK, LANES), F32)

    def lay(x):
        return jnp.concatenate([x, jnp.zeros((BLK, LANES - BLK), F32)], axis=1)


    def returned(slot, y):
        a = used[slot][0]
        return remote(
            cross.at[slot, pl.ds(y * rows, rows)], cross_in.at[place_at, low], c_send.at[slot, y],
            c_recv.at[place_at, low], dist, at_place(a, y),
        )

    def product(slot):
        a = used[slot][0]
        for k in range(4):
            if slot == 2:
                for x in range(pieces):
                    over_z(slot, k, x, False, a).wait_recv()
            else:
                @pl.when(place_at == 3)
                def _():
                    for x in range(pieces):
                        over_z(slot, k, x, False, a).wait_recv()
        both = nt(stack[1 + slot], moved[slot])
        both = jnp.concatenate([both, jnp.zeros((2 * BLK, LANES - BLK), F32)], axis=1)
        cross[slot] = both.T[:BLK]
        for y in range(2):
            returned(slot, y).start()
        blk[flip(a)] = both[BLK:]

    for slot in (2, 1, 0):
        @pl.when(wanted_here(slot))
        def _():
            product(slot)

    blk[high] = lay(nt(stack[0, :BLK], halves[low]))
    other_rows = pl.ds(pl.multiple_of((1 - low) * rows, rows), rows)
    to_partner = remote(blk.at[:, other_rows], partner_in, p_send.at[0], p_recv.at[0], dist, partner)
    to_partner.start()

    came = {1: (0,), 2: (0, 1, 3), 3: (0, 1)}
    for src, takers in came.items():
        for a in takers:
            @pl.when(place_at == a)
            def _():
                for y in range(2):
                    remote(
                        cross.at[0, pl.ds(0, rows)], cross_in.at[src, y], c_send.at[0, 0], c_recv.at[src, y], dist, me
                    ).wait_recv()
                blk[flip(src), own_rows] = cross_in[src, 0] + cross_in[src, 1]
    to_partner.wait()
    tiles = [(blk[c, own_rows] + partner_in[c])[:, :BLK] for c in range(lines)]
    out_ref[...] = jnp.concatenate(tiles, axis=1)

    for copy in first_hop + second_hop + third_hop:
        copy.wait_send()
    for k in range(2):
        for x in range(pieces):
            over_y(0, k, x).wait_send()
            over_y(1, k, x).wait_send()
    for slot, senders in {0: (0, 1, 2), 1: (1, 2), 2: (3,)}.items():
        for a in senders:
            @pl.when(place_at == a)
            def _():
                for k in range(4):
                    for x in range(pieces):
                        over_z(slot, k, x, False, 0).wait_send()

        @pl.when(wanted_here(slot))
        def _():
            for y in range(2):
                returned(slot, y).wait_send()


def on_line(n, groups, atoms, source, occ, virt, pairs, tensor, green):
    slots, rows, width = tensor.shape
    blocks = green.shape[0] // 2
    lines = n // 2
    deep = BLK * LANES
    part_rows = rows // 2
    vmem = pl.BlockSpec(memory_space=pltpu.VMEM)
    dma = pltpu.SemaphoreType.DMA
    return pl.pallas_call(
        functools.partial(line_kernel, n, groups, atoms),
        out_shape=jax.ShapeDtypeStruct((rows, lines * BLK), F32),
        in_specs=[pl.BlockSpec(memory_space=pltpu.SMEM)] * 4 + [vmem, vmem],
        out_specs=vmem,
        scratch_shapes=[
            pltpu.VMEM((2 * n * blocks, BLK, LANES), BF16),
            pltpu.VMEM((2, BLK, deep), BF16),
            pltpu.VMEM((3, BLK, deep), BF16),
            pltpu.VMEM((4, 2 * BLK, deep), BF16),
            pltpu.VMEM((LANES, 3 * LANES), BF16),
            pltpu.VMEM((2, part_rows * BLK, LANES), F32),
            pltpu.VMEM((2, part_rows * BLK, 2 * LANES), BF16),
            pltpu.VMEM((2, part_rows, slots * BLK, LANES), BF16),
            pltpu.VMEM((2, part_rows * BLK, LANES), F32),
            pltpu.VMEM((4, slots * BLK, slots * BLK), BF16),
            pltpu.VMEM((4, 2 * LANES, slots * LANES), BF16),
            pltpu.VMEM((4, slots * BLK, slots * LANES), BF16),
            pltpu.VMEM((slots * LANES, slots * LANES), BF16),
            pltpu.VMEM((slots * LANES, slots * BLK), BF16),
            pltpu.VMEM((slots, 2 * LANES, LANES), BF16),
            pltpu.VMEM((LANES, slots * LANES), BF16),
            pltpu.VMEM((lines, BLK, LANES), F32),
            pltpu.VMEM((3, BLK, LANES), F32),
            pltpu.VMEM((lines, rows, LANES), F32),
            pltpu.VMEM((lines, 2, rows, LANES), F32),
            dma((4, lines)),
            dma((4, lines)),
            dma((2, 4)),
            dma((2, 4)),
            dma((3, 8)),
            dma((3, 8)),
            dma((3, 2)),
            dma((lines, 2)),
            dma((1,)),
            dma((1,)),
        ],
        compiler_params=pltpu.CompilerParams(
            collective_id=1, has_side_effects=True, vmem_limit_bytes=48 * 2**20
        ),
    )(*[jnp.transpose(x, (1, 2, 0)) for x in (source, occ, virt)], pairs.T, tensor, green)


def solution(mesh):
    n = mesh.shape["ctr"]
    groups = mesh.shape["dist"]

    def shards(three_centre, occupied_green, virtual_green, pair_index, source_slot, occupied_index, virtual_index):
        rows, slots, width = three_centre.shape
        blocks = occupied_green.shape[0]
        atoms = pair_index.shape[0]
        chunks = width // LANES
        cols = width // n
        tensor = jnp.transpose(three_centre, (1, 0, 2))
        green = jnp.concatenate([virtual_green, occupied_green], axis=0).reshape(2 * blocks, BLK, BLK)
        ids = jnp.concatenate(
            [x.reshape(-1) for x in (source_slot, occupied_index, virtual_index, pair_index)]
        )
        vmem = pl.BlockSpec(memory_space=pltpu.VMEM)
        dma = pltpu.SemaphoreType.DMA
        if n == 8 and groups % 2 == 0 and rows * 2 == BLK:
            return on_line(
                n, groups, atoms, source_slot, occupied_index, virtual_index, pair_index, tensor, green
            )
        return pl.pallas_call(
            functools.partial(kernel, n, groups, atoms),
            out_shape=jax.ShapeDtypeStruct((rows, n * rows), F32),
            in_specs=[pl.BlockSpec(memory_space=pltpu.SMEM), vmem, vmem],
            out_specs=vmem,
            scratch_shapes=[
                pltpu.VMEM((2 * n * blocks, BLK, LANES), BF16),
                pltpu.VMEM((rows * chunks, LANES), F32),
                pltpu.VMEM((slots, rows * chunks, LANES), BF16),
                pltpu.VMEM((slots * BLK, rows * LANES), BF16),
                pltpu.VMEM((BLK, slots * BLK), BF16),
                pltpu.VMEM((slots, n, rows, cols), BF16),
                pltpu.VMEM((n, slots, rows, cols), BF16),
                pltpu.VMEM((n, slots, rows, cols), BF16),
                pltpu.VMEM((n * rows, NPR * cols), BF16),
                pltpu.VMEM((n * rows, NPR * cols), BF16),
                pltpu.VMEM((n * rows, n * rows), F32),
                pltpu.VMEM((n * rows, n * rows), BF16),
                pltpu.VMEM((n, rows, n * rows), BF16),
                dma((4, n // 2)),
                dma((4, n // 2)),
                dma((n,)),
                dma((n,)),
                dma((slots, n)),
                dma((slots, n)),
                dma((n,)),
                dma((n,)),
                dma((2,)),
            ],
            compiler_params=pltpu.CompilerParams(
                collective_id=0, has_side_effects=True, vmem_limit_bytes=48 * 2**20
            ),
        )(ids, tensor, green)

    return jax.shard_map(
        shards,
        mesh=mesh,
        in_specs=(
            P(("dist", "ctr"), None, None),
            P(("dist", "ctr"), None),
            P(("dist", "ctr"), None),
            P(),
            P(),
            P(),
            P(),
        ),
        out_specs=P(("dist", "ctr"), None),
        check_vma=False,
    )
```

```python
import functools

import jax
import jax.numpy as jnp
from jax import lax
from jax.experimental import pallas as pl
from jax.experimental.pallas import tpu as pltpu
from jax.sharding import PartitionSpec as P

BLK = 64
NPR = 8
LANES = 128
F32 = jnp.float32
BF16 = jnp.bfloat16


def kernel(n, groups, atoms, ids, t_ref, green_ref, out_ref, table, tf, tt, wcat, ocat, usend, urecv, trecv,
           uk, tk, part, psend, precv, g_send, g_recv, t_send, t_recv, u_send, u_recv, p_send, p_recv, own_sem):
    slots, rows, width = t_ref.shape
    chunks = width // LANES
    blocks = green_ref.shape[0] // 2
    cols = width // n
    per = cols // LANES
    dist = lax.axis_index("dist")
    me = lax.axis_index("ctr")
    before = lax.rem(dist + groups - 1, groups)
    after = lax.rem(dist + 1, groups)

    far_first = sorted(range(1, n), key=lambda k: -min(k, n - k))

    def ahead(k):
        return lax.rem(me + k, n)

    def signal(d, c):
        pl.semaphore_signal(barrier, inc=1, device_id=(d, c), device_id_type=pl.DeviceIdType.MESH)

    def remote(src, dst, send, recv, d, c):
        return pltpu.make_async_remote_copy(
            src_ref=src, dst_ref=dst, send_sem=send, recv_sem=recv, device_id=(d, c),
            device_id_type=pl.DeviceIdType.MESH,
        )

    barrier = pltpu.get_barrier_semaphore()
    for k in range(1, n):
        signal(dist, ahead(k))
    signal(before, me)
    signal(after, me)

    row = lax.broadcasted_iota(jnp.int32, (BLK, BLK), 0)
    col = lax.broadcasted_iota(jnp.int32, (BLK, BLK), 1)
    half = BLK // 2
    wanted = jnp.where(row < half, 2 * row, 2 * (row - half) + 1)
    perm = (wanted == col).astype(BF16)
    mine = me * blocks
    for b in range(blocks):
        occ = green_ref[blocks + b]
        turned = lax.dot_general(perm, occ, (((1,), (1,)), ((), ())), preferred_element_type=F32).astype(BF16)
        turned = lax.dot_general(turned, perm, (((1,), (1,)), ((), ())), preferred_element_type=F32).astype(BF16)
        table[mine + b] = jnp.concatenate([green_ref[b], turned], axis=1)

    pl.semaphore_wait(barrier, n + 1)

    lines = n // 2
    high, low = me // 2, lax.rem(me, 2)
    partner = high * 2 + 1 - low

    def line(k):
        return lax.rem(high + k, lines) * 2

    def at_home(c):
        return table.at[pl.ds(c * blocks, blocks)]

    def across(c):
        return table.at[pl.ds((n + c) * blocks, blocks)]

    first_hop = [
        remote(at_home(me), at_home(me), g_send.at[0, k], g_recv.at[0, k], dist, line(k) + low)
        for k in range(1, lines)
    ]
    for copy in first_hop:
        copy.start()

    def t_part(c):
        return t_ref.at[:, :, pl.ds(pl.multiple_of(c * cols, LANES), cols)]

    tensor = [
        remote(t_part(ahead(k)), trecv.at[me], t_send.at[k], t_recv.at[k], dist, ahead(k)) for k in far_first
    ]
    for copy in tensor:
        copy.start()
    own_t = pltpu.make_async_copy(t_part(me), trecv.at[me], own_sem.at[0])
    own_t.start()

    second_hop, third_hop = [], []
    for k in range(lines):
        if k:
            first_hop[k - 1].wait_recv()
        c = line(lines - k) + low
        second_hop.append(remote(at_home(c), at_home(c), g_send.at[1, k], g_recv.at[1, k], dist, partner))
        second_hop[-1].start()
        third_hop.append(remote(at_home(c), across(c), g_send.at[2, k], g_recv.at[2, k], before, me))
        third_hop[-1].start()

    def turn(s, carry):
        for j in range(chunks):
            tf[j * rows:(j + 1) * rows, :] = t_ref[s, :, j * LANES:(j + 1) * LANES].astype(F32)
        for i in range(rows):
            tt[s, i * chunks:(i + 1) * chunks, :] = tf[pl.ds(i, chunks, stride=rows), :].astype(BF16)
        return carry

    lax.fori_loop(0, slots, turn, 0)

    for k in range(lines):
        second_hop[k].wait_recv()
        c = line(lines - k) + 1 - low
        third_hop.append(remote(at_home(c), across(c), g_send.at[3, k], g_recv.at[3, k], before, me))
        third_hop[-1].start()
    for copy in third_hop:
        copy.wait()
    for copy in first_hop + second_hop:
        copy.wait_send()

    size = atoms * slots
    atom = (dist * n + me) * rows // BLK
    total = n * blocks * groups
    base = dist * n * blocks

    def position(value):
        shift = value - base
        return jnp.minimum(jnp.where(shift < 0, shift + total, shift), 2 * n * blocks - 1)

    step_rows = 8 * chunks
    lane = lax.broadcasted_iota(jnp.int32, (half, LANES), 1)

    def update(s, carry):
        at = (atom * slots + s) * slots
        for r in range(slots):
            src = ids[at + r]
            live = jnp.where(src >= 0, 1.0, 0.0).astype(F32)
            src = jnp.maximum(src, 0)
            virt = table[position(ids[2 * size * slots + at + r])].astype(F32)[:, :BLK] * live
            zero = jnp.zeros((BLK, LANES), F32)
            twice = jnp.concatenate([virt, virt], axis=1)
            weight = jnp.concatenate(
                [jnp.concatenate([twice, zero], axis=1), jnp.concatenate([zero, twice], axis=1)], axis=0
            ).astype(BF16)
            ocat[:, r * BLK:(r + 1) * BLK] = table[position(ids[size * slots + at + r])][:, BLK:]
            for h in range(rows // 8):
                got = jnp.dot(
                    tt[src, h * step_rows:(h + 1) * step_rows, :], weight, preferred_element_type=F32
                ).astype(BF16)
                for x in range(8):
                    i = h * 8 + x
                    for e in range(2):
                        wcat[r * BLK + e * half:r * BLK + (e + 1) * half, i * LANES:(i + 1) * LANES] = got[
                            x * chunks:(x + 1) * chunks, e * LANES:(e + 1) * LANES
                        ]
        occ = ocat[...]
        for h in range(rows // 4):
            both = jnp.dot(occ, wcat[:, h * 4 * LANES:(h + 1) * 4 * LANES], preferred_element_type=F32)
            for x in range(4):
                i = h * 4 + x
                piece = both[:, x * LANES:(x + 1) * LANES]
                tf[i * chunks:(i + 1) * chunks, :] = jnp.where(lane < BLK, piece[:half], piece[half:])
        for q in range(chunks):
            usend[s, q // per, :, (q % per) * LANES:(q % per + 1) * LANES] = tf[
                pl.ds(q, rows, stride=chunks), :
            ].astype(BF16)
        for k in far_first:
            sent(s, k).start()
        return carry

    def sent(s, k):
        return remote(
            usend.at[s, ahead(k)], urecv.at[me, s], u_send.at[s, k], u_recv.at[s, k], dist, ahead(k)
        )

    lax.fori_loop(0, slots, update, 0)
    own_u = pltpu.make_async_copy(usend.at[:, me], urecv.at[me], own_sem.at[1])
    own_u.start()
    own_t.wait()
    for copy in tensor:
        copy.wait()

    first = dist * (n * rows // BLK)
    pairs = 3 * size * slots

    def pick(src, pair, p):
        where = pairs + (first + p * rows // BLK) * slots
        slot = jnp.int32(0)
        live = jnp.int32(0)
        for s in range(slots):
            hit = ids[where + s] == pair
            slot = jnp.where(hit, s, slot)
            live = jnp.where(hit, 1, live)
        return (src[p, slot].astype(F32) * live.astype(F32)).astype(BF16)

    def at_rows(p):
        return pl.ds(pl.multiple_of(p * rows, rows), rows)

    def at_cols(pair):
        return pl.ds(pl.multiple_of(pair * cols, LANES), cols)

    def tensor_pair(pair, carry):
        def gather(p, inner):
            tk[at_rows(p), at_cols(pair)] = pick(trecv, pair, p)
            return inner

        return lax.fori_loop(0, n, gather, carry)

    lax.fori_loop(0, NPR, tensor_pair, 0)

    def updated_pairs(p):
        where = pairs + (first + p * rows // BLK) * slots

        def one_pair(pair, carry):
            chosen = jnp.zeros((rows, cols), F32)
            for s in range(slots):
                hit = jnp.where(ids[where + s] == pair, 1.0, 0.0).astype(F32)
                chosen = chosen + urecv[p, s].astype(F32) * hit
            uk[at_rows(p), at_cols(pair)] = chosen.astype(BF16)
            return carry

        lax.fori_loop(0, NPR, one_pair, 0)

    own_u.wait()
    updated_pairs(me)
    for k in far_first[::-1]:
        for s in range(slots):
            sent(s, k).wait()
        updated_pairs(lax.rem(me - k + n, n))

    def block(p, carry):
        at = pl.ds(pl.multiple_of(p * 256, 256), 256)
        total = lax.dot_general(uk[at, :], tk[...], (((1,), (1,)), ((), ())), preferred_element_type=F32)
        part[at, :] = total
        psend[at, :] = total.astype(BF16)
        return carry

    lax.fori_loop(0, n * rows // 256, block, 0)

    def p_part(c):
        return psend.at[pl.ds(pl.multiple_of(c * rows, rows), rows)]

    shares = [
        remote(p_part(ahead(k)), precv.at[k], p_send.at[k], p_recv.at[k], dist, ahead(k)) for k in far_first
    ]
    for copy in shares:
        copy.start()
    result = part[pl.ds(pl.multiple_of(me * rows, rows), rows), :]
    for k, copy in zip(far_first, shares):
        copy.wait()
        result = result + precv[k].astype(F32)
    out_ref[...] = result


def iota(shape, dim):
    return lax.broadcasted_iota(jnp.int32, shape, dim)


def nt(a, b):
    return lax.dot_general(a, b, (((1,), (1,)), ((), ())), preferred_element_type=F32)


def nn(a, b):
    return jnp.dot(a, b, preferred_element_type=F32)


def line_kernel(n, groups, atoms, source_ids, occ_ids, virt_ids, pair_ids, t_ref, green_ref, out_ref, table, halves, moved, stack, match_op, tf, xg, wg, uf,
                first_op, second_op, gather, select, place, lift, turn_v, blk, cross, partner_in, cross_in,
                g_send, g_recv, y_send, y_recv, m_send, m_recv, c_send, c_recv, p_send, p_recv):
    slots, rows, width = t_ref.shape
    blocks = green_ref.shape[0] // 2
    chunks = width // LANES
    half = BLK // 2
    part_rows = rows // 2
    deep = BLK * LANES
    dist = lax.axis_index("dist")
    me = lax.axis_index("ctr")
    before = lax.rem(dist + groups - 1, groups)
    after = lax.rem(dist + 1, groups)
    lines = n // 2
    high, low = me // 2, lax.rem(me, 2)
    partner = high * 2 + 1 - low
    mirrored = lax.rem(dist, 2)

    def flip(a):
        return jnp.where(mirrored == 1, lines - 1 - a, a)

    place_at = flip(high)

    def at_place(a, y):
        return flip(a) * 2 + y

    def signal(d, c):
        pl.semaphore_signal(barrier, inc=1, device_id=(d, c), device_id_type=pl.DeviceIdType.MESH)

    def remote(src, dst, send, recv, d, c):
        return pltpu.make_async_remote_copy(
            src_ref=src, dst_ref=dst, send_sem=send, recv_sem=recv, device_id=(d, c),
            device_id_type=pl.DeviceIdType.MESH,
        )

    barrier = pltpu.get_barrier_semaphore()
    for k in range(1, n):
        signal(dist, lax.rem(me + k, n))
    signal(before, me)
    signal(after, me)

    row, col = iota((BLK, BLK), 0), iota((BLK, BLK), 1)
    wanted = jnp.where(row < half, 2 * row, 2 * (row - half) + 1)
    perm = (wanted == col).astype(BF16)
    mine = me * blocks
    for b in range(blocks):
        turned = nn(perm, green_ref[blocks + b]).astype(BF16)
        turned = nt(turned, perm).astype(BF16)
        table[mine + b] = jnp.concatenate([green_ref[b], turned], axis=1)

    pl.semaphore_wait(barrier, n + 1)

    def line(k):
        return lax.rem(high + k, lines) * 2

    def at_home(c):
        return table.at[pl.ds(c * blocks, blocks)]

    def across(c):
        return table.at[pl.ds((n + c) * blocks, blocks)]

    first_hop = [
        remote(at_home(me), at_home(me), g_send.at[0, k], g_recv.at[0, k], dist, line(k) + low)
        for k in range(1, lines)
    ]
    for copy in first_hop:
        copy.start()
    second_hop, third_hop = [], []

    def onward(k):
        c = line(lines - k) + low
        second_hop.append(remote(at_home(c), at_home(c), g_send.at[1, k], g_recv.at[1, k], dist, partner))
        second_hop[-1].start()
        third_hop.append(remote(at_home(c), across(c), g_send.at[2, k], g_recv.at[2, k], before, me))
        third_hop[-1].start()

    onward(0)

    wide = slots * LANES
    r_, c_ = iota((wide, wide), 0), iota((wide, wide), 1)
    select[...] = (
        r_ == ((c_ // half) % slots) * LANES + ((c_ // LANES) % 2) * BLK + (c_ // (2 * LANES)) * half + c_ % half
    ).astype(BF16)
    own_rows = pl.ds(pl.multiple_of(low * rows, rows), rows)
    per = 8
    for q in range(0, chunks, per):
        x = jnp.concatenate(
            [
                jnp.concatenate([t_ref[j, :, (q + p) * LANES:(q + p + 1) * LANES] for j in range(slots)], axis=1)
                for p in range(per)
            ],
            axis=0,
        )
        got = nn(x, select[...]).astype(BF16)
        for p in range(per):
            for h in range(2):
                for e in range(2):
                    at = (e * half + q + p) * LANES
                    halves[h, own_rows, at:at + LANES] = got[
                        p * rows:(p + 1) * rows, (h * 2 + e) * LANES:(h * 2 + e + 1) * LANES
                    ]

    def rows_of(k):
        y = low if k < 2 else 1 - low
        return pl.ds(pl.multiple_of(y * rows + (k % 2) * part_rows, part_rows), part_rows)

    pieces = 2
    piece = deep // pieces

    def over_y(phase, k, x):
        h = 1 - low if phase == 0 else low
        at = halves.at[h, rows_of(k), pl.ds(x * piece, piece)]
        sem = k * pieces + x
        return remote(at, at, y_send.at[phase, sem], y_recv.at[phase, sem], dist, partner)

    def from_y(phase, k, x):
        at = halves.at[low if phase == 0 else 1 - low, rows_of(2 + k), pl.ds(x * piece, piece)]
        sem = k * pieces + x
        return remote(at, at, y_send.at[phase, sem], y_recv.at[phase, sem], dist, partner)

    def over_z(slot, k, x, own, to):
        at, lanes = rows_of(k), pl.ds(x * piece, piece)
        src = halves.at[low, at, lanes] if own else moved.at[slot, at, lanes]
        sem = k * pieces + x
        return remote(
            src, moved.at[slot, at, lanes], m_send.at[slot, sem], m_recv.at[slot, sem], dist, at_place(to, low)
        )

    def spread(g):
        at_rows = rows_of(g)
        for h in range(2):
            for m in range(BLK):
                tf[h, m * part_rows:(m + 1) * part_rows, :] = halves[h, at_rows, m * LANES:(m + 1) * LANES].astype(F32)
            for i in range(part_rows):
                xg[g % 2, i * BLK:(i + 1) * BLK, h * LANES:(h + 1) * LANES] = tf[
                    h, pl.ds(i, BLK, stride=part_rows), :
                ].astype(BF16)

    starts = {0: (0, 1), 1: (1, 2), 3: (2, 2)}

    def send_own(k, places):
        for a in places:
            slot, to = starts[a]

            @pl.when(place_at == a)
            def _():
                for x in range(pieces):
                    over_z(slot, k, x, True, to).start()

    over_y(0, 0, 0).start()
    over_y(0, 0, 1).start()
    for k in range(2):
        send_own(k, (0, 1))
    for k in range(1, lines):
        first_hop[k - 1].wait_recv()
        onward(k)
    for phase, k in ((0, 1), (1, 0), (1, 1)):
        for x in range(pieces):
            over_y(phase, k, x).start()

    def relay(a, slot, k):
        @pl.when(place_at == a)
        def _():
            for x in range(pieces):
                over_z(slot, k, x, False, a).wait_recv()
                over_z(slot, k, x, False, a + 1).start()

    r_, c_ = iota((wide, slots * BLK), 0), iota((wide, slots * BLK), 1)
    place[...] = ((r_ % LANES >= BLK) & (c_ == (r_ // LANES) * BLK + r_ % LANES - BLK)).astype(BF16)
    r_, c_ = iota((2 * LANES, LANES), 0), iota((2 * LANES, LANES), 1)
    for t in range(slots):
        lift[t] = ((c_ < BLK) & (r_ == (c_ // half) * LANES + t * half + c_ % half)).astype(BF16)
    r_, c_ = iota((LANES, wide), 0), iota((LANES, wide), 1)
    turn_v[...] = ((r_ // half == c_ // LANES) & (c_ % LANES == low * half + r_ % half)).astype(BF16)

    def third(k):
        second_hop[k].wait_recv()
        c = line(lines - k) + 1 - low
        third_hop.append(remote(at_home(c), across(c), g_send.at[3, k], g_recv.at[3, k], before, me))
        third_hop[-1].start()

    third(0)
    for x in range(pieces):
        from_y(0, 0, x).wait_recv()
    send_own(2, (0, 1))
    for k in range(1, lines):
        third(k)
    relay(1, 0, 0)
    relay(2, 1, 0)
    relay(2, 1, 1)
    relay(1, 0, 1)
    total = n * blocks * groups
    base = dist * n * blocks
    atom = dist * lines + high

    def position(value):
        shift = value - base
        return jnp.minimum(jnp.where(shift < 0, shift + total, shift), 2 * n * blocks - 1)

    def atom_at(a):
        return dist * lines + flip(a)

    def feeding(a, s, j):
        r, live = jnp.int32(0), jnp.int32(0)
        for x in range(slots):
            hit = source_ids[s, x, a] == j
            r, live = jnp.where(hit, x, r), jnp.where(hit, 1, live)
        return r, live

    def green(a, s, r, live):
        return position(occ_ids[s, r, a]), position(virt_ids[s, r, a]), live.astype(F32)

    used = {0: (0, (1, 2, 3)), 1: (1, (2, 3)), 2: (3, (2,))}

    def wanted_here(slot):
        hit = place_at == used[slot][1][0]
        for a in used[slot][1][1:]:
            hit = hit | (place_at == a)
        return hit

    def adjoint_entries(a):
        other = atom_at(a)
        entries = []
        for t in range(slots):
            pair = pair_ids[t, atom]
            s, met = jnp.int32(0), jnp.int32(0)
            for x in range(slots):
                hit = pair_ids[x, other] == pair
                s, met = jnp.where(hit, x, s), jnp.where(hit, 1, met)
            row = []
            for o in range(slots):
                r, live = feeding(other, s, o)
                row.append(green(other, s, r, live * met))
            entries.append(row)
        return entries

    own_entries = [[green(atom, o, *feeding(atom, o, t)) for o in range(slots)] for t in range(slots)]
    entries = {slot: adjoint_entries(used[slot][0]) for slot in used}

    r_, c_ = iota((LANES, LANES), 0), iota((LANES, LANES), 1)
    for slot in used:
        other = atom_at(used[slot][0])
        match = jnp.zeros((LANES, LANES), F32)
        for s in range(slots):
            for t in range(slots):
                hit = jnp.where(pair_ids[s, atom] == pair_ids[t, other], 1.0, 0.0)
                match = jnp.where((r_ // half == s) & (c_ // half == t), hit.astype(F32), match)
        match_op[:, slot * LANES:(slot + 1) * LANES] = jnp.where(r_ % half == c_ % half, match, 0.0).astype(BF16)

    spread(0)
    spread(1)
    relay(2, 1, 2)
    relay(2, 0, 0)
    for copy in third_hop:
        copy.wait_recv()
    for k in range(3):
        send_own(k, (3,))

    for t in range(slots):
        virt = []
        for o in range(slots):
            occ_pos, virt_pos, live = own_entries[t][o]
            virt.append((table[virt_pos].astype(F32) * live).astype(BF16))
            gather[3, t * BLK:(t + 1) * BLK, o * LANES:(o + 1) * LANES] = table[occ_pos]
        b = nt(turn_v[...], jnp.concatenate(virt, axis=1)).astype(BF16)
        second_op[0, :, t * LANES:(t + 1) * LANES] = nt(lift[t][:, :BLK], b).astype(BF16)
    size_op = slots * BLK
    unit = (iota((size_op, size_op), 0) == iota((size_op, size_op), 1)).astype(BF16)
    first_op[0] = nt(unit, nn(gather[3], place[...]).astype(BF16)).astype(BF16)

    for x in range(pieces):
        from_y(0, 1, x).wait_recv()
    send_own(3, (0, 1, 3))

    def operators(slot):
        for t in range(slots):
            virt = []
            for o in range(slots):
                occ_pos, virt_pos, live = entries[slot][t][o]
                virt.append(
                    (table[virt_pos, pl.ds(pl.multiple_of(low * half, half), half), :].astype(F32) * live).astype(BF16)
                )
                gather[slot, o * BLK:(o + 1) * BLK, t * LANES:(t + 1) * LANES] = table[occ_pos]
            second_op[1 + slot, :, t * LANES:(t + 1) * LANES] = nt(lift[t], jnp.concatenate(virt, axis=0)).astype(BF16)
        first_op[1 + slot] = nn(gather[slot], place[...]).astype(BF16)

    for slot in used:
        operators(slot)

    lanes2 = (iota((BLK, 2 * LANES), 1) // half) % slots

    def first(k, u, g):
        got = nn(xg[lax.rem(g, 2)], second_op[k]).astype(BF16)
        for i in range(part_rows):
            for t in range(slots):
                wg[u, i, t * BLK:(t + 1) * BLK, :] = got[i * BLK:(i + 1) * BLK, t * LANES:(t + 1) * LANES]

    def second(k, u):
        for p in range(part_rows // 2):
            both = nn(first_op[k], jnp.concatenate([wg[u, 2 * p], wg[u, 2 * p + 1]], axis=1))
            res = both[:BLK]
            for o in range(1, slots):
                res = jnp.where(lanes2 == o, both[o * BLK:(o + 1) * BLK], res)
            for x in range(2):
                uf[u, (2 * p + x) * BLK:(2 * p + x + 1) * BLK, :] = res[:, x * LANES:(x + 1) * LANES]

    def keep(k, u, at_rows):
        for m in range(BLK):
            stack[k, at_rows, m * LANES:(m + 1) * LANES] = uf[u, pl.ds(m, part_rows, stride=BLK), :].astype(BF16)

    def two_stacks(k, at_rows, g):
        for u in range(2):
            first(k + u, u, g)
        for u in range(2):
            second(k + u, u)
        for u in range(2):
            keep(k + u, u, at_rows)

    def reorder(at_rows):
        x = jnp.concatenate([stack[0, at_rows, m * LANES:(m + 1) * LANES] for m in range(BLK)], axis=0)
        got = nn(x, match_op[...]).astype(BF16)
        below = pl.ds(at_rows.start + BLK, part_rows)
        for m in range(BLK):
            for slot in used:
                stack[1 + slot, below, m * LANES:(m + 1) * LANES] = got[
                    m * part_rows:(m + 1) * part_rows, slot * LANES:(slot + 1) * LANES
                ]

    due = ((0, 2, 0, 1), (1, 2, 1, 3), (0, 1, 0, 2), (2, 2, 0, 2), (2, 1, 0, 3), (4, 2, 0, 3))

    def step(g, carry):
        y = jnp.where(g < 2, low, 1 - low)
        at_rows = pl.ds(pl.multiple_of(y * rows + lax.rem(g, 2) * part_rows, part_rows), part_rows)
        for x in range(2):
            @pl.when(g == 2 + x)
            def _():
                for p in range(pieces):
                    from_y(1, x, p).wait_recv()
                spread(2 + x)

        def relays(side):
            for at, a, slot, group in due:
                if at % 2 == side:
                    @pl.when(g == at // 2)
                    def _():
                        relay(a, slot, group)

        two_stacks(0, at_rows, g)
        relays(0)

        @pl.when(place_at >= 2)
        def _():
            reorder(at_rows)
            two_stacks(2, at_rows, g)

        @pl.when(place_at == 1)
        def _():
            reorder(at_rows)
        relays(1)
        return carry

    lax.fori_loop(0, 4, step, 0)

    for c in range(lines):
        blk[c] = jnp.zeros((BLK, LANES), F32)

    def lay(x):
        return jnp.concatenate([x, jnp.zeros((BLK, LANES - BLK), F32)], axis=1)


    def returned(slot, y):
        a = used[slot][0]
        return remote(
            cross.at[slot, pl.ds(y * rows, rows)], cross_in.at[place_at, low], c_send.at[slot, y],
            c_recv.at[place_at, low], dist, at_place(a, y),
        )

    def product(slot):
        a = used[slot][0]
        for k in range(4):
            if slot == 2:
                for x in range(pieces):
                    over_z(slot, k, x, False, a).wait_recv()
            else:
                @pl.when(place_at == 3)
                def _():
                    for x in range(pieces):
                        over_z(slot, k, x, False, a).wait_recv()
        both = nt(stack[1 + slot], moved[slot])
        both = jnp.concatenate([both, jnp.zeros((2 * BLK, LANES - BLK), F32)], axis=1)
        cross[slot] = both.T[:BLK]
        for y in range(2):
            returned(slot, y).start()
        blk[flip(a)] = both[BLK:]

    for slot in (1, 0, 2):
        @pl.when(wanted_here(slot))
        def _():
            product(slot)

    blk[high] = lay(nt(stack[0, :BLK], halves[low]))
    other_rows = pl.ds(pl.multiple_of((1 - low) * rows, rows), rows)
    to_partner = remote(blk.at[:, other_rows], partner_in, p_send.at[0], p_recv.at[0], dist, partner)
    to_partner.start()

    came = {1: (0,), 2: (0, 1, 3), 3: (0, 1)}
    for src, takers in came.items():
        for a in takers:
            @pl.when(place_at == a)
            def _():
                for y in range(2):
                    remote(
                        cross.at[0, pl.ds(0, rows)], cross_in.at[src, y], c_send.at[0, 0], c_recv.at[src, y], dist, me
                    ).wait_recv()
                blk[flip(src), own_rows] = cross_in[src, 0] + cross_in[src, 1]
    to_partner.wait()
    tiles = [(blk[c, own_rows] + partner_in[c])[:, :BLK] for c in range(lines)]
    out_ref[...] = jnp.concatenate(tiles, axis=1)

    for copy in first_hop + second_hop + third_hop:
        copy.wait_send()
    for k in range(2):
        for x in range(pieces):
            over_y(0, k, x).wait_send()
            over_y(1, k, x).wait_send()
    for slot, senders in {0: (0, 1, 2), 1: (1, 2), 2: (3,)}.items():
        for a in senders:
            @pl.when(place_at == a)
            def _():
                for k in range(4):
                    for x in range(pieces):
                        over_z(slot, k, x, False, 0).wait_send()

        @pl.when(wanted_here(slot))
        def _():
            for y in range(2):
                returned(slot, y).wait_send()


def on_line(n, groups, atoms, source, occ, virt, pairs, tensor, green):
    slots, rows, width = tensor.shape
    blocks = green.shape[0] // 2
    lines = n // 2
    deep = BLK * LANES
    part_rows = rows // 2
    vmem = pl.BlockSpec(memory_space=pltpu.VMEM)
    dma = pltpu.SemaphoreType.DMA
    return pl.pallas_call(
        functools.partial(line_kernel, n, groups, atoms),
        out_shape=jax.ShapeDtypeStruct((rows, lines * BLK), F32),
        in_specs=[pl.BlockSpec(memory_space=pltpu.SMEM)] * 4 + [vmem, vmem],
        out_specs=vmem,
        scratch_shapes=[
            pltpu.VMEM((2 * n * blocks, BLK, LANES), BF16),
            pltpu.VMEM((2, BLK, deep), BF16),
            pltpu.VMEM((3, BLK, deep), BF16),
            pltpu.VMEM((4, 2 * BLK, deep), BF16),
            pltpu.VMEM((LANES, 3 * LANES), BF16),
            pltpu.VMEM((2, part_rows * BLK, LANES), F32),
            pltpu.VMEM((2, part_rows * BLK, 2 * LANES), BF16),
            pltpu.VMEM((2, part_rows, slots * BLK, LANES), BF16),
            pltpu.VMEM((2, part_rows * BLK, LANES), F32),
            pltpu.VMEM((4, slots * BLK, slots * BLK), BF16),
            pltpu.VMEM((4, 2 * LANES, slots * LANES), BF16),
            pltpu.VMEM((4, slots * BLK, slots * LANES), BF16),
            pltpu.VMEM((slots * LANES, slots * LANES), BF16),
            pltpu.VMEM((slots * LANES, slots * BLK), BF16),
            pltpu.VMEM((slots, 2 * LANES, LANES), BF16),
            pltpu.VMEM((LANES, slots * LANES), BF16),
            pltpu.VMEM((lines, BLK, LANES), F32),
            pltpu.VMEM((3, BLK, LANES), F32),
            pltpu.VMEM((lines, rows, LANES), F32),
            pltpu.VMEM((lines, 2, rows, LANES), F32),
            dma((4, lines)),
            dma((4, lines)),
            dma((2, 4)),
            dma((2, 4)),
            dma((3, 8)),
            dma((3, 8)),
            dma((3, 2)),
            dma((lines, 2)),
            dma((1,)),
            dma((1,)),
        ],
        compiler_params=pltpu.CompilerParams(
            collective_id=1, has_side_effects=True, vmem_limit_bytes=48 * 2**20
        ),
    )(*[jnp.transpose(x, (1, 2, 0)) for x in (source, occ, virt)], pairs.T, tensor, green)


def solution(mesh):
    n = mesh.shape["ctr"]
    groups = mesh.shape["dist"]

    def shards(three_centre, occupied_green, virtual_green, pair_index, source_slot, occupied_index, virtual_index):
        rows, slots, width = three_centre.shape
        blocks = occupied_green.shape[0]
        atoms = pair_index.shape[0]
        chunks = width // LANES
        cols = width // n
        tensor = jnp.transpose(three_centre, (1, 0, 2))
        green = jnp.concatenate([virtual_green, occupied_green], axis=0).reshape(2 * blocks, BLK, BLK)
        ids = jnp.concatenate(
            [x.reshape(-1) for x in (source_slot, occupied_index, virtual_index, pair_index)]
        )
        vmem = pl.BlockSpec(memory_space=pltpu.VMEM)
        dma = pltpu.SemaphoreType.DMA
        if n == 8 and groups % 2 == 0 and rows * 2 == BLK:
            return on_line(
                n, groups, atoms, source_slot, occupied_index, virtual_index, pair_index, tensor, green
            )
        return pl.pallas_call(
            functools.partial(kernel, n, groups, atoms),
            out_shape=jax.ShapeDtypeStruct((rows, n * rows), F32),
            in_specs=[pl.BlockSpec(memory_space=pltpu.SMEM), vmem, vmem],
            out_specs=vmem,
            scratch_shapes=[
                pltpu.VMEM((2 * n * blocks, BLK, LANES), BF16),
                pltpu.VMEM((rows * chunks, LANES), F32),
                pltpu.VMEM((slots, rows * chunks, LANES), BF16),
                pltpu.VMEM((slots * BLK, rows * LANES), BF16),
                pltpu.VMEM((BLK, slots * BLK), BF16),
                pltpu.VMEM((slots, n, rows, cols), BF16),
                pltpu.VMEM((n, slots, rows, cols), BF16),
                pltpu.VMEM((n, slots, rows, cols), BF16),
                pltpu.VMEM((n * rows, NPR * cols), BF16),
                pltpu.VMEM((n * rows, NPR * cols), BF16),
                pltpu.VMEM((n * rows, n * rows), F32),
                pltpu.VMEM((n * rows, n * rows), BF16),
                pltpu.VMEM((n, rows, n * rows), BF16),
                dma((4, n // 2)),
                dma((4, n // 2)),
                dma((n,)),
                dma((n,)),
                dma((slots, n)),
                dma((slots, n)),
                dma((n,)),
                dma((n,)),
                dma((2,)),
            ],
            compiler_params=pltpu.CompilerParams(
                collective_id=0, has_side_effects=True, vmem_limit_bytes=48 * 2**20
            ),
        )(ids, tensor, green)

    return jax.shard_map(
        shards,
        mesh=mesh,
        in_specs=(
            P(("dist", "ctr"), None, None),
            P(("dist", "ctr"), None),
            P(("dist", "ctr"), None),
            P(),
            P(),
            P(),
            P(),
        ),
        out_specs=P(("dist", "ctr"), None),
        check_vma=False,
    )
```

```python
import functools

import jax
import jax.numpy as jnp
from jax import lax
from jax.experimental import pallas as pl
from jax.experimental.pallas import tpu as pltpu
from jax.sharding import PartitionSpec as P

BLK = 64
NPR = 8
LANES = 128
F32 = jnp.float32
BF16 = jnp.bfloat16


def kernel(n, groups, atoms, ids, t_ref, green_ref, out_ref, table, tf, tt, wcat, ocat, usend, urecv, trecv,
           uk, tk, part, psend, precv, g_send, g_recv, t_send, t_recv, u_send, u_recv, p_send, p_recv, own_sem):
    slots, rows, width = t_ref.shape
    chunks = width // LANES
    blocks = green_ref.shape[0] // 2
    cols = width // n
    per = cols // LANES
    dist = lax.axis_index("dist")
    me = lax.axis_index("ctr")
    before = lax.rem(dist + groups - 1, groups)
    after = lax.rem(dist + 1, groups)

    far_first = sorted(range(1, n), key=lambda k: -min(k, n - k))

    def ahead(k):
        return lax.rem(me + k, n)

    def signal(d, c):
        pl.semaphore_signal(barrier, inc=1, device_id=(d, c), device_id_type=pl.DeviceIdType.MESH)

    def remote(src, dst, send, recv, d, c):
        return pltpu.make_async_remote_copy(
            src_ref=src, dst_ref=dst, send_sem=send, recv_sem=recv, device_id=(d, c),
            device_id_type=pl.DeviceIdType.MESH,
        )

    barrier = pltpu.get_barrier_semaphore()
    for k in range(1, n):
        signal(dist, ahead(k))
    signal(before, me)
    signal(after, me)

    row = lax.broadcasted_iota(jnp.int32, (BLK, BLK), 0)
    col = lax.broadcasted_iota(jnp.int32, (BLK, BLK), 1)
    half = BLK // 2
    wanted = jnp.where(row < half, 2 * row, 2 * (row - half) + 1)
    perm = (wanted == col).astype(BF16)
    mine = me * blocks
    for b in range(blocks):
        occ = green_ref[blocks + b]
        turned = lax.dot_general(perm, occ, (((1,), (1,)), ((), ())), preferred_element_type=F32).astype(BF16)
        turned = lax.dot_general(turned, perm, (((1,), (1,)), ((), ())), preferred_element_type=F32).astype(BF16)
        table[mine + b] = jnp.concatenate([green_ref[b], turned], axis=1)

    pl.semaphore_wait(barrier, n + 1)

    lines = n // 2
    high, low = me // 2, lax.rem(me, 2)
    partner = high * 2 + 1 - low

    def line(k):
        return lax.rem(high + k, lines) * 2

    def at_home(c):
        return table.at[pl.ds(c * blocks, blocks)]

    def across(c):
        return table.at[pl.ds((n + c) * blocks, blocks)]

    first_hop = [
        remote(at_home(me), at_home(me), g_send.at[0, k], g_recv.at[0, k], dist, line(k) + low)
        for k in range(1, lines)
    ]
    for copy in first_hop:
        copy.start()

    def t_part(c):
        return t_ref.at[:, :, pl.ds(pl.multiple_of(c * cols, LANES), cols)]

    tensor = [
        remote(t_part(ahead(k)), trecv.at[me], t_send.at[k], t_recv.at[k], dist, ahead(k)) for k in far_first
    ]
    for copy in tensor:
        copy.start()
    own_t = pltpu.make_async_copy(t_part(me), trecv.at[me], own_sem.at[0])
    own_t.start()

    second_hop, third_hop = [], []
    for k in range(lines):
        if k:
            first_hop[k - 1].wait_recv()
        c = line(lines - k) + low
        second_hop.append(remote(at_home(c), at_home(c), g_send.at[1, k], g_recv.at[1, k], dist, partner))
        second_hop[-1].start()
        third_hop.append(remote(at_home(c), across(c), g_send.at[2, k], g_recv.at[2, k], before, me))
        third_hop[-1].start()

    def turn(s, carry):
        for j in range(chunks):
            tf[j * rows:(j + 1) * rows, :] = t_ref[s, :, j * LANES:(j + 1) * LANES].astype(F32)
        for i in range(rows):
            tt[s, i * chunks:(i + 1) * chunks, :] = tf[pl.ds(i, chunks, stride=rows), :].astype(BF16)
        return carry

    lax.fori_loop(0, slots, turn, 0)

    for k in range(lines):
        second_hop[k].wait_recv()
        c = line(lines - k) + 1 - low
        third_hop.append(remote(at_home(c), across(c), g_send.at[3, k], g_recv.at[3, k], before, me))
        third_hop[-1].start()
    for copy in third_hop:
        copy.wait()
    for copy in first_hop + second_hop:
        copy.wait_send()

    size = atoms * slots
    atom = (dist * n + me) * rows // BLK
    total = n * blocks * groups
    base = dist * n * blocks

    def position(value):
        shift = value - base
        return jnp.minimum(jnp.where(shift < 0, shift + total, shift), 2 * n * blocks - 1)

    step_rows = 8 * chunks
    lane = lax.broadcasted_iota(jnp.int32, (half, LANES), 1)

    def update(s, carry):
        at = (atom * slots + s) * slots
        for r in range(slots):
            src = ids[at + r]
            live = jnp.where(src >= 0, 1.0, 0.0).astype(F32)
            src = jnp.maximum(src, 0)
            virt = table[position(ids[2 * size * slots + at + r])].astype(F32)[:, :BLK] * live
            zero = jnp.zeros((BLK, LANES), F32)
            twice = jnp.concatenate([virt, virt], axis=1)
            weight = jnp.concatenate(
                [jnp.concatenate([twice, zero], axis=1), jnp.concatenate([zero, twice], axis=1)], axis=0
            ).astype(BF16)
            ocat[:, r * BLK:(r + 1) * BLK] = table[position(ids[size * slots + at + r])][:, BLK:]
            for h in range(rows // 8):
                got = jnp.dot(
                    tt[src, h * step_rows:(h + 1) * step_rows, :], weight, preferred_element_type=F32
                ).astype(BF16)
                for x in range(8):
                    i = h * 8 + x
                    for e in range(2):
                        wcat[r * BLK + e * half:r * BLK + (e + 1) * half, i * LANES:(i + 1) * LANES] = got[
                            x * chunks:(x + 1) * chunks, e * LANES:(e + 1) * LANES
                        ]
        occ = ocat[...]
        for h in range(rows // 4):
            both = jnp.dot(occ, wcat[:, h * 4 * LANES:(h + 1) * 4 * LANES], preferred_element_type=F32)
            for x in range(4):
                i = h * 4 + x
                piece = both[:, x * LANES:(x + 1) * LANES]
                tf[i * chunks:(i + 1) * chunks, :] = jnp.where(lane < BLK, piece[:half], piece[half:])
        for q in range(chunks):
            usend[s, q // per, :, (q % per) * LANES:(q % per + 1) * LANES] = tf[
                pl.ds(q, rows, stride=chunks), :
            ].astype(BF16)
        for k in far_first:
            sent(s, k).start()
        return carry

    def sent(s, k):
        return remote(
            usend.at[s, ahead(k)], urecv.at[me, s], u_send.at[s, k], u_recv.at[s, k], dist, ahead(k)
        )

    lax.fori_loop(0, slots, update, 0)
    own_u = pltpu.make_async_copy(usend.at[:, me], urecv.at[me], own_sem.at[1])
    own_u.start()
    own_t.wait()
    for copy in tensor:
        copy.wait()

    first = dist * (n * rows // BLK)
    pairs = 3 * size * slots

    def pick(src, pair, p):
        where = pairs + (first + p * rows // BLK) * slots
        slot = jnp.int32(0)
        live = jnp.int32(0)
        for s in range(slots):
            hit = ids[where + s] == pair
            slot = jnp.where(hit, s, slot)
            live = jnp.where(hit, 1, live)
        return (src[p, slot].astype(F32) * live.astype(F32)).astype(BF16)

    def at_rows(p):
        return pl.ds(pl.multiple_of(p * rows, rows), rows)

    def at_cols(pair):
        return pl.ds(pl.multiple_of(pair * cols, LANES), cols)

    def tensor_pair(pair, carry):
        def gather(p, inner):
            tk[at_rows(p), at_cols(pair)] = pick(trecv, pair, p)
            return inner

        return lax.fori_loop(0, n, gather, carry)

    lax.fori_loop(0, NPR, tensor_pair, 0)

    def updated_pairs(p):
        where = pairs + (first + p * rows // BLK) * slots

        def one_pair(pair, carry):
            chosen = jnp.zeros((rows, cols), F32)
            for s in range(slots):
                hit = jnp.where(ids[where + s] == pair, 1.0, 0.0).astype(F32)
                chosen = chosen + urecv[p, s].astype(F32) * hit
            uk[at_rows(p), at_cols(pair)] = chosen.astype(BF16)
            return carry

        lax.fori_loop(0, NPR, one_pair, 0)

    own_u.wait()
    updated_pairs(me)
    for k in far_first[::-1]:
        for s in range(slots):
            sent(s, k).wait()
        updated_pairs(lax.rem(me - k + n, n))

    def block(p, carry):
        at = pl.ds(pl.multiple_of(p * 256, 256), 256)
        total = lax.dot_general(uk[at, :], tk[...], (((1,), (1,)), ((), ())), preferred_element_type=F32)
        part[at, :] = total
        psend[at, :] = total.astype(BF16)
        return carry

    lax.fori_loop(0, n * rows // 256, block, 0)

    def p_part(c):
        return psend.at[pl.ds(pl.multiple_of(c * rows, rows), rows)]

    shares = [
        remote(p_part(ahead(k)), precv.at[k], p_send.at[k], p_recv.at[k], dist, ahead(k)) for k in far_first
    ]
    for copy in shares:
        copy.start()
    result = part[pl.ds(pl.multiple_of(me * rows, rows), rows), :]
    for k, copy in zip(far_first, shares):
        copy.wait()
        result = result + precv[k].astype(F32)
    out_ref[...] = result


def iota(shape, dim):
    return lax.broadcasted_iota(jnp.int32, shape, dim)


def nt(a, b):
    return lax.dot_general(a, b, (((1,), (1,)), ((), ())), preferred_element_type=F32)


def nn(a, b):
    return jnp.dot(a, b, preferred_element_type=F32)


def line_kernel(n, groups, atoms, source_ids, occ_ids, virt_ids, pair_ids, t_ref, green_ref, out_ref, table, halves, moved, stack, match_op, tf, xg, wg, uf,
                first_op, second_op, gather, select, place, lift, turn_v, blk, cross, partner_in, cross_in,
                g_send, g_recv, y_send, y_recv, m_send, m_recv, c_send, c_recv, p_send, p_recv):
    slots, rows, width = t_ref.shape
    blocks = green_ref.shape[0] // 2
    chunks = width // LANES
    half = BLK // 2
    part_rows = rows // 2
    deep = BLK * LANES
    dist = lax.axis_index("dist")
    me = lax.axis_index("ctr")
    before = lax.rem(dist + groups - 1, groups)
    after = lax.rem(dist + 1, groups)
    lines = n // 2
    high, low = me // 2, lax.rem(me, 2)
    partner = high * 2 + 1 - low
    mirrored = lax.rem(dist, 2)

    def flip(a):
        return jnp.where(mirrored == 1, lines - 1 - a, a)

    place_at = flip(high)

    def at_place(a, y):
        return flip(a) * 2 + y

    def signal(d, c):
        pl.semaphore_signal(barrier, inc=1, device_id=(d, c), device_id_type=pl.DeviceIdType.MESH)

    def remote(src, dst, send, recv, d, c):
        return pltpu.make_async_remote_copy(
            src_ref=src, dst_ref=dst, send_sem=send, recv_sem=recv, device_id=(d, c),
            device_id_type=pl.DeviceIdType.MESH,
        )

    barrier = pltpu.get_barrier_semaphore()
    for k in range(1, n):
        signal(dist, lax.rem(me + k, n))
    signal(before, me)
    signal(after, me)

    row, col = iota((BLK, BLK), 0), iota((BLK, BLK), 1)
    wanted = jnp.where(row < half, 2 * row, 2 * (row - half) + 1)
    perm = (wanted == col).astype(BF16)
    mine = me * blocks
    for b in range(blocks):
        turned = nn(perm, green_ref[blocks + b]).astype(BF16)
        turned = nt(turned, perm).astype(BF16)
        table[mine + b] = jnp.concatenate([green_ref[b], turned], axis=1)

    pl.semaphore_wait(barrier, n + 1)

    def line(k):
        return lax.rem(high + k, lines) * 2

    def at_home(c):
        return table.at[pl.ds(c * blocks, blocks)]

    def across(c):
        return table.at[pl.ds((n + c) * blocks, blocks)]

    first_hop = [
        remote(at_home(me), at_home(me), g_send.at[0, k], g_recv.at[0, k], dist, line(k) + low)
        for k in range(1, lines)
    ]
    for copy in first_hop:
        copy.start()
    second_hop, third_hop = [], []

    def onward(k):
        c = line(lines - k) + low
        second_hop.append(remote(at_home(c), at_home(c), g_send.at[1, k], g_recv.at[1, k], dist, partner))
        second_hop[-1].start()
        third_hop.append(remote(at_home(c), across(c), g_send.at[2, k], g_recv.at[2, k], before, me))
        third_hop[-1].start()

    onward(0)

    wide = slots * LANES
    r_, c_ = iota((wide, wide), 0), iota((wide, wide), 1)
    select[...] = (
        r_ == ((c_ // half) % slots) * LANES + ((c_ // LANES) % 2) * BLK + (c_ // (2 * LANES)) * half + c_ % half
    ).astype(BF16)
    own_rows = pl.ds(pl.multiple_of(low * rows, rows), rows)
    per = 8
    for q in range(0, chunks, per):
        x = jnp.concatenate(
            [
                jnp.concatenate([t_ref[j, :, (q + p) * LANES:(q + p + 1) * LANES] for j in range(slots)], axis=1)
                for p in range(per)
            ],
            axis=0,
        )
        got = nn(x, select[...]).astype(BF16)
        for p in range(per):
            for h in range(2):
                for e in range(2):
                    at = (e * half + q + p) * LANES
                    halves[h, own_rows, at:at + LANES] = got[
                        p * rows:(p + 1) * rows, (h * 2 + e) * LANES:(h * 2 + e + 1) * LANES
                    ]

    def rows_of(k):
        y = low if k < 2 else 1 - low
        return pl.ds(pl.multiple_of(y * rows + (k % 2) * part_rows, part_rows), part_rows)

    pieces = 2
    piece = deep // pieces

    def over_y(phase, k, x):
        h = 1 - low if phase == 0 else low
        at = halves.at[h, rows_of(k), pl.ds(x * piece, piece)]
        sem = k * pieces + x
        return remote(at, at, y_send.at[phase, sem], y_recv.at[phase, sem], dist, partner)

    def from_y(phase, k, x):
        at = halves.at[low if phase == 0 else 1 - low, rows_of(2 + k), pl.ds(x * piece, piece)]
        sem = k * pieces + x
        return remote(at, at, y_send.at[phase, sem], y_recv.at[phase, sem], dist, partner)

    def over_z(slot, k, x, own, to):
        at, lanes = rows_of(k), pl.ds(x * piece, piece)
        src = halves.at[low, at, lanes] if own else moved.at[slot, at, lanes]
        sem = k * pieces + x
        return remote(
            src, moved.at[slot, at, lanes], m_send.at[slot, sem], m_recv.at[slot, sem], dist, at_place(to, low)
        )

    def spread(g):
        at_rows = rows_of(g)
        for h in range(2):
            for m in range(BLK):
                tf[h, m * part_rows:(m + 1) * part_rows, :] = halves[h, at_rows, m * LANES:(m + 1) * LANES].astype(F32)
            for i in range(part_rows):
                xg[g % 2, i * BLK:(i + 1) * BLK, h * LANES:(h + 1) * LANES] = tf[
                    h, pl.ds(i, BLK, stride=part_rows), :
                ].astype(BF16)

    starts = {0: (0, 1), 1: (1, 2), 3: (2, 2)}

    def send_own(k, places):
        for a in places:
            slot, to = starts[a]

            @pl.when(place_at == a)
            def _():
                for x in range(pieces):
                    over_z(slot, k, x, True, to).start()

    over_y(0, 0, 0).start()
    over_y(0, 0, 1).start()
    for k in range(2):
        send_own(k, (0, 1))
    for k in range(1, lines):
        first_hop[k - 1].wait_recv()
        onward(k)
    for phase, k in ((0, 1), (1, 0), (1, 1)):
        for x in range(pieces):
            over_y(phase, k, x).start()

    def relay(a, slot, k):
        @pl.when(place_at == a)
        def _():
            for x in range(pieces):
                over_z(slot, k, x, False, a).wait_recv()
                over_z(slot, k, x, False, a + 1).start()

    r_, c_ = iota((wide, slots * BLK), 0), iota((wide, slots * BLK), 1)
    place[...] = ((r_ % LANES >= BLK) & (c_ == (r_ // LANES) * BLK + r_ % LANES - BLK)).astype(BF16)
    r_, c_ = iota((2 * LANES, LANES), 0), iota((2 * LANES, LANES), 1)
    for t in range(slots):
        lift[t] = ((c_ < BLK) & (r_ == (c_ // half) * LANES + t * half + c_ % half)).astype(BF16)
    r_, c_ = iota((LANES, wide), 0), iota((LANES, wide), 1)
    turn_v[...] = ((r_ // half == c_ // LANES) & (c_ % LANES == low * half + r_ % half)).astype(BF16)

    def third(k):
        second_hop[k].wait_recv()
        c = line(lines - k) + 1 - low
        third_hop.append(remote(at_home(c), across(c), g_send.at[3, k], g_recv.at[3, k], before, me))
        third_hop[-1].start()

    third(0)
    for x in range(pieces):
        from_y(0, 0, x).wait_recv()
    send_own(2, (0, 1))
    for k in range(1, lines):
        third(k)
    relay(1, 0, 0)
    relay(2, 1, 0)
    relay(2, 1, 1)
    relay(1, 0, 1)
    total = n * blocks * groups
    base = dist * n * blocks
    atom = dist * lines + high

    def position(value):
        shift = value - base
        return jnp.minimum(jnp.where(shift < 0, shift + total, shift), 2 * n * blocks - 1)

    def atom_at(a):
        return dist * lines + flip(a)

    def feeding(a, s, j):
        r, live = jnp.int32(0), jnp.int32(0)
        for x in range(slots):
            hit = source_ids[s, x, a] == j
            r, live = jnp.where(hit, x, r), jnp.where(hit, 1, live)
        return r, live

    def green(a, s, r, live):
        return position(occ_ids[s, r, a]), position(virt_ids[s, r, a]), live.astype(F32)

    used = {0: (0, (1, 2, 3)), 1: (1, (2, 3)), 2: (3, (2,))}

    def wanted_here(slot):
        hit = place_at == used[slot][1][0]
        for a in used[slot][1][1:]:
            hit = hit | (place_at == a)
        return hit

    def adjoint_entries(a):
        other = atom_at(a)
        entries = []
        for t in range(slots):
            pair = pair_ids[t, atom]
            s, met = jnp.int32(0), jnp.int32(0)
            for x in range(slots):
                hit = pair_ids[x, other] == pair
                s, met = jnp.where(hit, x, s), jnp.where(hit, 1, met)
            row = []
            for o in range(slots):
                r, live = feeding(other, s, o)
                row.append(green(other, s, r, live * met))
            entries.append(row)
        return entries

    own_entries = [[green(atom, o, *feeding(atom, o, t)) for o in range(slots)] for t in range(slots)]
    entries = {slot: adjoint_entries(used[slot][0]) for slot in used}

    r_, c_ = iota((LANES, LANES), 0), iota((LANES, LANES), 1)
    for slot in used:
        other = atom_at(used[slot][0])
        match = jnp.zeros((LANES, LANES), F32)
        for s in range(slots):
            for t in range(slots):
                hit = jnp.where(pair_ids[s, atom] == pair_ids[t, other], 1.0, 0.0)
                match = jnp.where((r_ // half == s) & (c_ // half == t), hit.astype(F32), match)
        match_op[:, slot * LANES:(slot + 1) * LANES] = jnp.where(r_ % half == c_ % half, match, 0.0).astype(BF16)

    spread(0)
    spread(1)
    relay(2, 1, 2)
    relay(2, 0, 0)
    for copy in third_hop:
        copy.wait_recv()
    for k in range(3):
        send_own(k, (3,))

    for t in range(slots):
        virt = []
        for o in range(slots):
            occ_pos, virt_pos, live = own_entries[t][o]
            virt.append((table[virt_pos].astype(F32) * live).astype(BF16))
            gather[3, t * BLK:(t + 1) * BLK, o * LANES:(o + 1) * LANES] = table[occ_pos]
        b = nt(turn_v[...], jnp.concatenate(virt, axis=1)).astype(BF16)
        second_op[0, :, t * LANES:(t + 1) * LANES] = nt(lift[t][:, :BLK], b).astype(BF16)
    size_op = slots * BLK
    unit = (iota((size_op, size_op), 0) == iota((size_op, size_op), 1)).astype(BF16)
    first_op[0] = nt(unit, nn(gather[3], place[...]).astype(BF16)).astype(BF16)

    for x in range(pieces):
        from_y(0, 1, x).wait_recv()
    send_own(3, (0, 1, 3))

    def operators(slot):
        for t in range(slots):
            virt = []
            for o in range(slots):
                occ_pos, virt_pos, live = entries[slot][t][o]
                virt.append(
                    (table[virt_pos, pl.ds(pl.multiple_of(low * half, half), half), :].astype(F32) * live).astype(BF16)
                )
                gather[slot, o * BLK:(o + 1) * BLK, t * LANES:(t + 1) * LANES] = table[occ_pos]
            second_op[1 + slot, :, t * LANES:(t + 1) * LANES] = nt(lift[t], jnp.concatenate(virt, axis=0)).astype(BF16)
        first_op[1 + slot] = nn(gather[slot], place[...]).astype(BF16)

    for slot in used:
        operators(slot)

    lanes2 = (iota((BLK, 2 * LANES), 1) // half) % slots

    def first(k, u, g):
        got = nn(xg[lax.rem(g, 2)], second_op[k]).astype(BF16)
        for i in range(part_rows):
            for t in range(slots):
                wg[u, i, t * BLK:(t + 1) * BLK, :] = got[i * BLK:(i + 1) * BLK, t * LANES:(t + 1) * LANES]

    def second(k, u):
        for p in range(part_rows // 2):
            both = nn(first_op[k], jnp.concatenate([wg[u, 2 * p], wg[u, 2 * p + 1]], axis=1))
            res = both[:BLK]
            for o in range(1, slots):
                res = jnp.where(lanes2 == o, both[o * BLK:(o + 1) * BLK], res)
            for x in range(2):
                uf[u, (2 * p + x) * BLK:(2 * p + x + 1) * BLK, :] = res[:, x * LANES:(x + 1) * LANES]

    def keep(k, u, at_rows):
        for m in range(BLK):
            stack[k, at_rows, m * LANES:(m + 1) * LANES] = uf[u, pl.ds(m, part_rows, stride=BLK), :].astype(BF16)

    def two_stacks(k, at_rows, g):
        for u in range(2):
            first(k + u, u, g)
        for u in range(2):
            second(k + u, u)
        for u in range(2):
            keep(k + u, u, at_rows)

    def reorder(at_rows):
        x = jnp.concatenate([stack[0, at_rows, m * LANES:(m + 1) * LANES] for m in range(BLK)], axis=0)
        got = nn(x, match_op[...]).astype(BF16)
        below = pl.ds(at_rows.start + BLK, part_rows)
        for m in range(BLK):
            for slot in used:
                stack[1 + slot, below, m * LANES:(m + 1) * LANES] = got[
                    m * part_rows:(m + 1) * part_rows, slot * LANES:(slot + 1) * LANES
                ]

    due = ((0, 2, 0, 1), (1, 2, 1, 3), (0, 1, 0, 2), (2, 2, 0, 2), (2, 1, 0, 3), (4, 2, 0, 3))

    def step(g, carry):
        y = jnp.where(g < 2, low, 1 - low)
        at_rows = pl.ds(pl.multiple_of(y * rows + lax.rem(g, 2) * part_rows, part_rows), part_rows)
        for x in range(2):
            @pl.when(g == 2 + x)
            def _():
                for p in range(pieces):
                    from_y(1, x, p).wait_recv()
                spread(2 + x)

        def relays(side):
            for at, a, slot, group in due:
                if at % 2 == side:
                    @pl.when(g == at // 2)
                    def _():
                        relay(a, slot, group)

        two_stacks(0, at_rows, g)
        relays(0)

        @pl.when(place_at >= 2)
        def _():
            reorder(at_rows)
            two_stacks(2, at_rows, g)

        @pl.when(place_at == 1)
        def _():
            reorder(at_rows)
        relays(1)
        return carry

    lax.fori_loop(0, 4, step, 0)

    for c in range(lines):
        blk[c] = jnp.zeros((BLK, LANES), F32)

    def lay(x):
        return jnp.concatenate([x, jnp.zeros((BLK, LANES - BLK), F32)], axis=1)


    def returned(slot, y):
        a = used[slot][0]
        return remote(
            cross.at[slot, pl.ds(y * rows, rows)], cross_in.at[place_at, low], c_send.at[slot, y],
            c_recv.at[place_at, low], dist, at_place(a, y),
        )

    def product(slot):
        a = used[slot][0]
        for k in range(4):
            if slot == 2:
                for x in range(pieces):
                    over_z(slot, k, x, False, a).wait_recv()
            else:
                @pl.when(place_at == 3)
                def _():
                    for x in range(pieces):
                        over_z(slot, k, x, False, a).wait_recv()
        both = nt(stack[1 + slot], moved[slot])
        both = jnp.concatenate([both, jnp.zeros((2 * BLK, LANES - BLK), F32)], axis=1)
        cross[slot] = both.T[:BLK]
        for y in range(2):
            returned(slot, y).start()
        blk[flip(a)] = both[BLK:]

    for slot, a in ((1, 3), (0, 1), (0, 2), (0, 3), (2, 2), (1, 2)):
        @pl.when(place_at == a)
        def _():
            product(slot)

    blk[high] = lay(nt(stack[0, :BLK], halves[low]))
    other_rows = pl.ds(pl.multiple_of((1 - low) * rows, rows), rows)
    to_partner = remote(blk.at[:, other_rows], partner_in, p_send.at[0], p_recv.at[0], dist, partner)
    to_partner.start()

    came = {1: (0,), 2: (0, 1, 3), 3: (0, 1)}
    for src, takers in came.items():
        for a in takers:
            @pl.when(place_at == a)
            def _():
                for y in range(2):
                    remote(
                        cross.at[0, pl.ds(0, rows)], cross_in.at[src, y], c_send.at[0, 0], c_recv.at[src, y], dist, me
                    ).wait_recv()
                blk[flip(src), own_rows] = cross_in[src, 0] + cross_in[src, 1]
    to_partner.wait()
    tiles = [(blk[c, own_rows] + partner_in[c])[:, :BLK] for c in range(lines)]
    out_ref[...] = jnp.concatenate(tiles, axis=1)

    for copy in first_hop + second_hop + third_hop:
        copy.wait_send()
    for k in range(2):
        for x in range(pieces):
            over_y(0, k, x).wait_send()
            over_y(1, k, x).wait_send()
    for slot, senders in {0: (0, 1, 2), 1: (1, 2), 2: (3,)}.items():
        for a in senders:
            @pl.when(place_at == a)
            def _():
                for k in range(4):
                    for x in range(pieces):
                        over_z(slot, k, x, False, 0).wait_send()

        @pl.when(wanted_here(slot))
        def _():
            for y in range(2):
                returned(slot, y).wait_send()


def on_line(n, groups, atoms, source, occ, virt, pairs, tensor, green):
    slots, rows, width = tensor.shape
    blocks = green.shape[0] // 2
    lines = n // 2
    deep = BLK * LANES
    part_rows = rows // 2
    vmem = pl.BlockSpec(memory_space=pltpu.VMEM)
    dma = pltpu.SemaphoreType.DMA
    return pl.pallas_call(
        functools.partial(line_kernel, n, groups, atoms),
        out_shape=jax.ShapeDtypeStruct((rows, lines * BLK), F32),
        in_specs=[pl.BlockSpec(memory_space=pltpu.SMEM)] * 4 + [vmem, vmem],
        out_specs=vmem,
        scratch_shapes=[
            pltpu.VMEM((2 * n * blocks, BLK, LANES), BF16),
            pltpu.VMEM((2, BLK, deep), BF16),
            pltpu.VMEM((3, BLK, deep), BF16),
            pltpu.VMEM((4, 2 * BLK, deep), BF16),
            pltpu.VMEM((LANES, 3 * LANES), BF16),
            pltpu.VMEM((2, part_rows * BLK, LANES), F32),
            pltpu.VMEM((2, part_rows * BLK, 2 * LANES), BF16),
            pltpu.VMEM((2, part_rows, slots * BLK, LANES), BF16),
            pltpu.VMEM((2, part_rows * BLK, LANES), F32),
            pltpu.VMEM((4, slots * BLK, slots * BLK), BF16),
            pltpu.VMEM((4, 2 * LANES, slots * LANES), BF16),
            pltpu.VMEM((4, slots * BLK, slots * LANES), BF16),
            pltpu.VMEM((slots * LANES, slots * LANES), BF16),
            pltpu.VMEM((slots * LANES, slots * BLK), BF16),
            pltpu.VMEM((slots, 2 * LANES, LANES), BF16),
            pltpu.VMEM((LANES, slots * LANES), BF16),
            pltpu.VMEM((lines, BLK, LANES), F32),
            pltpu.VMEM((3, BLK, LANES), F32),
            pltpu.VMEM((lines, rows, LANES), F32),
            pltpu.VMEM((lines, 2, rows, LANES), F32),
            dma((4, lines)),
            dma((4, lines)),
            dma((2, 4)),
            dma((2, 4)),
            dma((3, 8)),
            dma((3, 8)),
            dma((3, 2)),
            dma((lines, 2)),
            dma((1,)),
            dma((1,)),
        ],
        compiler_params=pltpu.CompilerParams(
            collective_id=1, has_side_effects=True, vmem_limit_bytes=48 * 2**20
        ),
    )(*[jnp.transpose(x, (1, 2, 0)) for x in (source, occ, virt)], pairs.T, tensor, green)


def solution(mesh):
    n = mesh.shape["ctr"]
    groups = mesh.shape["dist"]

    def shards(three_centre, occupied_green, virtual_green, pair_index, source_slot, occupied_index, virtual_index):
        rows, slots, width = three_centre.shape
        blocks = occupied_green.shape[0]
        atoms = pair_index.shape[0]
        chunks = width // LANES
        cols = width // n
        tensor = jnp.transpose(three_centre, (1, 0, 2))
        green = jnp.concatenate([virtual_green, occupied_green], axis=0).reshape(2 * blocks, BLK, BLK)
        ids = jnp.concatenate(
            [x.reshape(-1) for x in (source_slot, occupied_index, virtual_index, pair_index)]
        )
        vmem = pl.BlockSpec(memory_space=pltpu.VMEM)
        dma = pltpu.SemaphoreType.DMA
        if n == 8 and groups % 2 == 0 and rows * 2 == BLK:
            return on_line(
                n, groups, atoms, source_slot, occupied_index, virtual_index, pair_index, tensor, green
            )
        return pl.pallas_call(
            functools.partial(kernel, n, groups, atoms),
            out_shape=jax.ShapeDtypeStruct((rows, n * rows), F32),
            in_specs=[pl.BlockSpec(memory_space=pltpu.SMEM), vmem, vmem],
            out_specs=vmem,
            scratch_shapes=[
                pltpu.VMEM((2 * n * blocks, BLK, LANES), BF16),
                pltpu.VMEM((rows * chunks, LANES), F32),
                pltpu.VMEM((slots, rows * chunks, LANES), BF16),
                pltpu.VMEM((slots * BLK, rows * LANES), BF16),
                pltpu.VMEM((BLK, slots * BLK), BF16),
                pltpu.VMEM((slots, n, rows, cols), BF16),
                pltpu.VMEM((n, slots, rows, cols), BF16),
                pltpu.VMEM((n, slots, rows, cols), BF16),
                pltpu.VMEM((n * rows, NPR * cols), BF16),
                pltpu.VMEM((n * rows, NPR * cols), BF16),
                pltpu.VMEM((n * rows, n * rows), F32),
                pltpu.VMEM((n * rows, n * rows), BF16),
                pltpu.VMEM((n, rows, n * rows), BF16),
                dma((4, n // 2)),
                dma((4, n // 2)),
                dma((n,)),
                dma((n,)),
                dma((slots, n)),
                dma((slots, n)),
                dma((n,)),
                dma((n,)),
                dma((2,)),
            ],
            compiler_params=pltpu.CompilerParams(
                collective_id=0, has_side_effects=True, vmem_limit_bytes=48 * 2**20
            ),
        )(ids, tensor, green)

    return jax.shard_map(
        shards,
        mesh=mesh,
        in_specs=(
            P(("dist", "ctr"), None, None),
            P(("dist", "ctr"), None),
            P(("dist", "ctr"), None),
            P(),
            P(),
            P(),
            P(),
        ),
        out_specs=P(("dist", "ctr"), None),
        check_vma=False,
    )
```
